128 devices in a mesh: dp: 16 (over y, x), expert: 8 (over z, core).
Axes of the slice: x: 4, y: 4, z: 4, core: 2. Of those that a mesh axis runs over, the one named last changes fastest.
Arguments:
- tokens: bfloat16 [32768, 1024], P(('dp', 'expert'))
- cotangent: bfloat16 [32768, 1024], P(('dp', 'expert')), may hold values from -6 to 6
- routes: int32 [32768, 4], P(('dp', 'expert')), may hold values from 0 to 31, as said below
- slot_ids: int32 [32768, 4], P(('dp', 'expert')), may hold values from 0 to 63, as said below
- attn_gain: float32 [1024], replicated, may hold values from 0.25 to 1.75
- w_qkv: bfloat16 [1024, 2048], replicated, may hold values from -0.1875 to 0.1875
- b_qkv: float32 [2048], replicated, may hold values from -0.6 to 0.6
- w_out: bfloat16 [1024, 1024], replicated, may hold values from -0.75 to 0.75
- b_out: float32 [1024], replicated, may hold values from -0.6 to 0.6
- sink_logits: float32 [16], replicated, may hold values from 1 to 5
- moe_gain: float32 [1024], replicated, may hold values from 0.25 to 1.75
- w_router: bfloat16 [1024, 32], replicated, may hold values from -0.09375 to 0.09375
- b_router: float32 [32], replicated, may hold values from -1.5 to 1.5
- gu_weight: bfloat16 [32, 512, 2, 1024], P('expert', 'dp'), may hold values from -0.1875 to 0.1875
- gu_bias: float32 [32, 2, 512], P('expert'), may hold values from -0.6 to 0.6
- down_weight: bfloat16 [32, 512, 1024], P('expert', 'dp'), may hold values from -0.25 to 0.25
- down_bias: float32 [32, 1024], replicated, may hold values from -0.6 to 0.6
Outputs:
- block_out: bfloat16 [32768, 1024], P(('dp', 'expert'))
- d_tokens: bfloat16 [32768, 1024], P(('dp', 'expert'))
- d_attn_gain: float32 [1024], replicated
- d_w_qkv: float32 [1024, 2048], replicated
- d_b_qkv: float32 [2048], replicated
- d_w_out: float32 [1024, 1024], replicated
- d_b_out: float32 [1024], replicated
- d_sink_logits: float32 [16], replicated
- d_moe_gain: float32 [1024], replicated
- d_w_router: float32 [1024, 32], replicated
- d_b_router: float32 [32], replicated
- d_gu_weight: float32 [32, 512, 2, 1024], P('expert', 'dp')
- d_gu_bias: float32 [32, 2, 512], P('expert', None, 'dp')
- d_down_weight: float32 [32, 512, 1024], P('expert', 'dp')
- d_down_bias: float32 [32, 1024], replicated
The draws below stay inside these ranges and needn't reach their ends.
Inputs may be any that keep to these rules, and one draw needn't show every extreme that they name: `routes`: each row names 4 different experts. Among the 256 rows of one device each expert is named at most 64 times. On the devices that hold one sequence (8 devices in a row) one expert is named exactly 64 times on every device, and on each device a second expert too. `slot_ids`: among the rows of one device, the (row, choice) pairs that name one expert have distinct slot numbers.
All inputs are finite; a program needn't handle non-finite values.
Results may differ from the reference program's by a relative error of at most 0.015.
Values may be sent and summed in bfloat16 or wider, within the bound.
A program may use at most 192 MiB of HBM per device.

```python
import jax
import jax.numpy as jnp
from jax import lax

D = 1024
FF = 512
HEADS = 16
KV_HEADS = 8
HEAD_DIM = 64
TOPK = 4
TOK_DEV = 256
LEN = 2048
TOKENS = 32768
EXPERT_TOTAL = 32
CAP = 64


def routing(key):
    block_count = TOKENS // TOK_DEV
    per_group = LEN // TOK_DEV
    assigned = TOK_DEV * TOPK
    remaining_experts = EXPERT_TOTAL - 2
    baseline_load = (assigned - 2 * CAP) // remaining_experts
    remainder_count = assigned - 2 * CAP - remaining_experts * baseline_load
    group_key, block_key = jax.random.split(key)
    group_hot = jax.random.randint(group_key, (block_count // per_group,), 0, EXPERT_TOTAL)
    hot_first = jnp.repeat(group_hot, per_group)
    block_keys = jax.random.split(block_key, block_count)

    def one_block(one_key, hot_one):
        sub_keys = jax.random.split(one_key, 6)
        hot_two = (hot_one + 1 + jax.random.randint(sub_keys[0], (), 0, EXPERT_TOTAL - 1)) % EXPERT_TOTAL
        shuffled = jax.random.permutation(sub_keys[1], EXPERT_TOTAL).astype(jnp.int32)
        is_hot = ((shuffled == hot_one) | (shuffled == hot_two)).astype(jnp.int32)
        remainder_order = shuffled[jnp.argsort(is_hot * EXPERT_TOTAL + jnp.arange(EXPERT_TOTAL, dtype=jnp.int32))][:remaining_experts]
        shifts = jax.random.randint(sub_keys[2], (remaining_experts // 2,), 0, max(baseline_load, 1))
        signed_value = jnp.stack([shifts, -shifts], axis=1).reshape(remaining_experts)
        extra_single = (jnp.arange(remaining_experts) < remainder_count).astype(jnp.int32)
        per_expert_load = jnp.zeros((EXPERT_TOTAL,), jnp.int32).at[remainder_order].set(baseline_load + extra_single + signed_value)
        per_expert_load = per_expert_load.at[hot_one].set(CAP).at[hot_two].set(CAP)
        run_order = jax.random.permutation(sub_keys[3], EXPERT_TOTAL).astype(jnp.int32)
        run_loads = per_expert_load[run_order]
        run_ends = jnp.cumsum(run_loads)
        run_starts = run_ends - run_loads
        position = jnp.arange(assigned, dtype=jnp.int32)
        which_run = jnp.sum((position[:, None] >= run_ends[None, :]).astype(jnp.int32), axis=1)
        labels = run_order[which_run]
        run_ranks = position - run_starts[which_run]
        spread = jax.random.randint(sub_keys[4], (EXPERT_TOTAL, CAP), 0, 1 << 20) * CAP + jnp.arange(CAP, dtype=jnp.int32)[None, :]
        slot_table = jnp.argsort(spread, axis=1).astype(jnp.int32)
        slot_values = slot_table[labels, run_ranks]
        token_order = jax.random.permutation(sub_keys[5], TOK_DEV)
        return (labels.reshape(TOPK, TOK_DEV).T[token_order], slot_values.reshape(TOPK, TOK_DEV).T[token_order])
    route_blocks, slot_blocks = jax.vmap(one_block)(block_keys, hot_first)
    return (route_blocks.reshape(TOKENS, TOPK).astype(jnp.int32), slot_blocks.reshape(TOKENS, TOPK).astype(jnp.int32))


def draw_routes(key, part):
    return routing(key)[0]


def draw_slot_ids(key, part):
    return routing(key)[1]


def draw_tokens(key, part):
    key = jax.random.fold_in(key, 7)
    first_key, row_key, col_key = jax.random.split(key, 3)
    base_values = jax.random.normal(first_key, (TOKENS, D), jnp.float32)
    row_scale = jnp.exp(jax.random.uniform(row_key, (TOKENS, 1), jnp.float32) * jnp.log(10.0)) / 3.0
    col_scale = jnp.exp(jax.random.uniform(col_key, (1, D), jnp.float32, -1.0, 1.0) * jnp.log(3.3))
    return (base_values * row_scale * col_scale).astype(jnp.bfloat16)


def level_of(key, extent, cuts, smallest, top_value):
    factor_of = 1.0
    for axis_at, parts in cuts:
        draws = jax.random.uniform(jax.random.fold_in(jax.random.fold_in(key, 6), axis_at), (parts,), jnp.float32, smallest / len(cuts), top_value / len(cuts))
        factor_of = factor_of * jnp.repeat(jnp.exp(draws), extent[axis_at] // parts).reshape((-1,) + (1,) * (len(extent) - 1 - axis_at))
    return factor_of


def normal_values(own_key, dims, deviation, limit, cuts=(), held_as=jnp.bfloat16):
    drawn = jax.random.normal(own_key, dims, jnp.float32) * deviation
    if len(cuts) > 0:
        drawn = level_of(own_key, dims, cuts, -0.22, 0.18) * drawn
    return jnp.clip(drawn, min=-limit, max=limit).astype(held_as)


def setup_inputs(seed: int = 0) -> dict:
    key_of = jax.random.split(jax.random.key(seed), 18)
    return {
        "tokens": draw_tokens(jax.random.fold_in(key_of[17], 71), 0),
        "cotangent": normal_values(key_of[1], (TOKENS, D), 1.0, 6.0, ((0, 128),)),
        "routes": draw_routes(jax.random.fold_in(key_of[17], 71), 0),
        "slot_ids": draw_slot_ids(jax.random.fold_in(key_of[17], 71), 0),
        "attn_gain": jnp.clip(1.0 + 0.15 * jax.random.normal(key_of[4], (D,), jnp.float32), 0.25, 1.75),
        "w_qkv": normal_values(key_of[5], (D, (HEADS + 2 * KV_HEADS) * HEAD_DIM), D ** -0.5, 0.1875),
        "b_qkv": normal_values(key_of[6], ((HEADS + 2 * KV_HEADS) * HEAD_DIM,), 0.1, 0.6, (), jnp.float32),
        "w_out": normal_values(key_of[7], (HEADS * HEAD_DIM, D), (HEADS * HEAD_DIM // 16) ** -0.5, 0.75),
        "b_out": normal_values(key_of[8], (D,), 0.1, 0.6, (), jnp.float32),
        "sink_logits": jnp.clip(jax.random.uniform(key_of[9], (HEADS,), jnp.float32, 1.0, 5.0), 1.0, 5.0),
        "moe_gain": jnp.clip(1.0 + 0.15 * jax.random.normal(key_of[10], (D,), jnp.float32), 0.25, 1.75),
        "w_router": normal_values(key_of[11], (D, EXPERT_TOTAL), (4 * D) ** -0.5, 0.09375),
        "b_router": normal_values(key_of[12], (EXPERT_TOTAL,), 0.25, 1.5, (), jnp.float32),
        "gu_weight": normal_values(key_of[13], (EXPERT_TOTAL, FF, 2, D), D ** -0.5, 0.1875, ((0, 8), (1, 16))),
        "gu_bias": normal_values(key_of[14], (EXPERT_TOTAL, 2, FF), 0.1, 0.6, ((0, 8),), jnp.float32),
        "down_weight": normal_values(key_of[15], (EXPERT_TOTAL, FF, D), FF ** -0.5, 0.25, ((0, 8), (1, 16))),
        "down_bias": normal_values(key_of[16], (EXPERT_TOTAL, D), 0.1, 0.6, (), jnp.float32),
    }


@jax.custom_vjp
def low(v):
    return lax.optimization_barrier(v.astype(jnp.bfloat16)).astype(jnp.float32)

@jax.custom_vjp
def low_back(v):
    return v

def low_keep(v):
    return (low(v), None)

def low_pass(kept, grad):
    return (grad,)

def back_keep(v):
    return (v, None)

def back_low(kept, grad):
    return (low(grad),)
low.defvjp(low_keep, low_pass)
low_back.defvjp(back_keep, back_low)
EPS = 1e-05
THETA = 10000.0
LIMIT = 7.0
ALPHA = 1.702
NEG = -1000000000.0
HIGH = lax.Precision.HIGHEST

def rms_norm(stream, norm_gain):
    return stream * lax.rsqrt(lax.optimization_barrier(jnp.mean(stream * stream, axis=-1, keepdims=True)) + EPS) * norm_gain

def rotate(values_in, places):
    half_dim = values_in.shape[-1] // 2
    frequency = jnp.exp(jnp.arange(half_dim, dtype=jnp.float32) * (-2.0 * jnp.log(THETA) / values_in.shape[-1]))
    angles = places.astype(jnp.float32)[:, None] * frequency[None, :]
    cosine = jnp.cos(angles)[:, None, :]
    sine_part = jnp.sin(angles)[:, None, :]
    first_half = values_in[..., :half_dim]
    second = values_in[..., half_dim:]
    return jnp.concatenate([first_half * cosine - second * sine_part, second * cosine + first_half * sine_part], axis=-1)

def swiglu(gate_pre, up_pre):
    gate_clip = LIMIT * jnp.tanh(gate_pre / LIMIT)
    up_clip = LIMIT * jnp.tanh(up_pre / LIMIT)
    return (up_clip + 1.0) * gate_clip * jax.nn.sigmoid(ALPHA * gate_clip)

def attend(normed, w_qkv, b_qkv, sink_logits):
    length = normed.shape[0]
    n_query = HEADS * HEAD_DIM
    n_key = KV_HEADS * HEAD_DIM
    repeat = HEADS // KV_HEADS
    places = jnp.arange(length, dtype=jnp.int32)
    qkv_mixed = low_back(jnp.dot(normed, w_qkv, precision=HIGH) + b_qkv)
    queries = low(rotate(qkv_mixed[:, :n_query].reshape(length, HEADS, HEAD_DIM), places))
    key_rows = low(rotate(qkv_mixed[:, n_query:n_query + n_key].reshape(length, KV_HEADS, HEAD_DIM), places))
    value_rows = low(qkv_mixed[:, n_query + n_key:].reshape(length, KV_HEADS, HEAD_DIM))
    queries = queries.reshape(length, KV_HEADS, repeat, HEAD_DIM)
    scores = low_back(jnp.einsum('qkgd,skd->kgqs', queries, key_rows, precision=HIGH) * HEAD_DIM ** (-0.5))
    allowed = places[:, None] >= places[None, :]
    scores = jnp.where(allowed, scores, NEG)
    sink_part = sink_logits.reshape(KV_HEADS, repeat)[:, :, None]
    row_max = jnp.maximum(lax.optimization_barrier(jnp.max(scores, axis=-1)), sink_part)
    exp_scores = jnp.exp(scores - row_max[..., None])
    row_total = lax.optimization_barrier(jnp.sum(exp_scores, axis=-1)) + jnp.exp(sink_part - row_max)
    weights_low = low(exp_scores / row_total[..., None])
    attended = jnp.einsum('kgqs,skd->qkgd', weights_low, value_rows, precision=HIGH)
    return low(low_back(attended.reshape(length, n_query)))

def forward(stream, attn_gain, w_qkv, b_qkv, w_out, b_out, sink_logits, moe_gain, w_router, b_router, gu_weight, gu_bias, down_weight, down_bias, routes, slot_ids):
    normed = low(rms_norm(stream, attn_gain))

    def per_sequence(seq_rows):
        return attend(seq_rows, w_qkv, b_qkv, sink_logits)
    attended = lax.map(jax.checkpoint(per_sequence), normed.reshape(TOKENS // LEN, LEN, D)).reshape(TOKENS, HEADS * HEAD_DIM)
    branch = low_back(jnp.dot(attended, w_out, precision=HIGH) + b_out)
    middle = stream + branch
    routed = low(rms_norm(middle, moe_gain))
    logits = jnp.dot(routed, w_router, precision=HIGH) + b_router
    gate_weights = jax.nn.softmax(jnp.take_along_axis(logits, routes, axis=1), axis=-1)
    block_ids = (jnp.arange(TOKENS, dtype=jnp.int32) // TOK_DEV)[:, None]
    place_ids = block_ids * CAP + slot_ids
    owner_rows = TOKENS // TOK_DEV * CAP
    token_ids = jnp.broadcast_to(jnp.arange(TOKENS, dtype=jnp.int32)[:, None], routes.shape)
    table = jnp.full((EXPERT_TOTAL, owner_rows), -1, jnp.int32).at[routes, place_ids].set(token_ids)

    def expert(operands):
        token_index, gu_one, gu_bias_one, down_one, down_bias_one = operands
        picked = jnp.where(token_index[:, None] >= 0, routed[jnp.maximum(token_index, 0)], 0.0)
        picked = low_back(picked)
        gate_pre = low_back(jnp.dot(picked, gu_one[:, 0, :].T, precision=HIGH) + gu_bias_one[0])
        up_pre = low_back(jnp.dot(picked, gu_one[:, 1, :].T, precision=HIGH) + gu_bias_one[1])
        active = low(swiglu(gate_pre, up_pre))
        return low(low_back(jnp.dot(active, down_one, precision=HIGH) + down_bias_one))
    outputs = lax.map(jax.checkpoint(expert), (table, gu_weight, gu_bias, down_weight, down_bias))
    gathered = outputs[routes, place_ids]
    return middle + lax.optimization_barrier(jnp.sum(gate_weights[:, :, None] * gathered, axis=1))

def reference(tokens, cotangent, routes, slot_ids, attn_gain, w_qkv, b_qkv, w_out, b_out, sink_logits, moe_gain, w_router, b_router, gu_weight, gu_bias, down_weight, down_bias):

    def forward_fn(stream, attn_gain, w_qkv, b_qkv, w_out, b_out, sink_logits, moe_gain, w_router, b_router, gu_weight, gu_bias, down_weight, down_bias):
        return forward(stream, attn_gain, w_qkv, b_qkv, w_out, b_out, sink_logits, moe_gain, w_router, b_router, gu_weight, gu_bias, down_weight, down_bias, routes, slot_ids)
    result, pullback = jax.vjp(forward_fn, tokens.astype(jnp.float32), attn_gain, w_qkv.astype(jnp.float32), b_qkv, w_out.astype(jnp.float32), b_out, sink_logits, moe_gain, w_router.astype(jnp.float32), b_router, gu_weight.astype(jnp.float32), gu_bias, down_weight.astype(jnp.float32), down_bias)
    grads = pullback(cotangent.astype(jnp.float32))
    return (result.astype(jnp.bfloat16), grads[0].astype(jnp.bfloat16), grads[1], grads[2], grads[3], grads[4], grads[5], grads[6], grads[7], grads[8], grads[9], grads[10], grads[11], grads[12], grads[13])
```

```python
import functools

import jax
import jax.numpy as jnp
import numpy as np
from jax import lax
from jax.experimental import pallas as pl
from jax.experimental.pallas import tpu as pltpu
from jax.sharding import PartitionSpec as P

MESH = pl.DeviceIdType.MESH
BF = jnp.bfloat16
F32 = jnp.float32
EPS = 1e-05
THETA = 10000.0
LIMIT = 7.0
ALPHA = 1.702
NEG = -1000000000.0
NSEM = 800
VLIM = 63 << 20
T = 256
D = 1024


def nt(a, b):
    return lax.dot_general(a, b, (((1,), (1,)), ((), ())), preferred_element_type=F32)


def tn(a, b):
    return lax.dot_general(a, b, (((0,), (0,)), ((), ())), preferred_element_type=F32)


def nn(a, b):
    return jnp.dot(a, b, preferred_element_type=F32)


def split_low(v):
    high = v.astype(BF)
    return high, (v - high.astype(F32)).astype(BF)


def layer_kernel(
    x_in, dy_in, w_in, target, attn_gain, w_qkv, b_qkv, w_out, b_out, sink_row, moe_gain,
    w_rt, b_rt, gu_bias, down_bias, cos_a, sin_a, cos_b, sin_b,
    block_out, d_tokens, d_weights, d_wqkv_t, d_wout, small, d_wrt, d_brt, d_gub,
    xg, dyg, h2g, gathered, qs, kk, vv, kkt, vvt, lse, att_send, att, middle, h2own, metag, meta_send,
    outb, drb, sib_in, half_in, full_in, rs_half, rs_full, rs2_half, rs2_full, dob, dgt_send, dgt_in,
    d_middle, gates_ref, sems, credit,
):
    dp = lax.axis_index("dp")
    g = lax.axis_index("expert")
    y, x = lax.div(dp, 4), lax.rem(dp, 4)
    z, c = lax.div(g, 2), lax.rem(g, 2)
    xs = [lax.rem(x + d, 4) for d in range(4)]
    ys = [lax.rem(y + d, 4) for d in range(4)]
    zs = [lax.rem(z + d, 4) for d in range(4)]
    gs = [lax.rem(g + d, 8) for d in range(8)]
    other = 1 - c
    sib = {"expert": z * 2 + (1 - c)}
    up = {"expert": zs[1] * 2 + c}
    down = {"expert": zs[3] * 2 + c}

    neighbours = {
        "x": [{"dp": y * 4 + xs[d]} for d in range(4)],
        "y": [{"dp": ys[d] * 4 + x} for d in range(4)],
    }

    def xy(axis, d):
        return neighbours[axis][d]

    places = [[[ys[db] * 4 + xs[da] for db in range(4)] for da in range(4)],
              [[ys[da] * 4 + xs[db] for db in range(4)] for da in range(4)]]

    def slot(h, da, db):
        return places[h][da][db]

    counter = [0]

    def sem():
        counter[0] += 1
        assert counter[0] <= NSEM
        return counter[0] - 1

    def sem_block(n):
        first = counter[0]
        counter[0] += n
        assert counter[0] <= NSEM
        return first

    pending = []
    pending_gather = []
    pending_weights = [[] for _ in range(4)]

    def view(ref):
        return ref() if callable(ref) else ref

    def send(src, dst, recv, dev, keep=pending):
        n = sem()

        def copy():
            return pltpu.make_async_remote_copy(
                src_ref=view(src), dst_ref=view(dst), send_sem=sems.at[n], recv_sem=sems.at[recv],
                device_id=dev, device_id_type=MESH)

        copy().start()
        keep.append(copy)

    def arrived(dst, recv):
        pltpu.make_async_remote_copy(
            src_ref=dst, dst_ref=dst, send_sem=sems.at[recv], recv_sem=sems.at[recv],
            device_id=sib, device_id_type=MESH,
        ).wait_recv()

    def drain(copies):
        for copy in copies:
            copy().wait_send()
        copies.clear()

    def local_copy(src, dst):
        n = sem()

        def copy():
            return pltpu.make_async_copy(view(src), view(dst), sems.at[n])

        copy().start()
        return copy

    barrier = pltpu.get_barrier_semaphore()
    for rel in range(1, 8):
        pl.semaphore_signal(barrier, inc=1, device_id={"expert": gs[rel]}, device_id_type=MESH)
    for axis in ("x", "y"):
        for d in (1, 3):
            pl.semaphore_signal(barrier, inc=1, device_id=xy(axis, d), device_id_type=MESH)
    pl.semaphore_wait(barrier, 11)

    class GatherZ:
        def __init__(self, buf, own):
            self.buf, self.own = buf, own
            self.k = sem_block(9)
            self.m1, self.p1, self.far = zs[3] * 2 + c, zs[1] * 2 + c, zs[2] * 2 + c
            s = 1 - c
            self.sm1, self.sp1, self.sfar, self.so = (
                zs[3] * 2 + s, zs[1] * 2 + s, zs[2] * 2 + s, z * 2 + s)

        def start(self):
            b, k = self.buf, self.k
            send(self.own, lambda: b.at[g], k + 1, up, pending_gather)
            send(self.own, lambda: b.at[g], k + 2, down, pending_gather)
            send(self.own, lambda: b.at[g], k + 0, sib, pending_gather)

        def step_m1(self):
            b, k, s = self.buf, self.k, self.m1
            arrived(b.at[s], k + 1)
            send(lambda: b.at[s, pl.ds(0, 128)], lambda: b.at[s, pl.ds(0, 128)], k + 3, up, pending_gather)
            send(lambda: b.at[s], lambda: b.at[s], k + 4, sib, pending_gather)

        def step_p1(self):
            b, k, s = self.buf, self.k, self.p1
            arrived(b.at[s], k + 2)
            send(lambda: b.at[s, pl.ds(128, 128)], lambda: b.at[s, pl.ds(128, 128)], k + 5, down, pending_gather)
            send(lambda: b.at[s], lambda: b.at[s], k + 6, sib, pending_gather)

        def step_far(self):
            b, k, s = self.buf, self.k, self.far
            for i, kr, ks in ((0, 3, 7), (128, 5, 8)):
                arrived(b.at[s, pl.ds(i, 128)], k + kr)
                send(lambda i=i: b.at[s, pl.ds(i, 128)], lambda i=i: b.at[s, pl.ds(i, 128)], k + ks, sib, pending_gather)

        def wait_sib_own(self):
            arrived(self.buf.at[self.so], self.k)

        def wait_sib_m1(self):
            arrived(self.buf.at[self.sm1], self.k + 4)

        def wait_sib_p1(self):
            arrived(self.buf.at[self.sp1], self.k + 6)

        def wait_sib_far(self):
            for i, ks in ((0, 7), (128, 8)):
                arrived(self.buf.at[self.sfar, pl.ds(i, 128)], self.k + ks)

    class ScatterZ:
        def __init__(self, buf, sib_ref, half_ref, full_ref):
            self.buf, self.r, self.h, self.f = buf, sib_ref, half_ref, full_ref
            self.k = sem_block(8)
            self.sent = []

        def chunks(self):
            return [zs[d] * 2 + (1 - c) for d in (2, 1, 3, 0)], [zs[d] * 2 + c for d in (2, 1, 3, 0)]

        def to_sibling(self, n):
            d = (2, 1, 3, 0)[n]
            zz = zs[d]
            send(lambda: self.buf.at[zz * 2 + (1 - c)], lambda: self.r(d), self.k + n, sib, self.sent)

        def add(self, chunk, refs):
            def body(i, carry):
                rows = pl.ds(i * 64, 64)
                v = self.buf[chunk, rows, :].astype(F32)
                for ref in refs:
                    v = v + ref[rows, :].astype(F32)
                self.buf[chunk, rows, :] = v.astype(BF)
                return carry
            lax.fori_loop(0, 4, body, 0)

        def add_half(self, chunk, base, ref):
            def body(i, carry):
                rows = pl.ds(base + i * 64, 64)
                v = self.buf[chunk, rows, :].astype(F32) + ref[pl.ds(i * 64, 64), :].astype(F32)
                self.buf[chunk, rows, :] = v.astype(BF)
                return carry
            lax.fori_loop(0, 2, body, 0)

        def step1(self):
            b, k = self.buf, self.k
            chunk = zs[2] * 2 + c
            arrived(self.r(2), k + 0)
            self.add(chunk, [self.r(2)])
            send(lambda: b.at[chunk, pl.ds(0, 128)], lambda: self.h(0), k + 4, up, self.sent)
            send(lambda: b.at[chunk, pl.ds(128, 128)], lambda: self.h(1), k + 5, down, self.sent)

        def step2(self):
            b, k = self.buf, self.k
            for d, n, hi, dev in ((1, 1, 0, up), (3, 2, 1, down)):
                chunk = zs[d] * 2 + c
                arrived(self.r(d), k + n)
                self.add(chunk, [self.r(d)])
                arrived(self.h(hi), k + 4 + hi)
                self.add_half(chunk, hi * 128, self.h(hi))
                send(lambda chunk=chunk: b.at[chunk], lambda hi=hi: self.f(hi), k + 6 + hi, dev, self.sent)

        def step3(self):
            arrived(self.r(0), self.k + 3)
            arrived(self.f(0), self.k + 6)
            arrived(self.f(1), self.k + 7)

        def result(self, rows):
            return (self.buf[g, rows, :].astype(F32) + self.r(0)[rows, :].astype(F32)
                    + self.f(0)[rows, :].astype(F32) + self.f(1)[rows, :].astype(F32))

    def axis_of(h, ax):
        return "x" if (ax == 0) == (h == 0) else "y"

    gk = sem_block(2 * 4 * 16)

    def gsem(h, e, da, db):
        return gk + ((h * 4 + e) * 4 + da) * 4 + db

    def gsend(h, e, da, db, ax, d):
        def src():
            return w_in.at[h, e] if (da, db) == (0, 0) else gathered.at[h, e, slot(h, da, db)]

        rda, rdb = ((da - d) % 4, db) if ax == 0 else (da, (db - d) % 4)
        send(src, lambda: gathered.at[h, e, slot(h, da, db)], gsem(h, e, rda, rdb), xy(axis_of(h, ax), d % 4),
             pending_weights[e])

    def grecv(h, e, da, db):
        arrived(gathered.at[h, e, slot(h, da, db)], gsem(h, e, da, db))

    def weights_start():
        for e in range(4):
            for h in range(2):
                gsend(h, e, 0, 0, 0, 1)
                gsend(h, e, 0, 0, 0, -1)
            for h in range(2):
                gsend(h, e, 0, 0, 1, 1)
                gsend(h, e, 0, 0, 1, -1)

    def weights_steps():
        for e in range(4):
            for h in range(2):
                grecv(h, e, 3, 0)
                if e % 2 == 0:
                    gsend(h, e, 3, 0, 0, 1)
                grecv(h, e, 1, 0)
                if e % 2 == 1:
                    gsend(h, e, 1, 0, 0, -1)
            for h in range(2):
                for da in (3, 1):
                    gsend(h, e, da, 0, 1, 1)
                    gsend(h, e, da, 0, 1, -1)
            yield "one"
        for e in range(4):
            for h in range(2):
                grecv(h, e, 2, 0)
                gsend(h, e, 2, 0, 1, 1)
                gsend(h, e, 2, 0, 1, -1)
            yield "two"
        for e in range(4):
            for da in (0, 3, 1, 2):
                for h in range(2):
                    grecv(h, e, da, 3)
                    if e % 2 == 0:
                        gsend(h, e, da, 3, 1, 1)
                    grecv(h, e, da, 1)
                    if e % 2 == 1:
                        gsend(h, e, da, 1, 1, -1)
                if da in (3, 2):
                    yield "three"
        for e in range(4):
            for h in range(2):
                for da in range(4):
                    grecv(h, e, da, 2)
            yield ("expert", e)

    small[...] = jnp.zeros((16, D), F32)
    local_x = local_copy(x_in, lambda: xg.at[g])
    gather_x = GatherZ(xg, x_in)
    gather_x.start()
    weights_start()
    local_dy = local_copy(dy_in, lambda: dyg.at[g])
    local_w = []
    for h in range(2):
        for e in range(4):
            local_w.append(local_copy(lambda h=h, e=e: w_in.at[h, e], lambda h=h, e=e: gathered.at[h, e, dp]))
    weights = weights_steps()

    def svc(n=1):
        for _ in range(n):
            if next(weights, None) is None:
                return

    lane = lax.broadcasted_iota(jnp.int32, (1, 128), 1)
    low_half = lane < 64
    first_quarter = (lane % 64) < 32
    mask0 = jnp.where(low_half, 1.0, 0.0).astype(F32)
    mask1 = 1.0 - mask0

    def swap(v):
        return jnp.where(first_quarter, pltpu.roll(v, 96, 1), pltpu.roll(v, 32, 1))

    def trig(r):
        cb, sb = cos_b[pl.ds(r, 1), :], sin_b[pl.ds(r, 1), :]
        ca, sa = cos_a[...], sin_a[...]
        cosine = ca * cb - sa * sb
        sine = sa * cb + ca * sb
        return cosine, jnp.where(first_quarter, -sine, sine)

    def h1_rows(r, rows):
        xf = xg[r, rows, :].astype(F32)
        inv = lax.rsqrt(jnp.mean(xf * xf, axis=-1, keepdims=True) + EPS)
        return (xf * inv * attn_gain[...]).astype(BF)

    def qkv_chunk(r):
        h1 = h1_rows(r, pl.ds(0, T))
        mixed = nn(h1, w_qkv[...]) + b_qkv[...]
        cosine, sine = trig(r)
        q = mixed[:, :128]
        kv = mixed[:, 128:]
        q = (q * cosine + swap(q) * sine) * 0.125
        kv = jnp.where(low_half, kv * cosine + swap(kv) * sine, kv)
        other = pltpu.roll(kv, 64, 1)
        kd = jnp.where(low_half, kv, other)
        vd = jnp.where(low_half, other, kv)
        qs[r] = q.astype(BF)
        kk[r] = kd.astype(BF)
        vv[r] = vd.astype(BF)
        kkt[r] = kd.T.astype(BF)
        vvt[r] = vd.T.astype(BF)

    gx = gather_x
    local_x().wait()
    qkv_chunk(g)
    gx.wait_sib_own()
    qkv_chunk(gx.so)
    gx.step_m1()
    gx.step_p1()
    qkv_chunk(gx.m1)
    svc(1)
    qkv_chunk(gx.p1)
    gx.wait_sib_m1()
    qkv_chunk(gx.sm1)
    svc(1)
    gx.wait_sib_p1()
    qkv_chunk(gx.sp1)
    gx.step_far()
    gather_dy = GatherZ(dyg, dy_in)
    gather_dy.start()
    qkv_chunk(gx.far)
    svc(1)
    gx.wait_sib_far()
    qkv_chunk(gx.sfar)
    svc(1)

    def stacked(v):
        vf = v.astype(F32)
        return jnp.concatenate([vf * mask0, vf * mask1], axis=0).astype(BF)

    key_at = lax.broadcasted_iota(jnp.int32, (T, 2 * T), 0)
    query_at = lax.broadcasted_iota(jnp.int32, (T, 2 * T), 1) % T
    allowed = key_at <= query_at

    att_k = sem_block(8)

    def attend(i, m_ref, l_ref, acc_ref):
        q2 = stacked(qs[i])
        m_ref[...] = sink_row[...]
        l_ref[...] = jnp.ones((1, 2 * T), F32)
        acc_ref[...] = jnp.zeros((128, 2 * T), F32)

        def block(j, diagonal):
            s = nt(kk[j], q2)
            if diagonal:
                s = jnp.where(allowed, s, NEG)
            m_old = m_ref[...]
            m_new = jnp.maximum(m_old, jnp.max(s, axis=0, keepdims=True))
            p = jnp.exp(s - m_new)
            alpha = jnp.exp(m_old - m_new)
            l_ref[...] = l_ref[...] * alpha + jnp.sum(p, axis=0, keepdims=True)
            acc_ref[...] = acc_ref[...] * alpha + nn(vvt[j], p.astype(BF))
            m_ref[...] = m_new

        if i > 0:
            def body(j, carry):
                block(j, False)
                return carry
            lax.fori_loop(0, i, body, 0)
        block(i, True)
        total = l_ref[...]
        lse[i] = m_ref[...] + jnp.log(total)
        o = (acc_ref[...] / total).T
        att_send[i] = jnp.where(low_half, o[:T], o[T:]).astype(BF)

        @pl.when(g != i)
        def _():
            pltpu.make_async_remote_copy(
                src_ref=att_send.at[i], dst_ref=att.at[:, pl.ds(pl.multiple_of(g * 128, 128), 128)],
                send_sem=sems.at[att_sk + i], recv_sem=sems.at[att_k + g],
                device_id={"expert": i}, device_id_type=MESH,
            ).start()

        @pl.when(g == i)
        def _():
            att[:, pl.ds(pl.multiple_of(g * 128, 128), 128)] = att_send[i]

    att_sk = sem_block(8)

    def forward_attention(m_ref, l_ref, acc_ref):
        gd = gather_dy
        for i in range(8):
            attend(i, m_ref, l_ref, acc_ref)
            if i == 3:
                gd.step_m1()
                gd.step_p1()
            if i == 6:
                gd.step_far()
            if i in (1, 2, 4, 5):
                svc(1)

    pl.run_scoped(
        forward_attention, pltpu.VMEM((1, 2 * T), F32), pltpu.VMEM((1, 2 * T), F32), pltpu.VMEM((128, 2 * T), F32))

    for i in range(8):
        @pl.when(g != i)
        def _(i=i):
            piece = att.at[:, pl.ds(i * 128, 128)]
            arrived(piece, att_k + i)
            pltpu.make_async_remote_copy(
                src_ref=att_send.at[i], dst_ref=piece, send_sem=sems.at[att_sk + i],
                recv_sem=sems.at[att_k + i], device_id={"expert": i}, device_id_type=MESH,
            ).wait_send()

    def project(i, carry):
        rows = pl.ds(pl.multiple_of(i * 64, 64), 64)
        m = xg[g, rows, :].astype(F32) + (nn(att[rows, :], w_out[...]) + b_out[...])
        middle[rows, :] = m
        inv = lax.rsqrt(jnp.mean(m * m, axis=-1, keepdims=True) + EPS)
        h2own[rows, :] = (m * inv * moe_gain[...]).astype(BF)
        return carry

    lax.fori_loop(0, 4, project, 0)
    gather_h = GatherZ(h2g, h2own)
    gather_h.start()
    h2g[g] = h2own[...]

    logits = nt(w_rt[...], h2own[...]) + b_rt[...]
    row = lax.broadcasted_iota(jnp.int32, (64, T), 0)
    expert_of_row = jnp.where(row % 8 < 4, (row // 8) * 4 + row % 8, -1)
    slots = jnp.full((64, T), -1.0, F32)
    for k in range(4):
        tgt = target[pl.ds(k, 1), :]
        slots = jnp.where(expert_of_row == tgt // 64, (tgt % 64).astype(F32), slots)
    member = slots >= 0.0
    masked = jnp.where(member, logits, NEG)
    top = jnp.max(masked, axis=0, keepdims=True)
    weight = jnp.where(member, jnp.exp(masked - top), 0.0)
    gates = weight / jnp.sum(weight, axis=0, keepdims=True)
    gates_ref[...] = gates
    for r in range(8):
        meta_send[r, pl.ds(0, 8), :] = gates[r * 8:r * 8 + 8]
        meta_send[r, pl.ds(8, 8), :] = slots[r * 8:r * 8 + 8]
    meta_k = sem_block(8)
    metag[g] = meta_send[g]
    for rel in range(1, 8):
        r = gs[rel]
        send(lambda r=r: meta_send.at[r], lambda: metag.at[g], meta_k + rel, {"expert": r})
    svc(2)
    gh = gather_h
    gh.wait_sib_own()
    gh.step_m1()
    gh.step_p1()
    svc(1)
    gh.step_far()
    for gz in (gather_dy, gh):
        gz.wait_sib_m1()
        gz.wait_sib_p1()
        gz.wait_sib_far()
    gather_dy.wait_sib_own()
    local_dy().wait()
    for rel in range(1, 8):
        arrived(metag.at[gs[8 - rel]], meta_k + rel)
    for copy in local_w:
        copy().wait()

    def weight_of(h, e, n):
        return gathered[h, e, :, pl.ds(n * 16, 16), :].reshape(T, D)

    slot_at = lax.broadcasted_iota(jnp.int32, (64, T), 0).astype(F32)

    def expert(e, rows_ref, grows_ref, dyr_ref, act_ref, dg_ref, du_ref):
        for item in weights:
            if item == ("expert", e):
                break

        def build(s, carry):
            hot = (slot_at == metag[s, pl.ds(8 + e, 1), :]).astype(F32)
            hot_low = hot.astype(BF)
            rows = pl.ds(pl.multiple_of(s * 64, 64), 64)
            rows_ref[rows, :] = nn(hot_low, h2g[s]).astype(BF)
            dyr = nn(hot_low, dyg[s])
            gcol = jnp.sum(hot * metag[s, pl.ds(e, 1), :], axis=1, keepdims=True)
            dyr_ref[rows, :] = dyr.astype(BF)
            grows_ref[rows, :] = (dyr * gcol).astype(BF)
            return carry

        lax.fori_loop(0, 8, build, 0)

        for h in range(2):
            cols = pl.ds(h * T, T)
            bias_g = gu_bias[e, pl.ds(0, 1), cols]
            bias_u = gu_bias[e, pl.ds(1, 1), cols]

            def hidden(i, carry, h=h, cols=cols, bias_g=bias_g, bias_u=bias_u):
                rows = pl.ds(pl.multiple_of(i * 128, 128), 128)
                wg = weight_of(h, e, 0)
                wu = weight_of(h, e, 1)
                wd = weight_of(h, e, 2)
                rv = rows_ref[rows, :]
                gc = LIMIT * jnp.tanh((nt(rv, wg) + bias_g) * (1.0 / LIMIT))
                uc = LIMIT * jnp.tanh((nt(rv, wu) + bias_u) * (1.0 / LIMIT))
                da = nt(grows_ref[rows, :], wd)
                sig = 1.0 / (1.0 + jnp.exp(-ALPHA * gc))
                glu = gc * sig
                act_ref[rows, cols] = ((uc + 1.0) * glu).astype(BF)
                gr, ur = gc * (1.0 / LIMIT), uc * (1.0 / LIMIT)
                dg = da * (uc + 1.0) * (sig + ALPHA * glu * (1.0 - sig)) * (1.0 - gr * gr)
                du = da * glu * (1.0 - ur * ur)
                dg_low, du_low = dg.astype(BF), du.astype(BF)
                dg_ref[rows, cols] = dg_low
                du_ref[rows, cols] = du_low
                return (carry[0] + jnp.sum(dg_low.astype(F32), axis=0, keepdims=True),
                        carry[1] + jnp.sum(du_low.astype(F32), axis=0, keepdims=True))

            zero = jnp.zeros((1, T), F32)
            sum_g, sum_u = lax.fori_loop(0, 4, hidden, (zero, zero))
            d_gub[e, pl.ds(0, 1), cols] = sum_g
            d_gub[e, pl.ds(1, 1), cols] = sum_u

        def outputs(i, carry):
            rows = pl.ds(pl.multiple_of(i * 128, 128), 128)
            out = down_bias[pl.ds(e, 1), :]
            drow = jnp.zeros((128, D), F32)
            for h in range(2):
                cols = pl.ds(h * T, T)
                out = out + nn(act_ref[rows, cols], weight_of(h, e, 2))
                drow = (drow + nn(dg_ref[rows, cols], weight_of(h, e, 0))
                        + nn(du_ref[rows, cols], weight_of(h, e, 1)))
            out_low = out.astype(BF)
            dgate = jnp.sum(dyr_ref[rows, :].astype(F32) * out_low.astype(F32), axis=1, keepdims=True)
            drow_low = drow.astype(BF)
            for n in range(2):
                s = i * 2 + n
                outb[s, pl.ds(e * 64, 64), :] = out_low[n * 64:n * 64 + 64]
                drb[s, pl.ds(e * 64, 64), :] = drow_low[n * 64:n * 64 + 64]
                hot = (slot_at == metag[s, pl.ds(8 + e, 1), :]).astype(F32)
                dgt_send[s, pl.ds(e, 1), :] = jnp.sum(hot * dgate[n * 64:n * 64 + 64], axis=0, keepdims=True)
            return carry + jnp.sum(grows_ref[rows, :].astype(F32), axis=0, keepdims=True)

        small[pl.ds(8 + e, 1), :] = lax.fori_loop(0, 4, outputs, jnp.zeros((1, D), F32))

        drain(pending_weights[e])
        for h in range(2):
            for n, (left, right) in enumerate(((dg_ref, rows_ref), (du_ref, rows_ref), (act_ref, grows_ref))):
                grad = tn(left[:, pl.ds(h * T, T)], right[...])
                gathered[h, e, :, pl.ds(n * 16, 16), :] = grad.astype(BF).reshape(16, 16, D)

    rs_k = sem_block(8 * 9)
    rs_kf = sem_block(8 * 8)
    out_copies = []

    def full_slot(e, h, side, da):
        if e < 2:
            return rs_full.at[e, h, side, da]
        return h2g.at[((e - 2) * 2 + h) * 2 + side, pl.ds(da * 48, 48)]

    def weight_scatter(e, h):
        k = rs_k + (e * 2 + h) * 9
        kf = rs_kf + (e * 2 + h) * 8
        fwd, back = xy(axis_of(h, 1), 1), xy(axis_of(h, 1), 3)
        fwd2, back2 = xy(axis_of(h, 0), 1), xy(axis_of(h, 0), 3)

        def add(s, refs):
            v = gathered[h, e, s].astype(F32)
            for ref in refs:
                v = v + ref[...].astype(F32)
            gathered[h, e, s] = v.astype(BF)

        for n in range(2):
            send(lambda n=n: gathered.at[h, e, slot(h, n, 2)], lambda n=n: rs_half.at[e, h, 0, n], k + n, fwd)
            send(lambda n=n: gathered.at[h, e, slot(h, n + 2, 2)], lambda n=n: rs_half.at[e, h, 1, n], k + 2 + n, back)
        yield 1
        for side, db, dev in ((0, 1, fwd), (1, 3, back)):
            if e == 2:
                pl.semaphore_wait(credit.at[h, side], 1)
            for n in range(2):
                arrived(rs_half.at[e, h, side, n], k + side * 2 + n)
                add(slot(h, side * 2 + n, db), [rs_half.at[e, h, side, n]])
            for da in range(4):
                send(lambda da=da, db=db: gathered.at[h, e, slot(h, da, db)],
                     lambda da=da, side=side: full_slot(e, h, side, da), kf + side * 4 + da, dev)
        yield 2
        for da in (2, 1, 3, 0):
            s = slot(h, da, 0)
            for side in range(2):
                arrived(full_slot(e, h, side, da), kf + side * 4 + da)
            add(s, [full_slot(e, h, 0, da), full_slot(e, h, 1, da)])
            if da == 2:
                send(lambda s=s: gathered.at[h, e, s], lambda: rs2_half.at[e, h], k + 4, fwd2 if e % 2 == 0 else back2)
        yield 3
        arrived(rs2_half.at[e, h], k + 4)
        add(slot(h, 1 if e % 2 == 0 else 3, 0), [rs2_half.at[e, h]])
        send(lambda: gathered.at[h, e, slot(h, 1, 0)], lambda: rs2_full.at[e, h, 0], k + 5, fwd2)
        send(lambda: gathered.at[h, e, slot(h, 3, 0)], lambda: rs2_full.at[e, h, 1], k + 6, back2)
        yield 4
        for side in range(2):
            arrived(rs2_full.at[e, h, side], k + 5 + side)
        add(slot(h, 0, 0), [rs2_full.at[e, h, 0], rs2_full.at[e, h, 1]])
        out_copies.append(local_copy(lambda: gathered.at[h, e, dp], lambda: d_weights.at[h, e]))
        yield 5

    scatters = [[weight_scatter(e, h) for h in range(2)] for e in range(4)]

    def wsvc(*experts):
        for e in experts:
            for h in range(2):
                next(scatters[e][h], None)

    def experts(*refs):
        for e in range(4):
            expert(e, *refs)
            if e == 3:
                drain(pending_gather)
                for h in range(2):
                    pl.semaphore_signal(credit.at[h, 1], inc=1, device_id=xy(axis_of(h, 1), 1), device_id_type=MESH)
                    pl.semaphore_signal(credit.at[h, 0], inc=1, device_id=xy(axis_of(h, 1), 3), device_id_type=MESH)
            wsvc(e)
            if e >= 1:
                wsvc(e - 1)

    pl.run_scoped(
        experts,
        pltpu.VMEM((512, D), BF), pltpu.VMEM((512, D), BF), pltpu.VMEM((512, D), BF),
        pltpu.VMEM((512, 512), BF), pltpu.VMEM((512, 512), BF), pltpu.VMEM((512, 512), BF))

    dg_k = sem_block(8)
    dgt_in[g] = dgt_send[g]
    for rel in range(1, 8):
        r = gs[rel]
        send(lambda r=r: dgt_send.at[r], lambda: dgt_in.at[g], dg_k + rel, {"expert": r})

    def combine(buf, s, gated):
        pieces = []
        for e in range(4):
            hot = (slot_at == metag[s, pl.ds(8 + e, 1), :]).astype(F32)
            if gated:
                hot = hot * metag[s, pl.ds(e, 1), :]
            pieces.append(hot)
        spread = jnp.concatenate(pieces, axis=0).T.astype(BF)
        buf[s] = nn(spread, buf[s]).astype(BF)

    scatter_d = ScatterZ(drb, lambda n: sib_in.at[n], lambda n: half_in.at[n], lambda n: full_in.at[n])
    far_chunks, own_chunks = scatter_d.chunks()
    for n in range(4):
        combine(drb, far_chunks[n], False)
        scatter_d.to_sibling(n)
    combine(drb, own_chunks[0], False)
    scatter_d.step1()
    combine(drb, own_chunks[1], False)
    combine(drb, own_chunks[2], False)
    wsvc(0)
    scatter_d.step2()
    combine(drb, own_chunks[3], False)
    wsvc(3)
    for n in range(4):
        combine(outb, far_chunks[n], True)
    for n in range(4):
        combine(outb, own_chunks[n], True)
    wsvc(0)
    scatter_d.step3()

    for rel in range(1, 8):
        arrived(dgt_in.at[gs[8 - rel]], dg_k + rel)
    d_gates = jnp.where(row % 8 < 4, jnp.concatenate([dgt_in[r] for r in range(8)], axis=0), 0.0)
    d_logits = gates_ref[...] * (d_gates - jnp.sum(gates_ref[...] * d_gates, axis=0, keepdims=True))
    dl_high, dl_low = split_low(d_logits)
    d_wrt[...] = nn(dl_high, h2own[...]) + nn(dl_low, h2own[...])
    d_brt[...] = jnp.broadcast_to(jnp.sum(d_logits, axis=1, keepdims=True), (64, 128))
    dl_high_t, dl_low_t = split_low(d_logits.T)
    d_middle[...] = nn(dl_high_t, w_rt[...]) + nn(dl_low_t, w_rt[...])
    drain(scatter_d.sent)
    att_at, branch_at = gs[1], gs[2]

    def middle_back(i, carry):
        rows = pl.ds(pl.multiple_of(i * 64, 64), 64)
        m = middle[rows, :]
        inv = lax.rsqrt(jnp.mean(m * m, axis=-1, keepdims=True) + EPS)
        d_h2 = scatter_d.result(rows) + d_middle[rows, :]
        v2 = d_h2 * moe_gain[...]
        inner = jnp.mean(v2 * m, axis=-1, keepdims=True)
        dm = dyg[g, rows, :].astype(F32) + inv * v2 - m * (inv * inv * inv * inner)
        d_middle[rows, :] = dm
        low = dm.astype(BF)
        drb[branch_at, rows, :] = low
        drb[att_at, rows, :] = nt(low, w_out[...]).astype(BF)
        return (carry[0] + jnp.sum(low.astype(F32), axis=0, keepdims=True),
                carry[1] + jnp.sum(d_h2 * m * inv, axis=0, keepdims=True))

    zero_row = jnp.zeros((1, D), F32)
    sum_b, sum_m = lax.fori_loop(0, 4, middle_back, (zero_row, zero_row))
    small[pl.ds(1, 1), :] = sum_b
    small[pl.ds(2, 1), :] = sum_m

    do_k = sem_block(8)
    att_sent = []
    dob[g] = drb[att_at, :, pl.ds(pl.multiple_of(g * 128, 128), 128)]
    for rel in range(1, 8):
        r = gs[rel]
        send(lambda r=r: drb.at[att_at, :, pl.ds(pl.multiple_of(r * 128, 128), 128)], lambda: dob.at[g], do_k + rel, {"expert": r}, att_sent)

    def wout_part(stage_ref):
        for n in range(4):
            rows = pl.ds(n * 256, 256)
            stage_ref[rows, :] = tn(att[:, rows], drb[branch_at]).astype(BF)
        wsvc(1)
        local_copy(stage_ref, d_wout)().wait()

    pl.run_scoped(wout_part, pltpu.VMEM((D, D), BF))
    for rel in range(1, 8):
        arrived(dob.at[gs[8 - rel]], do_k + rel)

    scatter_m = ScatterZ(
        outb, lambda n: dyg.at[n], lambda n: dyg.at[4, pl.ds(n * 128, 128)], lambda n: dyg.at[5 + n])
    for n in range(4):
        scatter_m.to_sibling(n)

    sub_low = lax.broadcasted_iota(jnp.int32, (128, 1), 0) < 64
    smask0 = jnp.where(sub_low, 1.0, 0.0).astype(F32)
    smask1 = 1.0 - smask0

    def stacked_t(v_t):
        return jnp.concatenate([v_t * smask0, v_t * smask1], axis=1).astype(BF)

    def attend_back(i, dk_ref, dv_ref, dqkv_ref, dq_ref):
        q2 = stacked(qs[i])
        q2t = stacked_t(qs[i].astype(F32).T)
        do2 = stacked(dob[i])
        do_t = dob[i].astype(F32).T
        do2t = stacked_t(do_t)
        prod = do_t * att_send[i].astype(F32).T
        delta = jnp.concatenate(
            [jnp.sum(prod[:64], axis=0, keepdims=True), jnp.sum(prod[64:], axis=0, keepdims=True)], axis=1)
        lse_row = lse[i]
        small[pl.ds(4, 1), pl.ds(0, 512)] -= jnp.exp(sink_row[...] - lse_row) * delta
        dq_ref[...] = jnp.zeros((128, 2 * T), F32)

        def block(j, diagonal):
            p = jnp.exp(nn(kk[j], q2t) - lse_row)
            if diagonal:
                p = jnp.where(allowed, p, 0.0)
            ds = (p * (nn(vv[j], do2t) - delta)).astype(BF)
            dv_ref[j] += nn(p.astype(BF), do2)
            dk_ref[j] += nn(ds, q2)
            dq_ref[...] += nn(kkt[j], ds)

        if i > 0:
            def body(j, carry):
                block(j, False)
                return carry
            lax.fori_loop(0, i, body, 0)
        block(i, True)
        dq = dq_ref[...].T
        dq = jnp.where(low_half, dq[:T], dq[T:]) * 0.125
        cosine, sine = trig(i)
        dqkv_ref[i, :, pl.ds(0, 128)] = (dq * cosine - swap(dq) * sine).astype(BF)

    def backward(dk_ref, dv_ref, dqkv_ref, dq_ref, dw_ref):
        dk_ref[...] = jnp.zeros((8, T, 128), F32)
        dv_ref[...] = jnp.zeros((8, T, 128), F32)
        plan = {0: (1,), 1: (0,), 2: (2,), 3: (1,), 4: (3,), 5: (2,), 6: (3,), 7: (2,)}
        for i in range(8):
            attend_back(i, dk_ref, dv_ref, dqkv_ref, dq_ref)
            wsvc(*plan[i])
            if i == 3:
                scatter_m.step1()
            if i == 5:
                scatter_m.step2()
        drain(att_sent)

        def finish(r, carry):
            cosine, sine = trig(r)
            dk = dk_ref[r]
            dk = dk + pltpu.roll(dk, 64, 1)
            dv = dv_ref[r]
            dv = dv + pltpu.roll(dv, 64, 1)
            dkv = jnp.where(low_half, dk * cosine - swap(dk) * sine, dv)
            dqkv_ref[r, :, pl.ds(128, 128)] = dkv.astype(BF)
            return carry + jnp.sum(dqkv_ref[r].astype(F32), axis=0, keepdims=True)

        small[pl.ds(3, 1), pl.ds(0, T)] = lax.fori_loop(0, 8, finish, jnp.zeros((1, T), F32))

        scatter_h = ScatterZ(drb, lambda n: sib_in.at[n], lambda n: half_in.at[n], lambda n: full_in.at[n])

        def d_h1_chunk(s):
            drb[s] = nt(dqkv_ref[s], w_qkv[...]).astype(BF)

        for n in range(4):
            d_h1_chunk(far_chunks[n])
            scatter_h.to_sibling(n)
        d_h1_chunk(own_chunks[0])
        scatter_h.step1()
        d_h1_chunk(own_chunks[1])
        d_h1_chunk(own_chunks[2])
        scatter_h.step2()
        d_h1_chunk(own_chunks[3])

        dw_ref[...] = jnp.zeros((T, D), F32)

        def dw_part(r, carry):
            dw_ref[...] += tn(dqkv_ref[r], h1_rows(r, pl.ds(0, T)))
            return carry

        lax.fori_loop(0, 8, dw_part, 0)
        cp = local_copy(dw_ref, d_wqkv_t)
        scatter_m.step3()

        def result(i, carry):
            rows = pl.ds(pl.multiple_of(i * 64, 64), 64)
            att[rows, :] = (middle[rows, :] + scatter_m.result(rows)).astype(BF)
            return carry

        lax.fori_loop(0, 4, result, 0)
        cp2 = local_copy(att, block_out)
        wsvc(3)
        scatter_h.step3()

        def tokens_back(i, carry):
            rows = pl.ds(pl.multiple_of(i * 64, 64), 64)
            xf = xg[g, rows, :].astype(F32)
            inv = lax.rsqrt(jnp.mean(xf * xf, axis=-1, keepdims=True) + EPS)
            d_h1 = scatter_h.result(rows)
            v1 = d_h1 * attn_gain[...]
            inner = jnp.mean(v1 * xf, axis=-1, keepdims=True)
            h2own[rows, :] = (d_middle[rows, :] + inv * v1 - xf * (inv * inv * inv * inner)).astype(BF)
            return carry + jnp.sum(d_h1 * xf * inv, axis=0, keepdims=True)

        small[pl.ds(0, 1), :] = lax.fori_loop(0, 4, tokens_back, zero_row)
        cp3 = local_copy(h2own, d_tokens)
        wsvc(3)
        drain(scatter_h.sent)
        drain(scatter_m.sent)
        for copy in (cp, cp2, cp3):
            copy().wait()

    pl.run_scoped(
        backward, pltpu.VMEM((8, T, 128), F32), pltpu.VMEM((8, T, 128), F32), pltpu.VMEM((8, T, T), BF),
        pltpu.VMEM((128, 2 * T), F32), pltpu.VMEM((T, D), F32))
    for e in range(4):
        wsvc(e, e, e, e)
    drain(pending)
    for copy in out_copies:
        copy().wait()


ANY = pl.BlockSpec(memory_space=pl.ANY)
VM = pl.BlockSpec(memory_space=pltpu.VMEM)


def angle_tables():
    frequency = np.exp(np.arange(32, dtype=np.float32) * np.float32(-2.0 * np.log(THETA) / 64)).astype(np.float64)
    freq = np.tile(frequency, 4)[None, :]
    near = np.arange(T, dtype=np.float64)[:, None] * freq
    far = np.arange(8, dtype=np.float64)[:, None] * T * freq
    return [f(a).astype(np.float32) for a in (near, far) for f in (np.cos, np.sin)]


def per_device(
    tokens, cotangent, routes, slot_ids, attn_gain, w_qkv, b_qkv, w_out, b_out, sink_logits, moe_gain,
    w_router, b_router, gu_weight, gu_bias, down_weight, down_bias,
):
    g = lax.axis_index("expert")
    both = jnp.concatenate([gu_weight.transpose(0, 2, 1, 3), down_weight[:, None]], axis=1)
    shard = both.reshape(4, 3, 2, 16, D).transpose(2, 0, 1, 3, 4).reshape(2, 4, 48, D)
    target = jnp.pad((routes * 64 + slot_ids).T, ((0, 4), (0, 0)))

    def own_columns(v):
        return jnp.concatenate(
            [lax.dynamic_slice_in_dim(v, g * 128, 128, 1), lax.dynamic_slice_in_dim(v, 1024 + g * 64, 64, 1),
             lax.dynamic_slice_in_dim(v, 1536 + g * 64, 64, 1)], axis=1)

    sinks = jnp.repeat(lax.dynamic_slice_in_dim(sink_logits, g * 2, 2, 0), T)[None, :]

    def padded(v):
        return jnp.pad(v.reshape(8, 4, -1), ((0, 0), (0, 4), (0, 0))).reshape(64, -1)

    w_rt = padded(w_router.T)
    b_rt = jnp.broadcast_to(padded(b_router), (64, T))
    gub = gu_bias.reshape(4, 2, 16, 2, 16).transpose(0, 1, 3, 2, 4).reshape(4, 2, 512)
    down_own = lax.dynamic_slice_in_dim(down_bias, g * 4, 4, 0)
    cos_a, sin_a, cos_b, sin_b = [jnp.asarray(t) for t in angle_tables()]
    shape = jax.ShapeDtypeStruct
    out = pl.pallas_call(
        layer_kernel,
        out_shape=(
            shape((T, D), BF), shape((T, D), BF), shape((2, 4, 48, D), BF), shape((T, D), F32), shape((D, D), BF),
            shape((16, D), F32), shape((64, D), F32), shape((64, 128), F32), shape((4, 2, 512), F32),
        ),
        in_specs=[ANY, ANY, ANY] + [VM] * 16,
        out_specs=[ANY, ANY, ANY, ANY, ANY, VM, VM, VM, VM],
        scratch_shapes=[
            pltpu.VMEM((8, T, D), BF), pltpu.VMEM((8, T, D), BF), pltpu.VMEM((8, T, D), BF),
            pltpu.VMEM((2, 4, 16, 48, D), BF),
            pltpu.VMEM((8, T, 128), BF), pltpu.VMEM((8, T, 128), BF), pltpu.VMEM((8, T, 128), BF),
            pltpu.VMEM((8, 128, T), BF), pltpu.VMEM((8, 128, T), BF),
            pltpu.VMEM((8, 1, 2 * T), F32), pltpu.VMEM((8, T, 128), BF), pltpu.VMEM((T, D), BF),
            pltpu.VMEM((T, D), F32), pltpu.VMEM((T, D), BF),
            pltpu.VMEM((8, 16, T), F32), pltpu.VMEM((8, 16, T), F32),
            pltpu.VMEM((8, T, D), BF), pltpu.VMEM((8, T, D), BF),
            pltpu.VMEM((4, T, D), BF), pltpu.VMEM((2, 128, D), BF), pltpu.VMEM((2, T, D), BF),
            pltpu.VMEM((4, 2, 2, 2, 48, D), BF), pltpu.VMEM((2, 2, 2, 4, 48, D), BF),
            pltpu.VMEM((4, 2, 48, D), BF), pltpu.VMEM((4, 2, 2, 48, D), BF),
            pltpu.VMEM((8, T, 128), BF), pltpu.VMEM((8, 8, T), F32), pltpu.VMEM((8, 8, T), F32),
            pltpu.VMEM((T, D), F32),
            pltpu.VMEM((64, T), F32),
            pltpu.SemaphoreType.DMA((NSEM,)), pltpu.SemaphoreType.REGULAR((2, 2)),
        ],
        compiler_params=pltpu.CompilerParams(collective_id=1, has_side_effects=True, vmem_limit_bytes=VLIM),
    )(tokens, cotangent, shard, target, attn_gain[None], own_columns(w_qkv), own_columns(b_qkv[None]), w_out, b_out[None],
      sinks, moe_gain[None], w_rt, b_rt, gub, down_own, cos_a, sin_a, cos_b, sin_b)
    block_out, d_tokens, d_weights, d_wq, d_wo, small, d_wrt, d_brt, d_gub = out

    def unpadded(v):
        return v.reshape(8, 8, -1)[:, :4].reshape(32, -1)

    d_wq = lax.all_gather(lax.psum(d_wq, "dp"), "expert", axis=0)
    own = lax.all_gather(lax.psum((small[3, :256], small[4, :512].reshape(2, 256).sum(1), small[8:12]), "dp"), "expert", axis=0)
    d_bq, d_sinks, d_down_bias = own
    every = lax.psum((small[0], small[1], small[2], unpadded(d_wrt), unpadded(d_brt)[:, 0], d_wo.astype(F32)), ("dp", "expert"))

    def whole(v):
        return jnp.concatenate([v[:, :128].reshape((1024,) + v.shape[2:]), v[:, 128:192].reshape((512,) + v.shape[2:]),
                                v[:, 192:].reshape((512,) + v.shape[2:])], axis=0)

    d_gub = lax.psum_scatter(d_gub.reshape(4, 2, 2, 16, 16).transpose(3, 0, 1, 2, 4).reshape(16, 4, 2, 32), "dp", scatter_dimension=0, tiled=False)
    dw = d_weights.astype(F32).reshape(2, 4, 3, 16, D).transpose(1, 0, 3, 2, 4).reshape(4, 32, 3, D)
    return (
        block_out, d_tokens, every[0], whole(d_wq).T, whole(d_bq), every[5], every[1], d_sinks.reshape(16),
        every[2], every[3].T, every[4], dw[:, :, :2], d_gub, dw[:, :, 2], d_down_bias.reshape(32, D),
    )


def solution(mesh):
    rows = P(("dp", "expert"), None)
    in_specs = (rows,) * 4 + (P(),) * 9 + (
        P("expert", "dp", None, None), P("expert", None, None), P("expert", "dp", None), P())
    out_specs = (rows,) * 2 + (P(),) * 9 + (
        P("expert", "dp", None, None), P("expert", None, "dp"), P("expert", "dp", None), P())
    return jax.shard_map(per_device, mesh=mesh, in_specs=in_specs, out_specs=out_specs, check_vma=False)
```

```python
import functools

import jax
import jax.numpy as jnp
import numpy as np
from jax import lax
from jax.experimental import pallas as pl
from jax.experimental.pallas import tpu as pltpu
from jax.sharding import PartitionSpec as P

MESH = pl.DeviceIdType.MESH
BF = jnp.bfloat16
F32 = jnp.float32
EPS = 1e-05
THETA = 10000.0
LIMIT = 7.0
ALPHA = 1.702
NEG = -1000000000.0
NSEM = 380
VLIM = 63 << 20
T = 256
D = 1024


def nt(a, b):
    return lax.dot_general(a, b, (((1,), (1,)), ((), ())), preferred_element_type=F32)


def tn(a, b):
    return lax.dot_general(a, b, (((0,), (0,)), ((), ())), preferred_element_type=F32)


def nn(a, b):
    return jnp.dot(a, b, preferred_element_type=F32)


def split_low(v):
    high = v.astype(BF)
    return high, (v - high.astype(F32)).astype(BF)


def layer_kernel(
    x_in, dy_in, w_in, w_qkv_in, target, attn_gain, b_qkv_in, w_out, b_out, sinks, moe_gain,
    w_rt, b_rt, gu_bias, down_bias, cos_a, sin_a, cos_b, sin_b,
    block_out, d_tokens, d_gate_w, d_up_w, d_down_w, d_wqkv, d_wout, early_out, final_out,
    xg, dyg, h2g, gathered, qs, kk, vv, kkt, vvt, lse, att_send, att, middle, h2own, metag, meta_send,
    outb, drb, sib_in, half_in, full_in, rs_half, rs_full, rs2_half, rs2_full, dob, dgt_send, dgt_in,
    d_middle, gates_ref, params, own_rows, common_rows, early, early_in, early_all, late, late_in, late_all,
    w_qkv, b_qkv, sink_row, final, sems, credit, free_z, free_xy, passed,
):
    dp = lax.axis_index("dp")
    g = lax.axis_index("expert")
    y, x = lax.div(dp, 4), lax.rem(dp, 4)
    z, c = lax.div(g, 2), lax.rem(g, 2)
    xs = [lax.rem(x + d, 4) for d in range(4)]
    ys = [lax.rem(y + d, 4) for d in range(4)]
    zs = [lax.rem(z + d, 4) for d in range(4)]
    gs = [lax.rem(g + d, 8) for d in range(8)]
    other = 1 - c
    sib = {"expert": z * 2 + (1 - c)}
    up = {"expert": zs[1] * 2 + c}
    down = {"expert": zs[3] * 2 + c}

    neighbours = {
        "x": [{"dp": y * 4 + xs[d]} for d in range(4)],
        "y": [{"dp": ys[d] * 4 + x} for d in range(4)],
    }

    def xy(axis, d):
        return neighbours[axis][d]

    first = [xs, ys]
    second = [ys, xs]

    lines = [[second[h][db] * 4 for db in range(4)] for h in range(2)]

    def slot(h, da, db):
        return second[h][db] * 4 + first[h][da]

    counter = [0]

    def sem():
        counter[0] += 1
        assert counter[0] <= NSEM
        return counter[0] - 1

    def sem_block(n):
        first = counter[0]
        counter[0] += n
        assert counter[0] <= NSEM
        return first

    def view(ref):
        return ref() if callable(ref) else ref

    class Ring:
        def __init__(self, n):
            self.base, self.n, self.at, self.live = sem_block(n), n, 0, {}

        def take(self, copy):
            k = self.base + self.at % self.n
            self.at += 1
            if k in self.live:
                self.live[k].wait()
            self.live[k] = copy
            return k

    class Remote:
        def __init__(self, src, dst, recv, dev, ring):
            self.src, self.dst, self.recv, self.dev, self.done = src, dst, recv, dev, False
            self.n = ring.take(self)
            self.make().start()

        def make(self):
            return pltpu.make_async_remote_copy(
                src_ref=view(self.src), dst_ref=view(self.dst), send_sem=sems.at[self.n], recv_sem=sems.at[self.recv],
                device_id=self.dev, device_id_type=MESH)

        def wait(self):
            if not self.done:
                self.make().wait_send()
                self.done = True

    class Local(Remote):
        def __init__(self, src, dst, ring):
            self.src, self.dst, self.done = src, dst, False
            self.n = ring.take(self)
            self.make().start()

        def make(self):
            return pltpu.make_async_copy(view(self.src), view(self.dst), sems.at[self.n])

        def wait(self):
            if not self.done:
                self.make().wait()
                self.done = True

    ring_w, ring_z, ring_l = Ring(120), Ring(80), Ring(40)
    pending = []
    pending_gather = []
    pending_weights = [[] for _ in range(4)]

    def send(src, dst, recv, dev, keep, ring=ring_z):
        keep.append(Remote(src, dst, recv, dev, ring))

    def local_copy(src, dst):
        return Local(src, dst, ring_l)

    def arrived(dst, recv):
        pltpu.make_async_remote_copy(
            src_ref=dst, dst_ref=dst, send_sem=sems.at[recv], recv_sem=sems.at[recv],
            device_id=sib, device_id_type=MESH,
        ).wait_recv()

    def drain(copies):
        for copy in copies:
            copy.wait()
        copies.clear()

    barrier = pltpu.get_barrier_semaphore()
    for rel in range(1, 8):
        pl.semaphore_signal(barrier, inc=1, device_id={"expert": gs[rel]}, device_id_type=MESH)
    for axis in ("x", "y"):
        for d in (1, 2, 3):
            pl.semaphore_signal(barrier, inc=1, device_id=xy(axis, d), device_id_type=MESH)
    pl.semaphore_wait(barrier, 13)

    class GatherZ:
        def __init__(self, buf, own):
            self.buf, self.own = buf, own
            self.k = sem_block(9)
            self.m1, self.p1, self.far = zs[3] * 2 + c, zs[1] * 2 + c, zs[2] * 2 + c
            s = 1 - c
            self.sm1, self.sp1, self.sfar, self.so = (
                zs[3] * 2 + s, zs[1] * 2 + s, zs[2] * 2 + s, z * 2 + s)

        def start(self):
            b, k = self.buf, self.k
            send(self.own, lambda: b.at[g], k + 1, up, pending_gather)
            send(self.own, lambda: b.at[g], k + 2, down, pending_gather)
            send(self.own, lambda: b.at[g], k + 0, sib, pending_gather)

        def step_m1(self):
            b, k, s = self.buf, self.k, self.m1
            arrived(b.at[s], k + 1)
            send(lambda: b.at[s, pl.ds(0, 128)], lambda: b.at[s, pl.ds(0, 128)], k + 3, up, pending_gather)
            send(lambda: b.at[s], lambda: b.at[s], k + 4, sib, pending_gather)

        def step_p1(self):
            b, k, s = self.buf, self.k, self.p1
            arrived(b.at[s], k + 2)
            send(lambda: b.at[s, pl.ds(128, 128)], lambda: b.at[s, pl.ds(128, 128)], k + 5, down, pending_gather)
            send(lambda: b.at[s], lambda: b.at[s], k + 6, sib, pending_gather)

        def step_far(self):
            b, k, s = self.buf, self.k, self.far
            for i, kr, ks in ((0, 3, 7), (128, 5, 8)):
                arrived(b.at[s, pl.ds(i, 128)], k + kr)
                send(lambda i=i: b.at[s, pl.ds(i, 128)], lambda i=i: b.at[s, pl.ds(i, 128)], k + ks, sib, pending_gather)

        def wait_sib_own(self):
            arrived(self.buf.at[self.so], self.k)

        def wait_sib_m1(self):
            arrived(self.buf.at[self.sm1], self.k + 4)

        def wait_sib_p1(self):
            arrived(self.buf.at[self.sp1], self.k + 6)

        def wait_sib_far(self):
            for i, ks in ((0, 7), (128, 8)):
                arrived(self.buf.at[self.sfar, pl.ds(i, 128)], self.k + ks)

    class ScatterZ:
        def __init__(self, k, buf, sib_ref, half_ref, full_ref, sizes=(128, 128)):
            self.buf, self.r, self.h, self.f = buf, sib_ref, half_ref, full_ref
            self.sizes, self.rows = sizes, sum(sizes)
            self.k = k
            self.sent = []

        def chunks(self):
            return [zs[d] * 2 + (1 - c) for d in (2, 1, 3, 0)], [zs[d] * 2 + c for d in (2, 1, 3, 0)]

        def to_sibling(self, n):
            d = (2, 1, 3, 0)[n]
            zz = zs[d]
            send(lambda: self.buf.at[zz * 2 + (1 - c), pl.ds(0, self.rows)], lambda: self.r(d), self.k + n, sib, self.sent)

        def add(self, chunk, refs, base=0, rows=None):
            rows = rows or self.rows
            step = 64 if rows % 64 == 0 else 16

            def body(i, carry):
                at = pl.ds(pl.multiple_of(base + i * step, 16), step)
                ref_at = pl.ds(pl.multiple_of(i * step, 16), step)
                v = self.buf[chunk, at, :].astype(F32)
                for ref in refs:
                    v = v + ref[ref_at, :].astype(F32)
                self.buf[chunk, at, :] = v.astype(BF)
                return carry
            lax.fori_loop(0, rows // step, body, 0)

        def step1(self):
            b, k = self.buf, self.k
            chunk = zs[2] * 2 + c
            arrived(self.r(2), k + 0)
            self.add(chunk, [self.r(2)])
            lo, hi = self.sizes
            send(lambda: b.at[chunk, pl.ds(0, lo)], lambda: self.h(0), k + 4, up, self.sent)
            send(lambda: b.at[chunk, pl.ds(lo, hi)], lambda: self.h(1), k + 5, down, self.sent)

        def step2(self):
            b, k = self.buf, self.k
            for d, n, hi, dev in ((1, 1, 0, up), (3, 2, 1, down)):
                chunk = zs[d] * 2 + c
                arrived(self.r(d), k + n)
                self.add(chunk, [self.r(d)])
                arrived(self.h(hi), k + 4 + hi)
                self.add(chunk, [self.h(hi)], hi * self.sizes[0], self.sizes[hi])
                send(lambda chunk=chunk: b.at[chunk, pl.ds(0, self.rows)], lambda hi=hi: self.f(hi), k + 6 + hi, dev, self.sent)

        def step3(self):
            arrived(self.r(0), self.k + 3)
            arrived(self.f(0), self.k + 6)
            arrived(self.f(1), self.k + 7)

        def result(self, rows):
            return (self.buf[g, rows, :].astype(F32) + self.r(0)[rows, :].astype(F32)
                    + self.f(0)[rows, :].astype(F32) + self.f(1)[rows, :].astype(F32))

    around = [xy("x", 1), xy("x", 3), xy("y", 1), xy("y", 3)]

    def axis_of(h, ax):
        return "x" if (ax == 0) == (h == 0) else "y"

    gk = sem_block(2 * 4 * 7)

    def wsem(h, e):
        return gk + (h * 4 + e) * 7

    def row_of(h, e, db):
        return gathered.at[h, e, pl.ds(second[h][db] * 4, 4)]

    def one_of(h, e, da):
        return gathered.at[h, e, slot(h, da, 0)]

    local_w = {}

    def weights_start():
        for e in range(4):
            for h in range(2):
                for n, d in ((0, 1), (1, 3)):
                    send(lambda h=h, e=e: w_in.at[h, e], lambda h=h, e=e: one_of(h, e, 0), wsem(h, e) + n,
                         xy(axis_of(h, 0), d), pending_weights[e], ring_w)
                local_w[h, e] = local_copy(lambda h=h, e=e: w_in.at[h, e], lambda h=h, e=e: one_of(h, e, 0))

    def weights_near(e):
        for h in range(2):
            k = wsem(h, e)
            arrived(one_of(h, e, 3), k)
            if e % 2 == 0:
                send(lambda h=h: one_of(h, e, 3), lambda h=h: one_of(h, e, 3), k + 2, xy(axis_of(h, 0), 1),
                     pending_weights[e], ring_w)
            arrived(one_of(h, e, 1), k + 1)
            if e % 2 == 1:
                send(lambda h=h: one_of(h, e, 1), lambda h=h: one_of(h, e, 1), k + 2, xy(axis_of(h, 0), 3),
                     pending_weights[e], ring_w)

    def weights_turn(e):
        for h in range(2):
            k = wsem(h, e)
            arrived(one_of(h, e, 2), k + 2)
            local_w[h, e].wait()
            for n, d in ((3, 1), (4, 3)):
                send(lambda h=h: row_of(h, e, 0), lambda h=h: row_of(h, e, 0), k + n, xy(axis_of(h, 1), d),
                     pending_weights[e], ring_w)

    def weights_row(e):
        for h in range(2):
            k = wsem(h, e)
            arrived(row_of(h, e, 3), k + 3)
            if e % 2 == 0:
                send(lambda h=h: row_of(h, e, 3), lambda h=h: row_of(h, e, 3), k + 5, xy(axis_of(h, 1), 1),
                     pending_weights[e], ring_w)
            arrived(row_of(h, e, 1), k + 4)
            if e % 2 == 1:
                send(lambda h=h: row_of(h, e, 1), lambda h=h: row_of(h, e, 1), k + 5, xy(axis_of(h, 1), 3),
                     pending_weights[e], ring_w)

    def weights_end(e):
        for h in range(2):
            arrived(row_of(h, e, 2), wsem(h, e) + 5)
        for dev in around:
            pl.semaphore_signal(passed.at[e], inc=1, device_id=dev, device_id_type=MESH)

    def weights_steps():
        order = [(weights_near, 0), (weights_near, 1), (weights_turn, 0), (weights_near, 2), (weights_turn, 1),
                 (weights_near, 3), (weights_turn, 2), (weights_turn, 3), (weights_row, 0), (weights_row, 1),
                 (weights_end, 0), (weights_row, 2), (weights_end, 1), (weights_row, 3), (weights_end, 2),
                 (weights_end, 3)]
        for step, e in order:
            step(e)
            yield (step, e)

    late[0] = jnp.zeros((8, D), F32)
    final[...] = jnp.zeros((8, D), F32)
    own_rows[...] = jnp.zeros((16, D), F32)
    common_rows[...] = jnp.zeros((8, D), F32)
    local_x = local_copy(x_in, lambda: xg.at[g])
    gather_x = GatherZ(xg, x_in)
    gather_x.start()
    weights_start()
    local_q = [
        local_copy(lambda: w_qkv_in.at[:, pl.ds(pl.multiple_of(g * 128, 128), 128)], lambda: w_qkv.at[:, pl.ds(0, 128)]),
        local_copy(lambda: w_qkv_in.at[:, pl.ds(pl.multiple_of(1024 + z * 128, 128), 128)], lambda: w_qkv.at[:, pl.ds(128, 128)]),
    ] + [
        local_copy(lambda n=n: w_qkv_in.at[pl.ds(n * T, T), pl.ds(pl.multiple_of(1536 + z * 128, 128), 128)],
                   lambda n=n: outb.at[n, :, pl.ds(0, 128)])
        for n in range(4)
    ]
    weights = weights_steps()

    def svc(n=1):
        for _ in range(n):
            if next(weights, None) is None:
                return

    lane = lax.broadcasted_iota(jnp.int32, (1, 128), 1)
    low_half = lane < 64
    first_quarter = (lane % 64) < 32
    mask0 = jnp.where(low_half, 1.0, 0.0).astype(F32)
    mask1 = 1.0 - mask0

    def swap(v):
        return jnp.where(first_quarter, pltpu.roll(v, 96, 1), pltpu.roll(v, 32, 1))

    def trig(r):
        cb, sb = cos_b[pl.ds(r, 1), :], sin_b[pl.ds(r, 1), :]
        ca, sa = cos_a[...], sin_a[...]
        cosine = ca * cb - sa * sb
        sine = sa * cb + ca * sb
        return cosine, jnp.where(first_quarter, -sine, sine)

    def h1_rows(r, rows):
        xf = xg[r, rows, :].astype(F32)
        inv = lax.rsqrt(jnp.mean(xf * xf, axis=-1, keepdims=True) + EPS)
        return (xf * inv * attn_gain[...]).astype(BF)

    def qkv_chunk(r):
        h1 = h1_rows(r, pl.ds(0, T))
        mixed = nn(h1, w_qkv[...]) + b_qkv[...]
        cosine, sine = trig(r)
        q = mixed[:, :128]
        kv = mixed[:, 128:]
        q = (q * cosine + swap(q) * sine) * 0.125
        kv = jnp.where(low_half, kv * cosine + swap(kv) * sine, kv)
        other = pltpu.roll(kv, 64, 1)
        kd = jnp.where(low_half, kv, other)
        vd = jnp.where(low_half, other, kv)
        qs[r] = q.astype(BF)
        kk[r] = kd.astype(BF)
        vv[r] = vd.astype(BF)
        kkt[r] = kd.T.astype(BF)
        vvt[r] = vd.T.astype(BF)

    even = c == 0

    def pair(first, second):
        k_own = jnp.where(even, first, pltpu.roll(first, 64, 1))
        v_own = jnp.where(even, pltpu.roll(second, 64, 1), second)
        return jnp.where(low_half, k_own, v_own)

    for copy in local_q:
        copy.wait()

    def pair_rows(i, carry):
        rows = pl.ds(pl.multiple_of(i * 256, 256), 256)
        w_qkv[rows, pl.ds(128, 128)] = pair(
            w_qkv[rows, pl.ds(128, 128)].astype(F32), outb[i, :, pl.ds(0, 128)].astype(F32)).astype(BF)
        return carry

    lax.fori_loop(0, 4, pair_rows, 0)
    b_qkv[:, pl.ds(0, 128)] = b_qkv_in[:, pl.ds(pl.multiple_of(g * 128, 128), 128)]
    b_qkv[:, pl.ds(128, 128)] = pair(
        b_qkv_in[:, pl.ds(pl.multiple_of(1024 + z * 128, 128), 128)],
        b_qkv_in[:, pl.ds(pl.multiple_of(1536 + z * 128, 128), 128)])
    lane_all = lax.broadcasted_iota(jnp.int32, (1, 128), 1)
    for n in range(2):
        one = jnp.sum(jnp.where(lane_all == g * 2 + n, sinks[...], 0.0), axis=1, keepdims=True)
        sink_row[:, pl.ds(n * T, T)] = jnp.broadcast_to(one, (1, T))

    gx = gather_x
    local_x.wait()
    qkv_chunk(g)
    gx.wait_sib_own()
    qkv_chunk(gx.so)
    svc(1)
    gx.step_m1()
    gx.step_p1()
    qkv_chunk(gx.m1)
    svc(1)
    qkv_chunk(gx.p1)
    svc(1)
    gx.wait_sib_m1()
    qkv_chunk(gx.sm1)
    svc(1)
    gx.wait_sib_p1()
    qkv_chunk(gx.sp1)
    svc(1)
    gx.step_far()
    local_dy = local_copy(dy_in, lambda: dyg.at[g])
    gather_dy = GatherZ(dyg, dy_in)
    gather_dy.start()
    qkv_chunk(gx.far)
    svc(1)
    gx.wait_sib_far()
    qkv_chunk(gx.sfar)
    svc(2)

    def stacked(v):
        vf = v.astype(F32)
        return jnp.concatenate([vf * mask0, vf * mask1], axis=0).astype(BF)

    key_at = lax.broadcasted_iota(jnp.int32, (T, 2 * T), 0)
    query_at = lax.broadcasted_iota(jnp.int32, (T, 2 * T), 1) % T
    allowed = key_at <= query_at

    att_k = sem_block(8)

    def attend(i, m_ref, l_ref, acc_ref):
        q2 = stacked(qs[i])
        m_ref[...] = sink_row[...]
        l_ref[...] = jnp.ones((1, 2 * T), F32)
        acc_ref[...] = jnp.zeros((128, 2 * T), F32)

        def block(j, diagonal):
            s = nt(kk[j], q2)
            if diagonal:
                s = jnp.where(allowed, s, NEG)
            m_old = m_ref[...]
            m_new = jnp.maximum(m_old, jnp.max(s, axis=0, keepdims=True))
            p = jnp.exp(s - m_new)
            alpha = jnp.exp(m_old - m_new)
            l_ref[...] = l_ref[...] * alpha + jnp.sum(p, axis=0, keepdims=True)
            acc_ref[...] = acc_ref[...] * alpha + nn(vvt[j], p.astype(BF))
            m_ref[...] = m_new

        if i > 0:
            def body(j, carry):
                block(j, False)
                return carry
            lax.fori_loop(0, i, body, 0)
        block(i, True)
        total = l_ref[...]
        lse[i] = m_ref[...] + jnp.log(total)
        o = (acc_ref[...] / total).T
        att_send[i] = jnp.where(low_half, o[:T], o[T:]).astype(BF)

        @pl.when(g != i)
        def _():
            pltpu.make_async_remote_copy(
                src_ref=att_send.at[i], dst_ref=att.at[:, pl.ds(pl.multiple_of(g * 128, 128), 128)],
                send_sem=sems.at[att_sk + i], recv_sem=sems.at[att_k + g],
                device_id={"expert": i}, device_id_type=MESH,
            ).start()

        @pl.when(g == i)
        def _():
            att[:, pl.ds(pl.multiple_of(g * 128, 128), 128)] = att_send[i]

    att_sk = sem_block(8)

    def forward_attention(m_ref, l_ref, acc_ref):
        gd = gather_dy
        for i in range(8):
            attend(i, m_ref, l_ref, acc_ref)
            if i == 3:
                gd.step_m1()
                gd.step_p1()
            if i == 6:
                gd.step_far()
            if i in (3, 5, 6):
                svc(1)

    pl.run_scoped(
        forward_attention, pltpu.VMEM((1, 2 * T), F32), pltpu.VMEM((1, 2 * T), F32), pltpu.VMEM((128, 2 * T), F32))

    for i in range(8):
        @pl.when(g != i)
        def _(i=i):
            piece = att.at[:, pl.ds(i * 128, 128)]
            arrived(piece, att_k + i)
            pltpu.make_async_remote_copy(
                src_ref=att_send.at[i], dst_ref=piece, send_sem=sems.at[att_sk + i],
                recv_sem=sems.at[att_k + i], device_id={"expert": i}, device_id_type=MESH,
            ).wait_send()

    def project(i, carry):
        rows = pl.ds(pl.multiple_of(i * 64, 64), 64)
        m = xg[g, rows, :].astype(F32) + (nn(att[rows, :], w_out[...]) + b_out[...])
        middle[rows, :] = m
        inv = lax.rsqrt(jnp.mean(m * m, axis=-1, keepdims=True) + EPS)
        h2own[rows, :] = (m * inv * moe_gain[...]).astype(BF)
        return carry

    lax.fori_loop(0, 4, project, 0)
    gather_h = GatherZ(h2g, h2own)
    gather_h.start()
    h2g[g] = h2own[...]

    logits = nt(w_rt[...], h2own[...]) + b_rt[...]
    row = lax.broadcasted_iota(jnp.int32, (64, T), 0)
    expert_of_row = jnp.where(row % 8 < 4, (row // 8) * 4 + row % 8, -1)
    slots = jnp.full((64, T), -1.0, F32)
    for k in range(4):
        tgt = target[pl.ds(k, 1), :]
        slots = jnp.where(expert_of_row == tgt // 64, (tgt % 64).astype(F32), slots)
    member = slots >= 0.0
    masked = jnp.where(member, logits, NEG)
    top = jnp.max(masked, axis=0, keepdims=True)
    weight = jnp.where(member, jnp.exp(masked - top), 0.0)
    gates = weight / jnp.sum(weight, axis=0, keepdims=True)
    gates_ref[...] = gates
    for r in range(8):
        meta_send[r, pl.ds(0, 8), :] = gates[r * 8:r * 8 + 8]
        meta_send[r, pl.ds(8, 8), :] = slots[r * 8:r * 8 + 8]
    meta_k = sem_block(8)
    meta_sent = []
    metag[g] = meta_send[g]
    for rel in range(1, 8):
        r = gs[rel]
        send(lambda r=r: meta_send.at[r], lambda: metag.at[g], meta_k + rel, {"expert": r}, meta_sent)
    svc(1)
    gh = gather_h
    gh.wait_sib_own()
    gh.step_m1()
    gh.step_p1()
    svc(1)
    gh.step_far()
    for gz in (gather_dy, gh):
        gz.wait_sib_m1()
        gz.wait_sib_p1()
        gz.wait_sib_far()
    gather_dy.wait_sib_own()
    local_dy.wait()
    for rel in range(1, 8):
        arrived(metag.at[gs[8 - rel]], meta_k + rel)
    drain(meta_sent)

    def weight_of(h, e, n):
        return gathered[h, e, :, pl.ds(n * 16, 16), :].reshape(T, D)

    slot_at = lax.broadcasted_iota(jnp.int32, (64, T), 0).astype(F32)

    def expert(e, rows_ref, grows_ref, dyr_ref, act_ref, dg_ref, du_ref):
        for item in weights:
            if item == (weights_end, e):
                break

        def build(s, carry):
            hot = (slot_at == metag[s, pl.ds(8 + e, 1), :]).astype(F32)
            hot_low = hot.astype(BF)
            rows = pl.ds(pl.multiple_of(s * 64, 64), 64)
            rows_ref[rows, :] = nn(hot_low, h2g[s]).astype(BF)
            dyr = nn(hot_low, dyg[s])
            gcol = jnp.sum(hot * metag[s, pl.ds(e, 1), :], axis=1, keepdims=True)
            dyr_ref[rows, :] = dyr.astype(BF)
            grows_ref[rows, :] = (dyr * gcol).astype(BF)
            return carry

        lax.fori_loop(0, 8, build, 0)

        for h in range(2):
            cols = pl.ds(h * T, T)
            bias_g = gu_bias[e, pl.ds(0, 1), cols]
            bias_u = gu_bias[e, pl.ds(1, 1), cols]

            def hidden(i, carry, h=h, cols=cols, bias_g=bias_g, bias_u=bias_u):
                rows = pl.ds(pl.multiple_of(i * 128, 128), 128)
                wg = weight_of(h, e, 0)
                wu = weight_of(h, e, 1)
                wd = weight_of(h, e, 2)
                rv = rows_ref[rows, :]
                gc = LIMIT * jnp.tanh((nt(rv, wg) + bias_g) * (1.0 / LIMIT))
                uc = LIMIT * jnp.tanh((nt(rv, wu) + bias_u) * (1.0 / LIMIT))
                da = nt(grows_ref[rows, :], wd)
                sig = 1.0 / (1.0 + jnp.exp(-ALPHA * gc))
                glu = gc * sig
                act_ref[rows, cols] = ((uc + 1.0) * glu).astype(BF)
                gr, ur = gc * (1.0 / LIMIT), uc * (1.0 / LIMIT)
                dg = da * (uc + 1.0) * (sig + ALPHA * glu * (1.0 - sig)) * (1.0 - gr * gr)
                du = da * glu * (1.0 - ur * ur)
                dg_low, du_low = dg.astype(BF), du.astype(BF)
                dg_ref[rows, cols] = dg_low
                du_ref[rows, cols] = du_low
                return (carry[0] + jnp.sum(dg_low.astype(F32), axis=0, keepdims=True),
                        carry[1] + jnp.sum(du_low.astype(F32), axis=0, keepdims=True))

            zero = jnp.zeros((1, T), F32)
            sum_g, sum_u = lax.fori_loop(0, 4, hidden, (zero, zero))
            own_rows[pl.ds(8 + e, 1), pl.ds(h * T, T)] = sum_g
            own_rows[pl.ds(8 + e, 1), pl.ds(512 + h * T, T)] = sum_u

        def outputs(i, carry):
            rows = pl.ds(pl.multiple_of(i * 128, 128), 128)
            out = down_bias[pl.ds(e, 1), :]
            drow = jnp.zeros((128, D), F32)
            for h in range(2):
                cols = pl.ds(h * T, T)
                out = out + nn(act_ref[rows, cols], weight_of(h, e, 2))
                drow = (drow + nn(dg_ref[rows, cols], weight_of(h, e, 0))
                        + nn(du_ref[rows, cols], weight_of(h, e, 1)))
            out_low = out.astype(BF)
            dgate = jnp.sum(dyr_ref[rows, :].astype(F32) * out_low.astype(F32), axis=1, keepdims=True)
            drow_low = drow.astype(BF)
            for n in range(2):
                s = i * 2 + n
                outb[s, pl.ds(e * 64, 64), :] = out_low[n * 64:n * 64 + 64]
                drb[s, pl.ds(e * 64, 64), :] = drow_low[n * 64:n * 64 + 64]
                hot = (slot_at == metag[s, pl.ds(8 + e, 1), :]).astype(F32)
                dgt_send[s, pl.ds(e, 1), :] = jnp.sum(hot * dgate[n * 64:n * 64 + 64], axis=0, keepdims=True)
            return carry + jnp.sum(grows_ref[rows, :].astype(F32), axis=0, keepdims=True)

        own_rows[pl.ds(4 + e, 1), :] = lax.fori_loop(0, 4, outputs, jnp.zeros((1, D), F32))

        drain(pending_weights[e])
        for h in range(2):
            for n, (left, right) in enumerate(((dg_ref, rows_ref), (du_ref, rows_ref), (act_ref, grows_ref))):
                grad = tn(left[:, pl.ds(h * T, T)], right[...])
                gathered[h, e, :, pl.ds(n * 16, 16), :] = grad.astype(BF).reshape(16, 16, D)

    out_copies = []

    class WeightPieces:
        def __init__(self, e, h):
            self.e, self.h, self.k = e, h, wsem(h, e)

        def own(self, s):
            return gathered.at[self.h, self.e, s]

        def rows(self, first_slot, n):
            return gathered.at[self.h, self.e, pl.ds(first_slot, n)]

        def half(self, side):
            return rs_half.at[self.e, self.h, side]

        def full(self, side):
            if self.e < 2:
                return rs_full.at[self.e, self.h, side]
            return h2g.at[self.lent(side), pl.ds(0, 192)]

        def lent(self, side):
            return ((self.e - 2) * 2 + self.h) * 2 + side

        def full_one(self, side, a):
            if self.e < 2:
                return rs_full.at[self.e, self.h, side, a]
            return h2g.at[self.lent(side), pl.ds(a * 48 if isinstance(a, int) else pl.multiple_of(a * 48, 48), 48)]

        def send_row(self, first_slot, side, recv, dev, keep):
            if self.e < 2:
                send(lambda: self.rows(first_slot, 4), lambda: self.full(side), recv, dev, keep, ring_w)
            else:
                for a in range(4):
                    send(lambda a=a: self.own(first_slot + a), lambda a=a: self.full_one(side, a), recv, dev, keep, ring_w)

        def half2(self):
            return rs2_half.at[self.e, self.h]

        def full2(self, side):
            return rs2_full.at[self.e, self.h, side]

        def finish(self):
            for n, out in enumerate((d_gate_w, d_up_w, d_down_w)):
                out_copies.append(local_copy(
                    lambda n=n: self.own(slot(self.h, 0, 0)).at[pl.ds(n * 16, 16)],
                    lambda out=out: out.at[self.e, pl.ds(self.h * 16, 16)]))

    class ParamPieces(WeightPieces):
        def __init__(self, h):
            self.e, self.h, self.k = 0, h, wsem(h, 0)

        def own(self, s):
            return params.at[self.h, s]

        def rows(self, first_slot, n):
            return params.at[self.h, pl.ds(first_slot, n)]

        def half(self, side):
            return rs_half.at[0, self.h, side, :, pl.ds(0, 16), pl.ds(0, 768)]

        def full(self, side):
            return rs_full.at[0, self.h, side, :, pl.ds(0, 16), pl.ds(0, 768)]

        def full_one(self, side, a):
            return rs_full.at[0, self.h, side, a, pl.ds(0, 16), pl.ds(0, 768)]

        def half2(self):
            return rs2_half.at[0, self.h, pl.ds(0, 16), pl.ds(0, 768)]

        def full2(self, side):
            return rs2_full.at[0, self.h, side, pl.ds(0, 16), pl.ds(0, 768)]

        def finish(self):
            pass

    def scatter_xy(p, even_way, wait_for, keep):
        h, k = p.h, p.k
        fwd, back = xy(axis_of(h, 1), 1), xy(axis_of(h, 1), 3)
        fwd2, back2 = xy(axis_of(h, 0), 1), xy(axis_of(h, 0), 3)
        line = lines[h]

        def add(s, refs):
            v = p.own(s)[...].astype(F32)
            for ref in refs:
                v = v + ref[...].astype(F32)
            p.own(s)[...] = v.astype(BF)

        send(lambda: p.rows(line[2], 2), lambda: p.half(0), k, fwd, keep, ring_w)
        send(lambda: p.rows(line[2] + 2, 2), lambda: p.half(1), k + 1, back, keep, ring_w)
        yield 1
        for side, db, dev in ((0, 1, fwd), (1, 3, back)):
            if wait_for:
                pl.semaphore_wait(credit.at[h, side], 1)
            arrived(p.half(side), k + side)
            for n in range(2):
                add(line[db] + side * 2 + n, [p.half(side).at[n]])
            p.send_row(line[db], side, k + 2 + side, dev, keep)
        yield 2
        arrived(p.full(0), k + 2)
        arrived(p.full(1), k + 3)
        for da in (2, 1, 3, 0):
            a = first[h][da]
            add(line[0] + a, [p.full_one(0, a), p.full_one(1, a)])
            if da == 2:
                send(lambda: p.own(slot(h, 2, 0)), p.half2, k + 4, fwd2 if even_way else back2, keep, ring_w)
        yield 3
        arrived(p.half2(), k + 4)
        add(slot(h, 1 if even_way else 3, 0), [p.half2()])
        send(lambda: p.own(slot(h, 1, 0)), lambda: p.full2(0), k + 5, fwd2, keep, ring_w)
        send(lambda: p.own(slot(h, 3, 0)), lambda: p.full2(1), k + 6, back2, keep, ring_w)
        yield 4
        for side in range(2):
            arrived(p.full2(side), k + 5 + side)
        add(slot(h, 0, 0), [p.full2(0), p.full2(1)])
        p.finish()
        yield 5

    scatters = [[scatter_xy(WeightPieces(e, h), e % 2 == 0, e == 2, pending) for h in range(2)] for e in range(4)]

    started = set()

    def wsvc(*experts):
        for e in experts:
            if e not in started:
                started.add(e)
                pl.semaphore_wait(passed.at[e], 4)
            for h in range(2):
                next(scatters[e][h], None)

    def experts(*refs):
        for e in range(4):
            expert(e, *refs)
            if e == 3:
                drain(pending_gather)
                for h in range(2):
                    pl.semaphore_signal(credit.at[h, 1], inc=1, device_id=xy(axis_of(h, 1), 1), device_id_type=MESH)
                    pl.semaphore_signal(credit.at[h, 0], inc=1, device_id=xy(axis_of(h, 1), 3), device_id_type=MESH)
            wsvc(e)
            if e >= 1:
                wsvc(e - 1)

    pl.run_scoped(
        experts,
        pltpu.VMEM((512, D), BF), pltpu.VMEM((512, D), BF), pltpu.VMEM((512, D), BF),
        pltpu.VMEM((512, 512), BF), pltpu.VMEM((512, 512), BF), pltpu.VMEM((512, 512), BF))

    dg_k = att_k
    dgt_sent = []
    dgt_in[g] = dgt_send[g]
    for rel in range(1, 8):
        r = gs[rel]
        send(lambda r=r: dgt_send.at[r], lambda: dgt_in.at[g], dg_k + rel, {"expert": r}, dgt_sent)

    def combine(buf, s, gated):
        pieces = []
        for e in range(4):
            hot = (slot_at == metag[s, pl.ds(8 + e, 1), :]).astype(F32)
            if gated:
                hot = hot * metag[s, pl.ds(e, 1), :]
            pieces.append(hot)
        spread = jnp.concatenate(pieces, axis=0).T.astype(BF)
        buf[s] = nn(spread, buf[s]).astype(BF)

    scatter_d = ScatterZ(gather_x.k, drb, lambda n: sib_in.at[n], lambda n: half_in.at[n], lambda n: full_in.at[n])
    far_chunks, own_chunks = scatter_d.chunks()
    for n in range(4):
        combine(drb, far_chunks[n], False)
        scatter_d.to_sibling(n)
    combine(drb, own_chunks[0], False)
    scatter_d.step1()
    combine(drb, own_chunks[1], False)
    combine(drb, own_chunks[2], False)
    wsvc(0)
    scatter_d.step2()
    combine(drb, own_chunks[3], False)
    wsvc(3)
    for n in range(4):
        combine(outb, far_chunks[n], True)
    for n in range(4):
        combine(outb, own_chunks[n], True)
    wsvc(0)
    scatter_d.step3()

    for rel in range(1, 8):
        arrived(dgt_in.at[gs[8 - rel]], dg_k + rel)
    d_gates = jnp.where(row % 8 < 4, jnp.concatenate([dgt_in[r] for r in range(8)], axis=0), 0.0)
    d_logits = gates_ref[...] * (d_gates - jnp.sum(gates_ref[...] * d_gates, axis=0, keepdims=True))
    dl_high, dl_low = split_low(d_logits)
    d_wrt = nn(dl_high, h2own[...]) + nn(dl_low, h2own[...])
    common_rows[pl.ds(6, 1), pl.ds(0, 64)] = jnp.sum(d_logits.T, axis=0, keepdims=True)
    dl_high_t, dl_low_t = split_low(d_logits.T)
    d_middle[...] = nn(dl_high_t, w_rt[...]) + nn(dl_low_t, w_rt[...])
    drain(scatter_d.sent)
    att_grad, branch_at = h2own, 7

    def middle_back(i, carry):
        rows = pl.ds(pl.multiple_of(i * 64, 64), 64)
        m = middle[rows, :]
        inv = lax.rsqrt(jnp.mean(m * m, axis=-1, keepdims=True) + EPS)
        d_h2 = scatter_d.result(rows) + d_middle[rows, :]
        v2 = d_h2 * moe_gain[...]
        inner = jnp.mean(v2 * m, axis=-1, keepdims=True)
        dm = dyg[g, rows, :].astype(F32) + inv * v2 - m * (inv * inv * inv * inner)
        d_middle[rows, :] = dm
        low = dm.astype(BF)
        dyg[branch_at, rows, :] = low
        att_grad[rows, :] = nt(low, w_out[...]).astype(BF)
        return (carry[0] + jnp.sum(low.astype(F32), axis=0, keepdims=True),
                carry[1] + jnp.sum(d_h2 * m * inv, axis=0, keepdims=True))

    zero_row = jnp.zeros((1, D), F32)
    sum_b, sum_m = lax.fori_loop(0, 4, middle_back, (zero_row, zero_row))
    common_rows[pl.ds(4, 1), :] = sum_b
    common_rows[pl.ds(5, 1), :] = sum_m

    do_k = meta_k
    att_sent = []
    dob[g] = att_grad[:, pl.ds(pl.multiple_of(g * 128, 128), 128)]
    for rel in range(1, 8):
        r = gs[rel]
        send(lambda r=r: att_grad.at[:, pl.ds(pl.multiple_of(r * 128, 128), 128)], lambda: dob.at[g], do_k + rel, {"expert": r}, att_sent)
    drain(dgt_sent)

    eight = lax.broadcasted_iota(jnp.int32, (8, D), 0)
    for r in range(8):
        rows = pl.ds(r * 128, 128)
        drb[r, pl.ds(0, 128), :] = tn(att[:, rows], dyg[branch_at]).astype(BF)
        mine = jnp.where(g == r, 1.0, 0.0).astype(F32)
        top = jnp.where(eight < 4, d_wrt[r * 8:r * 8 + 8], own_rows[pl.ds(0, 8), :] * mine)
        low_rows = own_rows[pl.ds(8, 8), :] * mine
        if r == 0:
            low_rows = jnp.where(eight < 4, low_rows, common_rows[...])
        drb[r, pl.ds(128, 16), :] = jnp.concatenate([top, low_rows], axis=0).astype(BF)
    wsvc(1)
    for rel in range(1, 8):
        arrived(dob.at[gs[8 - rel]], do_k + rel)

    scatter_m = ScatterZ(
        gather_dy.k, outb, lambda n: dyg.at[n], lambda n: dyg.at[4, pl.ds(n * 128, 128)], lambda n: dyg.at[5 + n])
    for n in range(4):
        scatter_m.to_sibling(n)
    scatter_w = ScatterZ(
        gather_h.k, drb, lambda n: sib_in.at[n, pl.ds(0, 144)], lambda n: half_in.at[n, pl.ds(0, (80, 64)[n])],
        lambda n: full_in.at[n, pl.ds(0, 144)], (80, 64))
    for n in range(4):
        scatter_w.to_sibling(n)

    class Exchange:
        def __init__(self, stage, inbox, everyone, k):
            self.stage, self.inbox, self.everyone, self.spread_k = stage, inbox, everyone, k
            self.k = sem_block(6)
            self.sent = []

        def start(self, n):
            for d in (1, 2, 3):
                send(lambda: self.stage.at[n], lambda d=d: self.inbox.at[n, d - 1], self.k + n * 3 + d - 1,
                     xy("xy"[n], d), self.sent)

        def total(self, n):
            v = self.stage[n]
            for d in (1, 2, 3):
                arrived(self.inbox.at[n, d - 1], self.k + n * 3 + d - 1)
            for d in (1, 2, 3):
                v = v + self.inbox[n, d - 1]
            return v

        def spread(self):
            for rel in range(1, 8):
                send(lambda: self.everyone.at[g], lambda: self.everyone.at[g], self.spread_k + rel,
                     spread_group[rel], self.sent)

        def step(self, n):
            v = self.total(n)
            if n == 0:
                self.stage[1] = v
                self.start(1)
            else:
                self.everyone[g] = v
                self.spread()

        def finish(self):
            for rel in range(1, 8):
                arrived(self.everyone.at[gs[8 - rel]], self.spread_k + rel)

    early_sum = Exchange(early, early_in, early_all, att_k)
    late_sum = Exchange(late, late_in, late_all, meta_k)
    spread_group = [{"expert": gs[rel]} for rel in range(8)]

    sub_low = lax.broadcasted_iota(jnp.int32, (128, 1), 0) < 64
    smask0 = jnp.where(sub_low, 1.0, 0.0).astype(F32)
    smask1 = 1.0 - smask0

    def stacked_t(v_t):
        return jnp.concatenate([v_t * smask0, v_t * smask1], axis=1).astype(BF)

    def attend_back(i, dk_ref, dv_ref, dqkv_ref, dq_ref):
        q2 = stacked(qs[i])
        q2t = stacked_t(qs[i].astype(F32).T)
        do2 = stacked(dob[i])
        do_t = dob[i].astype(F32).T
        do2t = stacked_t(do_t)
        prod = do_t * att_send[i].astype(F32).T
        delta = jnp.concatenate(
            [jnp.sum(prod[:64], axis=0, keepdims=True), jnp.sum(prod[64:], axis=0, keepdims=True)], axis=1)
        lse_row = lse[i]
        share = jnp.exp(sink_row[...] - lse_row) * delta
        for n in range(2):
            part = jnp.sum(share[:, n * T:n * T + T], axis=1, keepdims=True)
            late[0, pl.ds(2, 1), pl.ds(0, 128)] -= jnp.where(lane == n, part, 0.0)
        dq_ref[...] = jnp.zeros((128, 2 * T), F32)

        def block(j, diagonal):
            p = jnp.exp(nn(kk[j], q2t) - lse_row)
            if diagonal:
                p = jnp.where(allowed, p, 0.0)
            ds = (p * (nn(vv[j], do2t) - delta)).astype(BF)
            dv_ref[j] += nn(p.astype(BF), do2)
            dk_ref[j] += nn(ds, q2)
            dq_ref[...] += nn(kkt[j], ds)

        if i > 0:
            def body(j, carry):
                block(j, False)
                return carry
            lax.fori_loop(0, i, body, 0)
        block(i, True)
        dq = dq_ref[...].T
        dq = jnp.where(low_half, dq[:T], dq[T:]) * 0.125
        cosine, sine = trig(i)
        dqkv_ref[i, :, pl.ds(0, 128)] = (dq * cosine - swap(dq) * sine).astype(BF)

    def place_projection():
        for t in range(8):
            v = scatter_w.result(pl.ds(t * 16, 16)).astype(BF)
            for side in range(2):
                for h in range(2):
                    at = side * 512 + h * 256
                    params[h, side * 8 + t, :, pl.ds(0, 256)] = v[:, at:at + 256]
        early[0] = scatter_w.result(pl.ds(128, 16))

    zloc = [(lax.div(zs[d], 2), lax.rem(zs[d], 2)) for d in range(4)]

    def param_piece(h, col, s):
        return gathered.at[h, col, s, pl.ds(0, 32), pl.ds(0, 768)]

    def param_row(h, d):
        hi, lo = zloc[d]
        return gathered.at[h, c * 2 + hi, slot(h, 0, 0), pl.ds(pl.multiple_of(lo * 16, 16), 16), pl.ds(0, 768)]

    param_sent = []

    def own_line(h, e, db):
        return gathered.at[h, c * 2 + e, pl.ds(second[h][db] * 4, 4), pl.ds(0, 32), pl.ds(0, 768)]

    def own_piece(h, e, da):
        return param_piece(h, c * 2 + e, slot(h, da, 0))

    def psem(h, e):
        return wsem(h, 1 + e)

    def forward(piece, recv, dev):
        send(piece, piece, recv, dev, param_sent, ring_w)

    out_k = [sem_block(1) for _ in range(2)]

    def place_out(core, e):
        for h in range(2):
            col = core * 2 + e
            for zl in range(2):
                rows = pl.ds(zl * 16, 16)
                member = (e * 2 + zl) * 2 + core
                for side in range(2):
                    pltpu.make_async_copy(
                        gathered.at[h, col, pl.ds(side * 8, 8), rows, pl.ds(0, 256)],
                        d_wout.at[member, :, :, pl.ds(side * 512 + h * 256, 256)], sems.at[out_k[0]]).start()
                    for part, to in ((0, member * 128), (1, 1024 + core * 512 + (e * 2 + zl) * 128)):
                        pltpu.make_async_copy(
                            gathered.at[h, col, :, rows, pl.ds(256 + side * 256 + part * 128, 128)],
                            d_wqkv.at[:, pl.ds(h * 32 + side * 16, 16), pl.ds(pl.multiple_of(to, 128), 128)],
                            sems.at[out_k[1]]).start()

    def params_gather():
        z_k = wsem(0, 3)
        for h in range(2):
            param_row(h, 0)[...] = params[h, slot(h, 0, 0)]
            forward(lambda h=h: param_row(h, 0), z_k + h * 3, up)
            forward(lambda h=h: param_row(h, 0), z_k + h * 3 + 1, down)
        yield 1
        arrived(param_row(0, 3), z_k + 0)
        forward(lambda: param_row(0, 3), z_k + 2, up)
        arrived(param_row(1, 1), z_k + 4)
        forward(lambda: param_row(1, 1), z_k + 5, down)
        arrived(param_row(0, 1), z_k + 1)
        arrived(param_row(1, 3), z_k + 3)
        yield 2
        arrived(param_row(0, 2), z_k + 2)
        arrived(param_row(1, 2), z_k + 5)
        for e in range(2):
            for h in range(2):
                for n, d in ((0, 1), (1, 3)):
                    forward(lambda h=h, e=e: own_piece(h, e, 0), psem(h, e) + n, xy(axis_of(h, 0), d))
        yield 3
        for e in range(2):
            for h in range(2):
                k = psem(h, e)
                arrived(own_piece(h, e, 3), k)
                if e == 0:
                    forward(lambda h=h, e=e: own_piece(h, e, 3), k + 2, xy(axis_of(h, 0), 1))
                arrived(own_piece(h, e, 1), k + 1)
                if e == 1:
                    forward(lambda h=h, e=e: own_piece(h, e, 1), k + 2, xy(axis_of(h, 0), 3))
        for e in range(2):
            for h in range(2):
                k = psem(h, e)
                arrived(own_piece(h, e, 2), k + 2)
                for n, d in ((3, 1), (4, 3)):
                    forward(lambda h=h, e=e: own_line(h, e, 0), k + n, xy(axis_of(h, 1), d))
        for e in range(2):
            for h in range(2):
                forward(lambda h=h, e=e: own_line(h, e, 0), sib_k(h, e), sib)
        yield 4
        for e in range(2):
            for h in range(2):
                k = psem(h, e)
                arrived(own_line(h, e, 3), k + 3)
                if e == 0:
                    forward(lambda h=h, e=e: own_line(h, e, 3), k + 5, xy(axis_of(h, 1), 1))
                arrived(own_line(h, e, 1), k + 4)
                if e == 1:
                    forward(lambda h=h, e=e: own_line(h, e, 1), k + 5, xy(axis_of(h, 1), 3))
                for db in (3, 1):
                    forward(lambda h=h, e=e, db=db: own_line(h, e, db), sib_k(h, e), sib)
        yield 5
        for e in range(2):
            for h in range(2):
                arrived(own_line(h, e, 2), psem(h, e) + 5)
                forward(lambda h=h, e=e: own_line(h, e, 2), sib_k(h, e), sib)
            place_out(c, e)
        yield 6
        for e in range(2):
            for h in range(2):
                arrived(gathered.at[h, other * 2 + e, :, pl.ds(0, 32), pl.ds(0, 768)], sib_k(h, e))
            place_out(other, e)
        yield 7

    def sib_k(h, e):
        return wsem(1, 3) + h * 2 + e

    param_scatters = [scatter_xy(ParamPieces(h), h == 0, False, param_sent) for h in range(2)]

    def psvc():
        for h in range(2):
            next(param_scatters[h], None)

    def backward(dk_ref, dv_ref, dqkv_ref, dq_ref):
        dk_ref[...] = jnp.zeros((8, T, 128), F32)
        dv_ref[...] = jnp.zeros((8, T, 128), F32)
        plan = {0: (1,), 1: (0,), 2: (2,), 3: (1,), 4: (3,), 5: (2,), 6: (3,), 7: (2, 3)}
        for i in range(8):
            attend_back(i, dk_ref, dv_ref, dqkv_ref, dq_ref)
            wsvc(*plan[i])
            if i == 1:
                scatter_w.step1()
            if i == 3:
                scatter_m.step1()
                scatter_w.step2()
            if i == 5:
                scatter_m.step2()
                scatter_w.step3()
                place_projection()
                for dev in (sib, up, down):
                    pl.semaphore_signal(free_z, inc=1, device_id=dev, device_id_type=MESH)
                early_sum.start(0)
            if i == 6:
                early_sum.step(0)
        early_sum.step(1)
        wsvc(3)
        drain(pending)
        drain(out_copies)
        for dev in (sib, up, down, xy("x", 1), xy("x", 3), xy("y", 1), xy("y", 3)):
            pl.semaphore_signal(free_xy, inc=1, device_id=dev, device_id_type=MESH)
        drain(att_sent)

        def finish(r, carry):
            cosine, sine = trig(r)
            dk = dk_ref[r]
            dk = dk + pltpu.roll(dk, 64, 1)
            dv = dv_ref[r]
            dv = dv + pltpu.roll(dv, 64, 1)
            dkv = jnp.where(low_half, dk * cosine - swap(dk) * sine, dv)
            dqkv_ref[r, :, pl.ds(128, 128)] = dkv.astype(BF)
            return carry + jnp.sum(dqkv_ref[r].astype(F32), axis=0, keepdims=True)

        late[0, pl.ds(1, 1), pl.ds(0, T)] = lax.fori_loop(0, 8, finish, jnp.zeros((1, T), F32))
        swap_k = gather_dy.k + 8
        swap_sent = []
        for r in range(8):
            send(lambda r=r: dqkv_ref.at[r, :, pl.ds(128, 128)], lambda r=r: dyg.at[7, :, pl.ds(r * 128, 128)],
                 swap_k, sib, swap_sent)

        drain(scatter_w.sent)
        scatter_h = ScatterZ(gather_x.k, drb, lambda n: sib_in.at[n], lambda n: half_in.at[n], lambda n: full_in.at[n])

        def d_h1_chunk(s):
            drb[s] = nt(dqkv_ref[s], w_qkv[...]).astype(BF)

        pl.semaphore_wait(free_z, 3)
        for n in range(4):
            d_h1_chunk(far_chunks[n])
            scatter_h.to_sibling(n)
        for n in range(4):
            d_h1_chunk(own_chunks[n])

        dk_ref[...] = jnp.zeros((8, T, 128), F32)

        arrived(dyg.at[7], swap_k)
        drain(swap_sent)

        def dw_part(r, carry):
            both = dyg[7, :, pl.ds(pl.multiple_of(r * 128, 128), 128)].astype(F32)
            own = dqkv_ref[r, :, pl.ds(128, 128)].astype(F32)
            mixed = jnp.where(low_half == even, own, pltpu.roll(both, 64, 1)).astype(BF)
            h1 = h1_rows(r, pl.ds(0, T))
            v = jnp.concatenate([tn(dqkv_ref[r, :, pl.ds(0, 128)], h1), tn(mixed, h1)], axis=0)
            for n in range(8):
                dk_ref[n] += v[:, n * 128:n * 128 + 128]
            return carry

        lax.fori_loop(0, 8, dw_part, 0)
        for n in range(8):
            dw = dk_ref[n].T
            for s in range(2):
                for h in range(2):
                    rows = dw[s * 64 + h * 32:s * 64 + h * 32 + 32]
                    params[h, n * 2 + s, :, pl.ds(256, 512)] = jnp.concatenate([rows[:16], rows[16:]], axis=1).astype(BF)
        pl.semaphore_wait(free_xy, 7)
        psvc()
        scatter_h.step1()
        psvc()
        scatter_h.step2()
        scatter_m.step3()

        def result(i, carry):
            rows = pl.ds(pl.multiple_of(i * 64, 64), 64)
            att[rows, :] = (middle[rows, :] + scatter_m.result(rows)).astype(BF)
            return carry

        lax.fori_loop(0, 4, result, 0)
        cp2 = local_copy(att, block_out)
        psvc()
        psvc()
        psvc()
        gather_p = params_gather()
        next(gather_p)
        scatter_h.step3()

        def tokens_back(i, carry):
            rows = pl.ds(pl.multiple_of(i * 64, 64), 64)
            xf = xg[g, rows, :].astype(F32)
            inv = lax.rsqrt(jnp.mean(xf * xf, axis=-1, keepdims=True) + EPS)
            d_h1 = scatter_h.result(rows)
            v1 = d_h1 * attn_gain[...]
            inner = jnp.mean(v1 * xf, axis=-1, keepdims=True)
            h2own[rows, :] = (d_middle[rows, :] + inv * v1 - xf * (inv * inv * inv * inner)).astype(BF)
            return carry + jnp.sum(d_h1 * xf * inv, axis=0, keepdims=True)

        next(gather_p)
        next(gather_p)
        late[0, pl.ds(0, 1), :] = lax.fori_loop(0, 4, tokens_back, zero_row)
        late_sum.start(0)
        cp3 = local_copy(h2own, d_tokens)
        next(gather_p)
        late_sum.step(0)
        next(gather_p)
        early_sum.finish()
        late_sum.step(1)
        late_sum.finish()
        sink_at = lane
        for r in range(8):
            final[pl.ds(0, 1), :] += late_all[r, pl.ds(0, 1), :]
            final[pl.ds(3, 1), pl.ds(r * 128, 128)] = late_all[r, pl.ds(1, 1), pl.ds(0, 128)]
            two = late_all[r, pl.ds(2, 1), pl.ds(0, 128)]
            two = pltpu.roll(two, 2 * r, 1) if r else two
            final[pl.ds(5, 1), pl.ds(0, 128)] += jnp.where((lane >= 2 * r) & (lane < 2 * r + 2), two, 0.0)
        for n in range(4):
            a = late_all[2 * n, pl.ds(1, 1), pl.ds(128, 128)]
            b = late_all[2 * n + 1, pl.ds(1, 1), pl.ds(128, 128)]
            final[pl.ds(4, 1), pl.ds(n * 128, 128)] = jnp.where(low_half, a, pltpu.roll(b, 64, 1))
            final[pl.ds(4, 1), pl.ds(512 + n * 128, 128)] = jnp.where(low_half, pltpu.roll(a, 64, 1), b)
        final[pl.ds(1, 2), :] = early_all[0, pl.ds(12, 2), :]
        cp4 = local_copy(early_all, early_out)
        cp5 = local_copy(final, final_out)
        for _ in gather_p:
            pass
        drain(scatter_h.sent)
        drain(scatter_m.sent)
        drain([cp2, cp3, cp4, cp5])
        pltpu.make_async_copy(d_wout, d_wout, sems.at[out_k[0]]).wait()
        pltpu.make_async_copy(d_wqkv, d_wqkv, sems.at[out_k[1]]).wait()

    pl.run_scoped(
        backward, pltpu.VMEM((8, T, 128), F32), pltpu.VMEM((8, T, 128), F32), pltpu.VMEM((8, T, T), BF),
        pltpu.VMEM((128, 2 * T), F32))
    drain(param_sent)
    drain(early_sum.sent)
    drain(late_sum.sent)


ANY = pl.BlockSpec(memory_space=pl.ANY)
VM = pl.BlockSpec(memory_space=pltpu.VMEM)


def angle_tables():
    frequency = np.exp(np.arange(32, dtype=np.float32) * np.float32(-2.0 * np.log(THETA) / 64)).astype(np.float64)
    freq = np.tile(frequency, 4)[None, :]
    near = np.arange(T, dtype=np.float64)[:, None] * freq
    far = np.arange(8, dtype=np.float64)[:, None] * T * freq
    return [f(a).astype(np.float32) for a in (near, far) for f in (np.cos, np.sin)]


def per_device(
    tokens, cotangent, routes, slot_ids, attn_gain, w_qkv, b_qkv, w_out, b_out, sink_logits, moe_gain,
    w_router, b_router, gu_weight, gu_bias, down_weight, down_bias,
):
    g = lax.axis_index("expert")
    both = jnp.concatenate([gu_weight.transpose(0, 2, 1, 3), down_weight[:, None]], axis=1)
    shard = both.reshape(4, 3, 2, 16, D).transpose(2, 0, 1, 3, 4).reshape(2, 4, 48, D)
    target = jnp.pad((routes * 64 + slot_ids).T, ((0, 4), (0, 0)))

    def padded(v):
        return jnp.pad(v.reshape(8, 4, -1), ((0, 0), (0, 4), (0, 0))).reshape(64, -1)

    w_rt = padded(w_router.T)
    b_rt = jnp.broadcast_to(padded(b_router), (64, T))
    gub = gu_bias.reshape(4, 2, 4, 4, 2, 16)
    gub = jnp.concatenate([gub[:, :, :, :, 0].reshape(4, 2, 256), gub[:, :, :, :, 1].transpose(0, 1, 3, 2, 4).reshape(4, 2, 256)], axis=2)
    down_own = lax.dynamic_slice_in_dim(down_bias, g * 4, 4, 0)
    cos_a, sin_a, cos_b, sin_b = [jnp.asarray(t) for t in angle_tables()]
    shape = jax.ShapeDtypeStruct
    out = pl.pallas_call(
        layer_kernel,
        out_shape=(
            shape((T, D), BF), shape((T, D), BF), shape((4, 32, D), BF), shape((4, 32, D), BF), shape((4, 32, D), BF),
            shape((16, 64, 2048), BF), shape((8, 8, 16, D), BF), shape((8, 16, D), F32), shape((8, D), F32),
        ),
        in_specs=[ANY] * 4 + [VM] * 15,
        out_specs=[ANY] * 9,
        scratch_shapes=[
            pltpu.VMEM((8, T, D), BF), pltpu.VMEM((8, T, D), BF), pltpu.VMEM((8, T, D), BF),
            pltpu.VMEM((2, 4, 16, 48, D), BF),
            pltpu.VMEM((8, T, 128), BF), pltpu.VMEM((8, T, 128), BF), pltpu.VMEM((8, T, 128), BF),
            pltpu.VMEM((8, 128, T), BF), pltpu.VMEM((8, 128, T), BF),
            pltpu.VMEM((8, 1, 2 * T), F32), pltpu.VMEM((8, T, 128), BF), pltpu.VMEM((T, D), BF),
            pltpu.VMEM((T, D), F32), pltpu.VMEM((T, D), BF),
            pltpu.VMEM((8, 16, T), F32), pltpu.VMEM((8, 16, T), F32),
            pltpu.VMEM((8, T, D), BF), pltpu.VMEM((8, T, D), BF),
            pltpu.VMEM((4, T, D), BF), pltpu.VMEM((2, 128, D), BF), pltpu.VMEM((2, T, D), BF),
            pltpu.VMEM((4, 2, 2, 2, 48, D), BF), pltpu.VMEM((2, 2, 2, 4, 48, D), BF),
            pltpu.VMEM((4, 2, 48, D), BF), pltpu.VMEM((4, 2, 2, 48, D), BF),
            pltpu.VMEM((8, T, 128), BF), pltpu.VMEM((8, 8, T), F32), pltpu.VMEM((8, 8, T), F32),
            pltpu.VMEM((T, D), F32),
            pltpu.VMEM((64, T), F32), pltpu.VMEM((2, 16, 16, 768), BF),
            pltpu.VMEM((16, D), F32), pltpu.VMEM((8, D), F32),
            pltpu.VMEM((2, 16, D), F32), pltpu.VMEM((2, 3, 16, D), F32), pltpu.VMEM((8, 16, D), F32),
            pltpu.VMEM((2, 8, D), F32), pltpu.VMEM((2, 3, 8, D), F32), pltpu.VMEM((8, 8, D), F32),
            pltpu.VMEM((D, 256), BF), pltpu.VMEM((1, 256), F32), pltpu.VMEM((1, 512), F32), pltpu.VMEM((8, D), F32),
            pltpu.SemaphoreType.DMA((NSEM,)), pltpu.SemaphoreType.REGULAR((2, 2)),
            pltpu.SemaphoreType.REGULAR, pltpu.SemaphoreType.REGULAR, pltpu.SemaphoreType.REGULAR((4,)),
        ],
        compiler_params=pltpu.CompilerParams(collective_id=1, has_side_effects=True, vmem_limit_bytes=VLIM),
    )(tokens, cotangent, shard, w_qkv, target, attn_gain[None], b_qkv[None], w_out, b_out[None],
      jnp.pad(sink_logits, (0, 112))[None], moe_gain[None], w_rt, b_rt, gub, down_own, cos_a, sin_a, cos_b, sin_b)
    block_out, d_tokens, d_gate_w, d_up_w, d_down_w, d_wqkv, d_wout, early, final = out
    d_wr = early[:, :4].reshape(32, D).T
    d_br = early[0, 14, :64].reshape(8, 8)[:, :4].reshape(32)
    d_gub = lax.dynamic_index_in_dim(early, g, 0, keepdims=False)[8:12].reshape(4, 2, 2, 16, 16)
    dp = lax.axis_index("dp")
    turned = (dp % 4) * 4 + dp // 4
    d_gub = jnp.concatenate([lax.dynamic_index_in_dim(d_gub[:, :, 0], dp, 2, keepdims=False),
                             lax.dynamic_index_in_dim(d_gub[:, :, 1], turned, 2, keepdims=False)], axis=-1)
    return (
        block_out, d_tokens, final[0], d_wqkv.reshape(D, 2048).astype(F32), final[3:5].reshape(2048),
        d_wout.reshape(D, D).astype(F32), final[1], final[5, :16], final[2], d_wr, d_br,
        jnp.stack([d_gate_w, d_up_w], axis=2).astype(F32), d_gub, d_down_w.astype(F32), early[:, 4:8].reshape(32, D),
    )


def solution(mesh):
    rows = P(("dp", "expert"), None)
    in_specs = (rows,) * 4 + (P(),) * 9 + (
        P("expert", "dp", None, None), P("expert", None, None), P("expert", "dp", None), P())
    out_specs = (rows,) * 2 + (P(),) * 9 + (
        P("expert", "dp", None, None), P("expert", None, "dp"), P("expert", "dp", None), P())
    return jax.shard_map(per_device, mesh=mesh, in_specs=in_specs, out_specs=out_specs, check_vma=False)
```

```python
import functools

import jax
import jax.numpy as jnp
import numpy as np
from jax import lax
from jax.experimental import pallas as pl
from jax.experimental.pallas import tpu as pltpu
from jax.sharding import PartitionSpec as P

MESH = pl.DeviceIdType.MESH
BF = jnp.bfloat16
F32 = jnp.float32
EPS = 1e-05
THETA = 10000.0
LIMIT = 7.0
ALPHA = 1.702
NEG = -1000000000.0
NSEM = 380
VLIM = (64 << 20) - (1 << 16)
T = 256
D = 1024


def nt(a, b):
    return lax.dot_general(a, b, (((1,), (1,)), ((), ())), preferred_element_type=F32)


def tn(a, b):
    return lax.dot_general(a, b, (((0,), (0,)), ((), ())), preferred_element_type=F32)


def nn(a, b):
    return jnp.dot(a, b, preferred_element_type=F32)


def split_low(v):
    high = v.astype(BF)
    return high, (v - high.astype(F32)).astype(BF)


def layer_kernel(
    x_in, dy_in, w_in, w_qkv_in, target, attn_gain, b_qkv_in, w_out, b_out, sinks, moe_gain,
    w_rt, b_rt, gu_bias, down_bias, cos_a, sin_a, cos_b, sin_b,
    block_out, d_tokens, d_gate_w, d_up_w, d_down_w, d_wqkv, d_wout, early_out, final_out,
    xg, dyg, h2g, gathered, qs, kk, vv, kkt, vvt, lse, att_send, att, middle, h2own, metag, meta_send,
    outb, drb, sib_in, half_in, full_in, rs_half, rs_full, rs2_half, rs2_full, dob, dgt_send, dgt_in,
    d_middle, gates_ref, params, own_rows, common_rows, early, early_in, early_all, late, late_in, late_all,
    w_qkv, b_qkv, sink_row, final, dall, sems, credit, free_xy, passed,
):
    dp = lax.axis_index("dp")
    g = lax.axis_index("expert")
    y, x = lax.div(dp, 4), lax.rem(dp, 4)
    z, c = lax.div(g, 2), lax.rem(g, 2)
    xs = [lax.rem(x + d, 4) for d in range(4)]
    ys = [lax.rem(y + d, 4) for d in range(4)]
    zs = [lax.rem(z + d, 4) for d in range(4)]
    gs = [lax.rem(g + d, 8) for d in range(8)]
    other = 1 - c
    sib = {"expert": z * 2 + (1 - c)}
    up = {"expert": zs[1] * 2 + c}
    down = {"expert": zs[3] * 2 + c}

    neighbours = {
        "x": [{"dp": y * 4 + xs[d]} for d in range(4)],
        "y": [{"dp": ys[d] * 4 + x} for d in range(4)],
    }

    def xy(axis, d):
        return neighbours[axis][d]

    first = [xs, ys]
    second = [ys, xs]

    lines = [[second[h][db] * 4 for db in range(4)] for h in range(2)]

    def slot(h, da, db):
        return second[h][db] * 4 + first[h][da]

    counter = [0]

    def sem():
        counter[0] += 1
        assert counter[0] <= NSEM
        return counter[0] - 1

    def sem_block(n):
        first = counter[0]
        counter[0] += n
        assert counter[0] <= NSEM
        return first

    def view(ref):
        return ref() if callable(ref) else ref

    class Ring:
        def __init__(self, n):
            self.base, self.n, self.at, self.live = sem_block(n), n, 0, {}

        def take(self, copy):
            k = self.base + self.at % self.n
            self.at += 1
            if k in self.live:
                self.live[k].wait()
            self.live[k] = copy
            return k

    class Remote:
        def __init__(self, src, dst, recv, dev, ring):
            self.src, self.dst, self.recv, self.dev, self.done = src, dst, recv, dev, False
            self.n = ring.take(self)
            self.make().start()

        def make(self):
            return pltpu.make_async_remote_copy(
                src_ref=view(self.src), dst_ref=view(self.dst), send_sem=sems.at[self.n], recv_sem=sems.at[self.recv],
                device_id=self.dev, device_id_type=MESH)

        def wait(self):
            if not self.done:
                self.make().wait_send()
                self.done = True

    class Local(Remote):
        def __init__(self, src, dst, ring):
            self.src, self.dst, self.done = src, dst, False
            self.n = ring.take(self)
            self.make().start()

        def make(self):
            return pltpu.make_async_copy(view(self.src), view(self.dst), sems.at[self.n])

        def wait(self):
            if not self.done:
                self.make().wait()
                self.done = True

    ring_w, ring_z, ring_l = Ring(100), Ring(80), Ring(40)
    pending = []
    pending_weights = [[] for _ in range(4)]

    def send(src, dst, recv, dev, keep, ring=ring_z):
        keep.append(Remote(src, dst, recv, dev, ring))

    def local_copy(src, dst):
        return Local(src, dst, ring_l)

    def arrived(dst, recv):
        pltpu.make_async_remote_copy(
            src_ref=dst, dst_ref=dst, send_sem=sems.at[recv], recv_sem=sems.at[recv],
            device_id=sib, device_id_type=MESH,
        ).wait_recv()

    def drain(copies):
        for copy in copies:
            copy.wait()
        copies.clear()

    barrier = pltpu.get_barrier_semaphore()
    for rel in range(1, 8):
        pl.semaphore_signal(barrier, inc=1, device_id={"expert": gs[rel]}, device_id_type=MESH)
    for axis in ("x", "y"):
        for d in (1, 2, 3):
            pl.semaphore_signal(barrier, inc=1, device_id=xy(axis, d), device_id_type=MESH)
    pl.semaphore_wait(barrier, 13)

    class GatherZ:
        def __init__(self, buf, own):
            self.buf, self.own = buf, own
            self.k = sem_block(9)
            self.sent = []
            self.m1, self.p1, self.far = zs[3] * 2 + c, zs[1] * 2 + c, zs[2] * 2 + c
            s = 1 - c
            self.sm1, self.sp1, self.sfar, self.so = (
                zs[3] * 2 + s, zs[1] * 2 + s, zs[2] * 2 + s, z * 2 + s)

        def start(self):
            b, k = self.buf, self.k
            send(self.own, lambda: b.at[g], k + 1, up, self.sent)
            send(self.own, lambda: b.at[g], k + 2, down, self.sent)
            send(self.own, lambda: b.at[g], k + 0, sib, self.sent)

        def step_m1(self):
            b, k, s = self.buf, self.k, self.m1
            arrived(b.at[s], k + 1)
            send(lambda: b.at[s, pl.ds(0, 128)], lambda: b.at[s, pl.ds(0, 128)], k + 3, up, self.sent)
            send(lambda: b.at[s], lambda: b.at[s], k + 4, sib, self.sent)

        def step_p1(self):
            b, k, s = self.buf, self.k, self.p1
            arrived(b.at[s], k + 2)
            send(lambda: b.at[s, pl.ds(128, 128)], lambda: b.at[s, pl.ds(128, 128)], k + 5, down, self.sent)
            send(lambda: b.at[s], lambda: b.at[s], k + 6, sib, self.sent)

        def step_far(self):
            b, k, s = self.buf, self.k, self.far
            for i, kr, ks in ((0, 3, 7), (128, 5, 8)):
                arrived(b.at[s, pl.ds(i, 128)], k + kr)
                send(lambda i=i: b.at[s, pl.ds(i, 128)], lambda i=i: b.at[s, pl.ds(i, 128)], k + ks, sib, self.sent)

        def wait_sib_own(self):
            arrived(self.buf.at[self.so], self.k)

        def wait_sib_m1(self):
            arrived(self.buf.at[self.sm1], self.k + 4)

        def wait_sib_p1(self):
            arrived(self.buf.at[self.sp1], self.k + 6)

        def wait_sib_far(self):
            for i, ks in ((0, 7), (128, 8)):
                arrived(self.buf.at[self.sfar, pl.ds(i, 128)], self.k + ks)

    class ScatterZ:
        def __init__(self, k, buf, sib_ref, half_ref, full_ref, sizes=(128, 128)):
            self.buf, self.r, self.h, self.f = buf, sib_ref, half_ref, full_ref
            self.sizes, self.rows = sizes, sum(sizes)
            self.mine = [zs[d] * 2 + c for d in range(4)]
            self.k = k
            self.sent = []

        def chunks(self):
            return [zs[d] * 2 + (1 - c) for d in (2, 1, 3, 0)], [zs[d] * 2 + c for d in (2, 1, 3, 0)]

        def to_sibling(self, n):
            d = (2, 1, 3, 0)[n]
            zz = zs[d]
            send(lambda: self.buf.at[zz * 2 + (1 - c), pl.ds(0, self.rows)], lambda: self.r(d), self.k + n, sib, self.sent)

        def add(self, chunk, refs, base=0, rows=None):
            rows = rows or self.rows
            step = 64 if rows % 64 == 0 else 16

            def body(i, carry):
                at = pl.ds(pl.multiple_of(base + i * step, 16), step)
                ref_at = pl.ds(pl.multiple_of(i * step, 16), step)
                v = self.buf[chunk, at, :].astype(F32)
                for ref in refs:
                    v = v + ref[ref_at, :].astype(F32)
                self.buf[chunk, at, :] = v.astype(BF)
                return carry
            lax.fori_loop(0, rows // step, body, 0)

        def step1(self):
            b, k = self.buf, self.k
            chunk = self.mine[2]
            arrived(self.r(2), k + 0)
            self.add(chunk, [self.r(2)])
            lo, hi = self.sizes
            send(lambda: b.at[chunk, pl.ds(0, lo)], lambda: self.h(0), k + 4, up, self.sent)
            send(lambda: b.at[chunk, pl.ds(lo, hi)], lambda: self.h(1), k + 5, down, self.sent)

        def step2(self):
            b, k = self.buf, self.k
            for d, n, hi, dev in ((1, 1, 0, up), (3, 2, 1, down)):
                chunk = self.mine[d]
                arrived(self.r(d), k + n)
                self.add(chunk, [self.r(d)])
                arrived(self.h(hi), k + 4 + hi)
                self.add(chunk, [self.h(hi)], hi * self.sizes[0], self.sizes[hi])
                send(lambda chunk=chunk: b.at[chunk, pl.ds(0, self.rows)], lambda hi=hi: self.f(hi), k + 6 + hi, dev, self.sent)

        def step3(self):
            arrived(self.r(0), self.k + 3)
            arrived(self.f(0), self.k + 6)
            arrived(self.f(1), self.k + 7)

        def result(self, rows):
            return (self.buf[g, rows, :].astype(F32) + self.r(0)[rows, :].astype(F32)
                    + self.f(0)[rows, :].astype(F32) + self.f(1)[rows, :].astype(F32))

    around = [xy("x", 1), xy("x", 3), xy("y", 1), xy("y", 3)]

    def axis_of(h, ax):
        return "x" if (ax == 0) == (h == 0) else "y"

    gk = sem_block(2 * 4 * 7)

    def wsem(h, e):
        return gk + (h * 4 + e) * 7

    def row_of(h, e, db):
        return gathered.at[h, e, pl.ds(second[h][db] * 4, 4)]

    def one_of(h, e, da):
        return gathered.at[h, e, slot(h, da, 0)]

    local_w = {}

    def weights_start():
        for e in range(4):
            for h in range(2):
                for n, d in ((0, 1), (1, 3)):
                    send(lambda h=h, e=e: w_in.at[h, e], lambda h=h, e=e: one_of(h, e, 0), wsem(h, e) + n,
                         xy(axis_of(h, 0), d), pending_weights[e], ring_w)
                local_w[h, e] = local_copy(lambda h=h, e=e: w_in.at[h, e], lambda h=h, e=e: one_of(h, e, 0))

    def weights_near(e):
        for h in range(2):
            k = wsem(h, e)
            arrived(one_of(h, e, 3), k)
            if e % 2 == 0:
                send(lambda h=h: one_of(h, e, 3), lambda h=h: one_of(h, e, 3), k + 2, xy(axis_of(h, 0), 1),
                     pending_weights[e], ring_w)
            arrived(one_of(h, e, 1), k + 1)
            if e % 2 == 1:
                send(lambda h=h: one_of(h, e, 1), lambda h=h: one_of(h, e, 1), k + 2, xy(axis_of(h, 0), 3),
                     pending_weights[e], ring_w)

    def weights_turn(e):
        for h in range(2):
            k = wsem(h, e)
            arrived(one_of(h, e, 2), k + 2)
            local_w[h, e].wait()
            for n, d in ((3, 1), (4, 3)):
                send(lambda h=h: row_of(h, e, 0), lambda h=h: row_of(h, e, 0), k + n, xy(axis_of(h, 1), d),
                     pending_weights[e], ring_w)

    def weights_row(e):
        for h in range(2):
            k = wsem(h, e)
            arrived(row_of(h, e, 3), k + 3)
            if e % 2 == 0:
                send(lambda h=h: row_of(h, e, 3), lambda h=h: row_of(h, e, 3), k + 5, xy(axis_of(h, 1), 1),
                     pending_weights[e], ring_w)
            arrived(row_of(h, e, 1), k + 4)
            if e % 2 == 1:
                send(lambda h=h: row_of(h, e, 1), lambda h=h: row_of(h, e, 1), k + 5, xy(axis_of(h, 1), 3),
                     pending_weights[e], ring_w)

    def weights_end(e):
        for h in range(2):
            arrived(row_of(h, e, 2), wsem(h, e) + 5)
        for dev in around:
            pl.semaphore_signal(passed.at[e], inc=1, device_id=dev, device_id_type=MESH)

    def weights_steps():
        order = [(weights_near, 0), (weights_near, 1), (weights_turn, 0), (weights_near, 2), (weights_turn, 1),
                 (weights_near, 3), (weights_turn, 2), (weights_turn, 3), (weights_row, 0), (weights_row, 1),
                 (weights_row, 2), (weights_row, 3), (weights_end, 0), (weights_end, 1), (weights_end, 2),
                 (weights_end, 3)]
        for step, e in order:
            step(e)
            yield (step, e)

    late[0] = jnp.zeros((8, D), F32)
    final[...] = jnp.zeros((8, D), F32)
    own_rows[...] = jnp.zeros((16, D), F32)
    common_rows[...] = jnp.zeros((8, D), F32)
    local_x = local_copy(x_in, lambda: xg.at[g])
    gather_x = GatherZ(xg, x_in)
    gather_x.start()
    weights_start()
    local_q = [
        local_copy(lambda: w_qkv_in.at[:, pl.ds(pl.multiple_of(g * 128, 128), 128)], lambda: w_qkv.at[:, pl.ds(0, 128)]),
        local_copy(lambda: w_qkv_in.at[:, pl.ds(pl.multiple_of(1024 + z * 128, 128), 128)], lambda: w_qkv.at[:, pl.ds(128, 128)]),
    ] + [
        local_copy(lambda n=n: w_qkv_in.at[pl.ds(n * T, T), pl.ds(pl.multiple_of(1536 + z * 128, 128), 128)],
                   lambda n=n: outb.at[n, :, pl.ds(0, 128)])
        for n in range(4)
    ]
    weights = weights_steps()

    def svc(n=1):
        for _ in range(n):
            if next(weights, None) is None:
                return

    lane = lax.broadcasted_iota(jnp.int32, (1, 128), 1)
    low_half = lane < 64
    first_quarter = (lane % 64) < 32
    mask0 = jnp.where(low_half, 1.0, 0.0).astype(F32)
    mask1 = 1.0 - mask0

    def swap(v):
        return jnp.where(first_quarter, pltpu.roll(v, 96, 1), pltpu.roll(v, 32, 1))

    def trig(r):
        cb, sb = cos_b[pl.ds(r, 1), :], sin_b[pl.ds(r, 1), :]
        ca, sa = cos_a[...], sin_a[...]
        cosine = ca * cb - sa * sb
        sine = sa * cb + ca * sb
        return cosine, jnp.where(first_quarter, -sine, sine)

    def h1_rows(r, rows):
        xf = xg[r, rows, :].astype(F32)
        inv = lax.rsqrt(jnp.mean(xf * xf, axis=-1, keepdims=True) + EPS)
        return (xf * inv * attn_gain[...]).astype(BF)

    def qkv_chunk(r):
        h1 = h1_rows(r, pl.ds(0, T))
        mixed = nn(h1, w_qkv[...]) + b_qkv[...]
        cosine, sine = trig(r)
        q = mixed[:, :128]
        kv = mixed[:, 128:]
        q = (q * cosine + swap(q) * sine) * 0.125
        kv = jnp.where(low_half, kv * cosine + swap(kv) * sine, kv)
        other = pltpu.roll(kv, 64, 1)
        kd = jnp.where(low_half, kv, other)
        vd = jnp.where(low_half, other, kv)
        qs[r] = q.astype(BF)
        kk[r] = kd.astype(BF)
        vv[r] = vd.astype(BF)
        kkt[r] = kd.T.astype(BF)
        vvt[r] = vd.T.astype(BF)

    even = c == 0

    def pair(first, second):
        k_own = jnp.where(even, first, pltpu.roll(first, 64, 1))
        v_own = jnp.where(even, pltpu.roll(second, 64, 1), second)
        return jnp.where(low_half, k_own, v_own)

    for copy in local_q:
        copy.wait()

    def pair_rows(i, carry):
        rows = pl.ds(pl.multiple_of(i * 256, 256), 256)
        w_qkv[rows, pl.ds(128, 128)] = pair(
            w_qkv[rows, pl.ds(128, 128)].astype(F32), outb[i, :, pl.ds(0, 128)].astype(F32)).astype(BF)
        return carry

    lax.fori_loop(0, 4, pair_rows, 0)
    b_qkv[:, pl.ds(0, 128)] = b_qkv_in[:, pl.ds(pl.multiple_of(g * 128, 128), 128)]
    b_qkv[:, pl.ds(128, 128)] = pair(
        b_qkv_in[:, pl.ds(pl.multiple_of(1024 + z * 128, 128), 128)],
        b_qkv_in[:, pl.ds(pl.multiple_of(1536 + z * 128, 128), 128)])
    lane_all = lax.broadcasted_iota(jnp.int32, (1, 128), 1)
    for n in range(2):
        one = jnp.sum(jnp.where(lane_all == g * 2 + n, sinks[...], 0.0), axis=1, keepdims=True)
        sink_row[:, pl.ds(n * T, T)] = jnp.broadcast_to(one, (1, T))

    gx = gather_x
    local_x.wait()
    qkv_chunk(g)
    gx.wait_sib_own()
    qkv_chunk(gx.so)
    svc(1)
    gx.step_m1()
    gx.step_p1()
    qkv_chunk(gx.m1)
    svc(1)
    qkv_chunk(gx.p1)
    svc(1)
    gx.wait_sib_m1()
    qkv_chunk(gx.sm1)
    svc(1)
    gx.wait_sib_p1()
    qkv_chunk(gx.sp1)
    svc(1)
    gx.step_far()
    local_dy = local_copy(dy_in, lambda: dyg.at[g])
    gather_dy = GatherZ(dyg, dy_in)
    gather_dy.start()
    qkv_chunk(gx.far)
    svc(1)
    gx.wait_sib_far()
    qkv_chunk(gx.sfar)
    svc(2)

    def stacked(v):
        vf = v.astype(F32)
        return jnp.concatenate([vf * mask0, vf * mask1], axis=0).astype(BF)

    key_at = lax.broadcasted_iota(jnp.int32, (T, 2 * T), 0)
    query_at = lax.broadcasted_iota(jnp.int32, (T, 2 * T), 1) % T
    allowed = key_at <= query_at

    att_k = sem_block(8)

    def own_tile(n):
        return pl.ds(pl.multiple_of(n * 128, 128), 128)

    def attend(rel, m_ref, l_ref, acc_ref):
        i = gs[rel % 8]
        q2 = stacked(qs[i])
        m_ref[...] = sink_row[...]
        l_ref[...] = jnp.ones((1, 2 * T), F32)
        acc_ref[...] = jnp.zeros((128, 2 * T), F32)

        def blocks(keys, diagonal):
            scores = [nt(kk[j], q2) for j in keys]
            if diagonal:
                scores = [jnp.where(allowed, s, NEG) for s in scores]
            m_old = m_ref[...]
            m_new = m_old
            for s in scores:
                m_new = jnp.maximum(m_new, jnp.max(s, axis=0, keepdims=True))
            alpha = jnp.exp(m_old - m_new)
            total = l_ref[...] * alpha
            acc = acc_ref[...] * alpha
            for j, s in zip(keys, scores):
                p = jnp.exp(s - m_new)
                total = total + jnp.sum(p, axis=0, keepdims=True)
                acc = acc + nn(vvt[j], p.astype(BF))
            l_ref[...] = total
            acc_ref[...] = acc
            m_ref[...] = m_new

        def body(j, carry):
            blocks((2 * j, 2 * j + 1), False)
            return carry

        lax.fori_loop(0, lax.div(i, 2), body, 0)

        @pl.when(lax.rem(i, 2) == 1)
        def _():
            blocks((i - 1,), False)

        blocks((i,), True)
        total = l_ref[...]
        lse[i] = m_ref[...] + jnp.log(total)
        o = (acc_ref[...] / total).T
        att_send[i] = jnp.where(low_half, o[:T], o[T:]).astype(BF)

        if rel < 8:
            send(lambda: att_send.at[i], lambda: att.at[:, own_tile(g)], att_k + rel, {"expert": i}, att_fwd)
        else:
            att[:, own_tile(g)] = att_send[i]

    att_fwd = []

    def forward_attention(m_ref, l_ref, acc_ref):
        gd = gather_dy
        for i in range(8):
            attend(i + 1, m_ref, l_ref, acc_ref)
            if i == 3:
                gd.step_m1()
                gd.step_p1()
            if i == 6:
                gd.step_far()
            if i in (3, 6):
                svc(1)

    pl.run_scoped(
        forward_attention, pltpu.VMEM((1, 2 * T), F32), pltpu.VMEM((1, 2 * T), F32), pltpu.VMEM((128, 2 * T), F32))

    for rel in range(1, 8):
        arrived(att.at[:, own_tile(gs[8 - rel])], att_k + rel)
    drain(att_fwd)

    def project(i, carry):
        rows = pl.ds(pl.multiple_of(i * 64, 64), 64)
        m = xg[g, rows, :].astype(F32) + (nn(att[rows, :], w_out[...]) + b_out[...])
        middle[rows, :] = m
        inv = lax.rsqrt(jnp.mean(m * m, axis=-1, keepdims=True) + EPS)
        h2own[rows, :] = (m * inv * moe_gain[...]).astype(BF)
        return carry

    lax.fori_loop(0, 4, project, 0)
    gather_h = GatherZ(h2g, h2own)
    gather_h.start()

    logits = nt(w_rt[...], h2own[...]) + b_rt[...]
    row = lax.broadcasted_iota(jnp.int32, (64, T), 0)
    expert_of_row = jnp.where(row % 8 < 4, (row // 8) * 4 + row % 8, -1)
    slots = jnp.full((64, T), -1.0, F32)
    for k in range(4):
        tgt = target[pl.ds(k, 1), :]
        slots = jnp.where(expert_of_row == tgt // 64, (tgt % 64).astype(F32), slots)
    member = slots >= 0.0
    masked = jnp.where(member, logits, NEG)
    top = jnp.max(masked, axis=0, keepdims=True)
    weight = jnp.where(member, jnp.exp(masked - top), 0.0)
    gates = weight / jnp.sum(weight, axis=0, keepdims=True)
    gates_ref[...] = gates
    for r in range(8):
        meta_send[r, pl.ds(0, 8), :] = gates[r * 8:r * 8 + 8]
        meta_send[r, pl.ds(8, 8), :] = slots[r * 8:r * 8 + 8]
    meta_k = sem_block(8)
    meta_sent = []
    metag[g] = meta_send[g]
    for rel in range(1, 8):
        r = gs[rel]
        send(lambda r=r: meta_send.at[r], lambda: metag.at[g], meta_k + rel, {"expert": r}, meta_sent)
    svc(1)
    gh = gather_h
    slot_at = lax.broadcasted_iota(jnp.int32, (64, T), 0).astype(F32)

    def hot_rows(s, e):
        return (slot_at == metag[s, pl.ds(8 + e, 1), :]).astype(F32)

    def take(buf, s, src=None):
        hot = jnp.concatenate([hot_rows(s, e) for e in range(4)], axis=0).astype(BF)
        buf[s] = nn(hot, buf[s] if src is None else src[...]).astype(BF)

    take(h2g, g, h2own)
    gd = gather_dy
    local_dy.wait()
    gd.wait_sib_own()
    gd.wait_sib_m1()
    gd.wait_sib_p1()
    gd.wait_sib_far()
    drain(gd.sent)
    for rel in range(1, 8):
        arrived(metag.at[gs[8 - rel]], meta_k + rel)
    drain(meta_sent)
    gh.wait_sib_own()
    take(h2g, gh.so)
    for s in (g, gd.so, gd.sm1, gd.sp1):
        take(dyg, s)
    svc(1)
    gh.step_m1()
    gh.step_p1()
    for s in (gd.sfar, gd.m1, gd.p1, gd.far):
        take(dyg, s)
    gh.wait_sib_m1()
    take(h2g, gh.sm1)
    gh.wait_sib_p1()
    take(h2g, gh.sp1)
    gh.step_far()
    gh.wait_sib_far()
    take(h2g, gh.sfar)
    drain(gh.sent)
    for s in (gh.m1, gh.p1, gh.far):
        take(h2g, s)

    def weight_of(h, e, n):
        return gathered[h, e, :, pl.ds(n * 16, 16), :].reshape(T, D)

    def rows_of(buf, e, i):
        return buf[pl.ds(i * 4, 4), pl.ds(e * 64, 64), :].reshape(T, D)

    def expert(e, gated_ref, dg_ref, du_ref):
        for item in weights:
            if item == (weights_end, e):
                break

        def some_rows(i, carry):
            rows = pl.ds(pl.multiple_of(i * T, T), T)
            rv = rows_of(h2g, e, i)
            dyv = rows_of(dyg, e, i)
            hots = [hot_rows(i * 4 + n, e) for n in range(4)]
            gcol = jnp.concatenate(
                [jnp.sum(hots[n] * metag[i * 4 + n, pl.ds(e, 1), :], axis=1, keepdims=True) for n in range(4)], axis=0)
            sums = []
            acts, grads = [], []
            for h in range(2):
                cols = pl.ds(h * T, T)
                wg, wu, wd = weight_of(h, e, 0), weight_of(h, e, 1), weight_of(h, e, 2)
                gr = jnp.tanh((nt(rv, wg) + gu_bias[e, pl.ds(0, 1), cols]) * (1.0 / LIMIT))
                ur = jnp.tanh((nt(rv, wu) + gu_bias[e, pl.ds(1, 1), cols]) * (1.0 / LIMIT))
                da = nt(dyv, wd) * gcol
                gc = LIMIT * gr
                uc = LIMIT * ur + 1.0
                sig = 0.5 * jnp.tanh((0.5 * ALPHA) * gc) + 0.5
                glu = gc * sig
                act = uc * glu
                act_low = act.astype(BF)
                gated_ref[rows, cols] = (act * gcol).astype(BF)
                dg = (da * uc * (sig + ALPHA * glu * (1.0 - sig)) * (1.0 - gr * gr)).astype(BF)
                du = (da * glu * (1.0 - ur * ur)).astype(BF)
                dg_ref[rows, cols] = dg
                du_ref[rows, cols] = du
                sums.append(jnp.sum(dg.astype(F32), axis=0, keepdims=True))
                sums.append(jnp.sum(du.astype(F32), axis=0, keepdims=True))
                acts.append(act_low)
                grads.extend([dg, du])
            for h in range(2):
                part = nn(acts[h], weight_of(h, e, 2))
                out = part + down_bias[pl.ds(e, 1), :] if h == 0 else out + part
            out_low = out.astype(BF)
            dyf = dyv.astype(F32)
            dgate = jnp.sum(dyf * out_low.astype(F32), axis=1, keepdims=True)
            for n in range(4):
                s = i * 4 + n
                outb[s, pl.ds(e * 64, 64), :] = out_low[n * 64:n * 64 + 64]
                dgt_send[s, pl.ds(e, 1), :] = jnp.sum(hots[n] * dgate[n * 64:n * 64 + 64], axis=0, keepdims=True)
            for n, (h, m) in enumerate(((0, 0), (0, 1), (1, 0), (1, 1))):
                part = nn(grads[n], weight_of(h, e, m))
                drow = part if n == 0 else drow + part
            drow_low = drow.astype(BF)
            for n in range(4):
                drb[i * 4 + n, pl.ds(e * 64, 64), :] = drow_low[n * 64:n * 64 + 64]
            sums.append(jnp.sum(dyf * gcol, axis=0, keepdims=True))
            return tuple(a + b for a, b in zip(carry, sums))

        zero = jnp.zeros((1, T), F32)
        sums = lax.fori_loop(0, 2, some_rows, (zero, zero, zero, zero, jnp.zeros((1, D), F32)))
        for h in range(2):
            own_rows[pl.ds(8 + e, 1), pl.ds(h * T, T)] = sums[2 * h]
            own_rows[pl.ds(8 + e, 1), pl.ds(512 + h * T, T)] = sums[2 * h + 1]
        own_rows[pl.ds(4 + e, 1), :] = sums[4]

    def weight_grads(e, gated_ref, dg_ref, du_ref):
        drain(pending_weights[e])
        for h in range(2):
            for n, (left, buf) in enumerate(((dg_ref, h2g), (du_ref, h2g), (gated_ref, dyg))):
                right = buf[:, pl.ds(e * 64, 64), :].reshape(512, D)
                grad = tn(left[:, pl.ds(h * T, T)], right)
                gathered[h, e, :, pl.ds(n * 16, 16), :] = grad.astype(BF).reshape(16, 16, D)

    out_copies = []

    class WeightPieces:
        def __init__(self, e, h):
            self.e, self.h, self.k = e, h, wsem(h, e)

        def own(self, s):
            return gathered.at[self.h, self.e, s]

        def rows(self, first_slot, n):
            return gathered.at[self.h, self.e, pl.ds(first_slot, n)]

        def half(self, side):
            return rs_half.at[self.e, self.h, side]

        def full(self, side):
            if self.e < 2:
                return rs_full.at[self.e, self.h, side]
            return h2g.at[self.lent(side), pl.ds(0, 192)]

        def lent(self, side):
            return ((self.e - 2) * 2 + self.h) * 2 + side

        def full_one(self, side, a):
            if self.e < 2:
                return rs_full.at[self.e, self.h, side, a]
            return h2g.at[self.lent(side), pl.ds(a * 48 if isinstance(a, int) else pl.multiple_of(a * 48, 48), 48)]

        def send_row(self, first_slot, side, recv, dev, keep):
            if self.e < 2:
                send(lambda: self.rows(first_slot, 4), lambda: self.full(side), recv, dev, keep, ring_w)
            else:
                for a in range(4):
                    send(lambda a=a: self.own(first_slot + a), lambda a=a: self.full_one(side, a), recv, dev, keep, ring_w)

        def half2(self):
            return rs2_half.at[self.e, self.h]

        def full2(self, side):
            return rs2_full.at[self.e, self.h, side]

        def finish(self):
            for n, out in enumerate((d_gate_w, d_up_w, d_down_w)):
                out_copies.append(local_copy(
                    lambda n=n: self.own(slot(self.h, 0, 0)).at[pl.ds(n * 16, 16)],
                    lambda out=out: out.at[self.e, pl.ds(self.h * 16, 16)]))

    class ParamPieces(WeightPieces):
        def __init__(self, h):
            self.e, self.h, self.k = 0, h, wsem(h, 0)

        def own(self, s):
            return params.at[self.h, s]

        def rows(self, first_slot, n):
            return params.at[self.h, pl.ds(first_slot, n)]

        def half(self, side):
            return rs_half.at[0, self.h, side, :, pl.ds(0, 16), pl.ds(0, 768)]

        def full(self, side):
            return rs_full.at[0, self.h, side, :, pl.ds(0, 16), pl.ds(0, 768)]

        def full_one(self, side, a):
            return rs_full.at[0, self.h, side, a, pl.ds(0, 16), pl.ds(0, 768)]

        def half2(self):
            return rs2_half.at[0, self.h, pl.ds(0, 16), pl.ds(0, 768)]

        def full2(self, side):
            return rs2_full.at[0, self.h, side, pl.ds(0, 16), pl.ds(0, 768)]

        def finish(self):
            pass

    def scatter_xy(p, even_way, wait_for, keep):
        h, k = p.h, p.k
        fwd, back = xy(axis_of(h, 1), 1), xy(axis_of(h, 1), 3)
        fwd2, back2 = xy(axis_of(h, 0), 1), xy(axis_of(h, 0), 3)
        line = lines[h]

        def add(s, refs):
            v = p.own(s)[...].astype(F32)
            for ref in refs:
                v = v + ref[...].astype(F32)
            p.own(s)[...] = v.astype(BF)

        send(lambda: p.rows(line[2], 2), lambda: p.half(0), k, fwd, keep, ring_w)
        send(lambda: p.rows(line[2] + 2, 2), lambda: p.half(1), k + 1, back, keep, ring_w)
        yield 1
        for side, db, dev in ((0, 1, fwd), (1, 3, back)):
            if wait_for:
                pl.semaphore_wait(credit.at[h, side], 1)
            arrived(p.half(side), k + side)
            for n in range(2):
                add(line[db] + side * 2 + n, [p.half(side).at[n]])
            p.send_row(line[db], side, k + 2 + side, dev, keep)
        yield 2
        arrived(p.full(0), k + 2)
        arrived(p.full(1), k + 3)
        for da in (2, 1, 3, 0):
            a = first[h][da]
            add(line[0] + a, [p.full_one(0, a), p.full_one(1, a)])
            if da == 2:
                send(lambda: p.own(slot(h, 2, 0)), p.half2, k + 4, fwd2 if even_way else back2, keep, ring_w)
        yield 3
        arrived(p.half2(), k + 4)
        add(slot(h, 1 if even_way else 3, 0), [p.half2()])
        send(lambda: p.own(slot(h, 1, 0)), lambda: p.full2(0), k + 5, fwd2, keep, ring_w)
        send(lambda: p.own(slot(h, 3, 0)), lambda: p.full2(1), k + 6, back2, keep, ring_w)
        yield 4
        for side in range(2):
            arrived(p.full2(side), k + 5 + side)
        add(slot(h, 0, 0), [p.full2(0), p.full2(1)])
        p.finish()
        yield 5

    scatters = [[scatter_xy(WeightPieces(e, h), e % 2 == 0, e == 2, pending) for h in range(2)] for e in range(4)]

    started = set()

    def wsvc(*experts):
        for e in experts:
            if e not in started:
                started.add(e)
                pl.semaphore_wait(passed.at[e], 4)
            for h in range(2):
                next(scatters[e][h], None)

    dg_k = att_k
    dgt_sent = []

    def combine(buf, s, gated):
        pieces = []
        for e in range(4):
            hot = hot_rows(s, e)
            if gated:
                hot = hot * metag[s, pl.ds(e, 1), :]
            pieces.append(hot)
        spread = jnp.concatenate(pieces, axis=0).T.astype(BF)
        buf[s] = nn(spread, buf[s]).astype(BF)

    scatter_d = ScatterZ(gather_x.k, drb, lambda n: sib_in.at[n], lambda n: half_in.at[n], lambda n: full_in.at[n])
    far_chunks, own_chunks = scatter_d.chunks()

    def experts(*refs):
        for e in range(4):
            expert(e, *refs)
            if e < 3:
                weight_grads(e, *refs)
                wsvc(e)
            if e in (1, 2):
                wsvc(e - 1)
        dgt_in[g] = dgt_send[g]
        for rel in range(1, 8):
            r = gs[rel]
            send(lambda r=r: dgt_send.at[r], lambda: dgt_in.at[g], dg_k + rel, {"expert": r}, dgt_sent)
        for n in range(4):
            combine(drb, far_chunks[n], False)
            scatter_d.to_sibling(n)
        combine(drb, own_chunks[0], False)
        scatter_d.step1()
        weight_grads(3, *refs)
        for h in range(2):
            pl.semaphore_signal(credit.at[h, 1], inc=1, device_id=xy(axis_of(h, 1), 1), device_id_type=MESH)
            pl.semaphore_signal(credit.at[h, 0], inc=1, device_id=xy(axis_of(h, 1), 3), device_id_type=MESH)
        wsvc(3)
        combine(drb, own_chunks[1], False)
        combine(drb, own_chunks[2], False)
        scatter_d.step2()
        combine(drb, own_chunks[3], False)

    pl.run_scoped(
        experts,
        pltpu.VMEM((512, 512), BF), pltpu.VMEM((512, 512), BF), pltpu.VMEM((512, 512), BF))
    local_dy = local_copy(dy_in, lambda: dyg.at[g])
    wsvc(2, 0)
    for n in range(4):
        combine(outb, far_chunks[n], True)
    for n in range(4):
        combine(outb, own_chunks[n], True)
    scatter_d.step3()

    for rel in range(1, 8):
        arrived(dgt_in.at[gs[8 - rel]], dg_k + rel)
    d_gates = jnp.where(row % 8 < 4, jnp.concatenate([dgt_in[r] for r in range(8)], axis=0), 0.0)
    d_logits = gates_ref[...] * (d_gates - jnp.sum(gates_ref[...] * d_gates, axis=0, keepdims=True))
    dl_high, dl_low = split_low(d_logits)
    d_wrt = nn(dl_high, h2own[...]) + nn(dl_low, h2own[...])
    common_rows[pl.ds(6, 1), pl.ds(0, 64)] = jnp.sum(d_logits.T, axis=0, keepdims=True)
    dl_high_t, dl_low_t = split_low(d_logits.T)
    d_middle[...] = nn(dl_high_t, w_rt[...]) + nn(dl_low_t, w_rt[...])
    drain(scatter_d.sent)
    drain(gather_x.sent)
    local_dy.wait()
    att_grad, branch_at = h2own, 7

    def middle_back(i, carry):
        rows = pl.ds(pl.multiple_of(i * 64, 64), 64)
        m = middle[rows, :]
        inv = lax.rsqrt(jnp.mean(m * m, axis=-1, keepdims=True) + EPS)
        d_h2 = scatter_d.result(rows) + d_middle[rows, :]
        v2 = d_h2 * moe_gain[...]
        inner = jnp.mean(v2 * m, axis=-1, keepdims=True)
        dm = dyg[g, rows, :].astype(F32) + inv * v2 - m * (inv * inv * inv * inner)
        d_middle[rows, :] = dm
        low = dm.astype(BF)
        dyg[branch_at, rows, :] = low
        att_grad[rows, :] = nt(low, w_out[...]).astype(BF)
        return (carry[0] + jnp.sum(low.astype(F32), axis=0, keepdims=True),
                carry[1] + jnp.sum(d_h2 * m * inv, axis=0, keepdims=True))

    zero_row = jnp.zeros((1, D), F32)
    sum_b, sum_m = lax.fori_loop(0, 4, middle_back, (zero_row, zero_row))
    common_rows[pl.ds(4, 1), :] = sum_b
    common_rows[pl.ds(5, 1), :] = sum_m

    do_k = meta_k
    att_sent = []
    dob[g] = att_grad[:, pl.ds(pl.multiple_of(g * 128, 128), 128)]
    for rel in range(1, 8):
        r = gs[rel]
        send(lambda r=r: att_grad.at[:, pl.ds(pl.multiple_of(r * 128, 128), 128)], lambda: dob.at[g], do_k + rel, {"expert": r}, att_sent)
    drain(dgt_sent)

    eight = lax.broadcasted_iota(jnp.int32, (8, D), 0)
    for r in range(8):
        rows = pl.ds(r * 128, 128)
        drb[r, pl.ds(0, 128), :] = tn(att[:, rows], dyg[branch_at]).astype(BF)
        mine = jnp.where(g == r, 1.0, 0.0).astype(F32)
        top = jnp.where(eight < 4, d_wrt[r * 8:r * 8 + 8], own_rows[pl.ds(0, 8), :] * mine)
        low_rows = own_rows[pl.ds(8, 8), :] * mine
        if r == 0:
            low_rows = jnp.where(eight < 4, low_rows, common_rows[...])
        drb[r, pl.ds(128, 16), :] = jnp.concatenate([top, low_rows], axis=0).astype(BF)
    wsvc(1, 3)
    for rel in range(1, 8):
        arrived(dob.at[gs[8 - rel]], do_k + rel)

    scatter_m = ScatterZ(
        gather_dy.k, outb, lambda n: dyg.at[n], lambda n: dyg.at[4, pl.ds(n * 128, 128)], lambda n: dyg.at[5 + n])
    for n in range(4):
        scatter_m.to_sibling(n)
    scatter_w = ScatterZ(
        gather_h.k, drb, lambda n: sib_in.at[n, pl.ds(0, 144)], lambda n: half_in.at[n, pl.ds(0, (80, 64)[n])],
        lambda n: full_in.at[n, pl.ds(0, 144)], (80, 64))
    for n in range(4):
        scatter_w.to_sibling(n)

    class Exchange:
        def __init__(self, stage, inbox, everyone, k):
            self.stage, self.inbox, self.everyone, self.spread_k = stage, inbox, everyone, k
            self.k = sem_block(6)
            self.sent = []

        def start(self, n):
            for d in (1, 2, 3):
                send(lambda: self.stage.at[n], lambda d=d: self.inbox.at[n, d - 1], self.k + n * 3 + d - 1,
                     xy("xy"[n], d), self.sent)

        def total(self, n):
            v = self.stage[n]
            for d in (1, 2, 3):
                arrived(self.inbox.at[n, d - 1], self.k + n * 3 + d - 1)
            for d in (1, 2, 3):
                v = v + self.inbox[n, d - 1]
            return v

        def spread(self):
            for rel in range(1, 8):
                send(lambda: self.everyone.at[g], lambda: self.everyone.at[g], self.spread_k + rel,
                     spread_group[rel], self.sent)

        def step(self, n):
            v = self.total(n)
            if n == 0:
                self.stage[1] = v
                self.start(1)
            else:
                self.everyone[g] = v
                self.spread()

        def finish(self):
            for rel in range(1, 8):
                arrived(self.everyone.at[gs[8 - rel]], self.spread_k + rel)

    early_sum = Exchange(early, early_in, early_all, att_k)
    late_sum = Exchange(late, late_in, late_all, meta_k)
    spread_group = [{"expert": gs[rel]} for rel in range(8)]

    sub_low = lax.broadcasted_iota(jnp.int32, (128, 1), 0) < 64
    smask0 = jnp.where(sub_low, 1.0, 0.0).astype(F32)
    smask1 = 1.0 - smask0

    def stacked_t(v_t):
        return jnp.concatenate([v_t * smask0, v_t * smask1], axis=1).astype(BF)

    def attend_back(rel, dk_ref, dv_ref, dqkv_ref, dq_ref):
        i = gs[rel % 8]
        q2 = stacked(qs[i])
        q2t = stacked_t(qs[i].astype(F32).T)
        do2 = stacked(dob[i])
        do_t = dob[i].astype(F32).T
        do2t = stacked_t(do_t)
        prod = do_t * att_send[i].astype(F32).T
        delta = jnp.concatenate(
            [jnp.sum(prod[:64], axis=0, keepdims=True), jnp.sum(prod[64:], axis=0, keepdims=True)], axis=1)
        lse_row = lse[i]
        share = jnp.exp(sink_row[...] - lse_row) * delta
        for n in range(2):
            part = jnp.sum(share[:, n * T:n * T + T], axis=1, keepdims=True)
            late[0, pl.ds(2, 1), pl.ds(0, 128)] -= jnp.where(lane == n, part, 0.0)
        dq_ref[...] = jnp.zeros((128, 2 * T), F32)

        def blocks(keys, diagonal):
            probs = [jnp.exp(nn(kk[j], q2t) - lse_row) for j in keys]
            if diagonal:
                probs = [jnp.where(allowed, p, 0.0) for p in probs]
            dq = dq_ref[...]
            for j, p in zip(keys, probs):
                ds = (p * (nn(vv[j], do2t) - delta)).astype(BF)
                dv_ref[j] += nn(p.astype(BF), do2)
                dk_ref[j] += nn(ds, q2)
                dq = dq + nn(kkt[j], ds)
            dq_ref[...] = dq

        def body(j, carry):
            blocks((2 * j, 2 * j + 1), False)
            return carry

        lax.fori_loop(0, lax.div(i, 2), body, 0)

        @pl.when(lax.rem(i, 2) == 1)
        def _():
            blocks((i - 1,), False)

        blocks((i,), True)
        dq = dq_ref[...].T
        dq = jnp.where(low_half, dq[:T], dq[T:]) * 0.125
        cosine, sine = trig(i)
        dqkv_ref[i, 0] = (dq * cosine - swap(dq) * sine).astype(BF)
        give(0, rel, dqkv_ref, dq_sent)

    dq_k = [sem_block(8), sem_block(8)]
    swap_k = sem_block(1)
    dq_sent = []

    def give(part, rel, dqkv_ref, keep):
        i = gs[rel % 8]
        if rel < 8:
            send(lambda: dqkv_ref.at[i, part], lambda: dall.at[part, :, own_tile(g)], dq_k[part] + rel,
                 {"expert": i}, keep)
        else:
            dall[part, :, own_tile(g)] = dqkv_ref[i, part]

    def finish(rel, dk_ref, dv_ref, dqkv_ref, swap_sent):
        r = gs[rel % 8]
        cosine, sine = trig(r)
        dk = dk_ref[r]
        dk = dk + pltpu.roll(dk, 64, 1)
        dv = dv_ref[r]
        dv = dv + pltpu.roll(dv, 64, 1)
        dqkv_ref[r, 1] = jnp.where(low_half, dk * cosine - swap(dk) * sine, dv).astype(BF)
        for n in range(2):
            late[0, pl.ds(1, 1), pl.ds(n * 128, 128)] += jnp.sum(dqkv_ref[r, n].astype(F32), axis=0, keepdims=True)
        send(lambda: dqkv_ref.at[r, 1], lambda: dyg.at[7, :, own_tile(r)], swap_k, sib, swap_sent)
        give(1, rel, dqkv_ref, dq_sent)

    def load_projection():
        return [local_copy(lambda n=n, half=half: w_qkv_in.at[pl.ds(n * T, T), pl.ds(half * D, D)],
                           lambda n=n, half=half: drb.at[n * 2 + half]) for n in range(4) for half in range(2)]

    def order_projection(copies):
        drain(copies)

        def some(i, carry):
            rows = pl.ds(pl.multiple_of(lax.rem(i, 4) * 64, 64), 64)
            at = lax.div(i, 4) * 2 + 1
            v = drb[at, rows, :].astype(F32)
            tiles = [v[:, n * 128:n * 128 + 128] for n in range(8)]
            turned = [pltpu.roll(t, 64, 1) for t in tiles]
            for n in range(4):
                drb[at, rows, pl.ds(n * 256, 128)] = jnp.where(low_half, tiles[n], turned[n + 4]).astype(BF)
                drb[at, rows, pl.ds(n * 256 + 128, 128)] = jnp.where(low_half, turned[n], tiles[n + 4]).astype(BF)
            return carry

        lax.fori_loop(0, 16, some, 0)

    def place_projection():
        for t in range(8):
            v = scatter_w.result(pl.ds(t * 16, 16)).astype(BF)
            for side in range(2):
                for h in range(2):
                    at = side * 512 + h * 256
                    params[h, side * 8 + t, :, pl.ds(0, 256)] = v[:, at:at + 256]
        early[0] = scatter_w.result(pl.ds(128, 16))

    zloc = [(lax.div(zs[d], 2), lax.rem(zs[d], 2)) for d in range(4)]

    def param_piece(h, col, s):
        return gathered.at[h, col, s, pl.ds(0, 32), pl.ds(0, 768)]

    def param_row(h, d):
        hi, lo = zloc[d]
        return gathered.at[h, c * 2 + hi, slot(h, 0, 0), pl.ds(pl.multiple_of(lo * 16, 16), 16), pl.ds(0, 768)]

    param_sent = []

    def own_line(h, e, db):
        return gathered.at[h, c * 2 + e, pl.ds(second[h][db] * 4, 4), pl.ds(0, 32), pl.ds(0, 768)]

    def own_piece(h, e, da):
        return param_piece(h, c * 2 + e, slot(h, da, 0))

    def psem(h, e):
        return wsem(h, 1 + e)

    def forward(piece, recv, dev):
        send(piece, piece, recv, dev, param_sent, ring_w)

    out_k = [sem_block(1) for _ in range(2)]

    def place_out(core, e):
        for h in range(2):
            col = core * 2 + e
            for zl in range(2):
                rows = pl.ds(zl * 16, 16)
                member = (e * 2 + zl) * 2 + core
                for side in range(2):
                    pltpu.make_async_copy(
                        gathered.at[h, col, pl.ds(side * 8, 8), rows, pl.ds(0, 256)],
                        d_wout.at[member, :, :, pl.ds(side * 512 + h * 256, 256)], sems.at[out_k[0]]).start()
                    for part, to in ((0, member * 128), (1, 1024 + core * 512 + (e * 2 + zl) * 128)):
                        pltpu.make_async_copy(
                            gathered.at[h, col, :, rows, pl.ds(256 + side * 256 + part * 128, 128)],
                            d_wqkv.at[:, pl.ds(h * 32 + side * 16, 16), pl.ds(pl.multiple_of(to, 128), 128)],
                            sems.at[out_k[1]]).start()

    def params_gather():
        z_k = wsem(0, 3)
        for h in range(2):
            param_row(h, 0)[...] = params[h, slot(h, 0, 0)]
            forward(lambda h=h: param_row(h, 0), z_k + h * 3, up)
            forward(lambda h=h: param_row(h, 0), z_k + h * 3 + 1, down)
        yield 1
        arrived(param_row(0, 3), z_k + 0)
        forward(lambda: param_row(0, 3), z_k + 2, up)
        arrived(param_row(1, 1), z_k + 4)
        forward(lambda: param_row(1, 1), z_k + 5, down)
        arrived(param_row(0, 1), z_k + 1)
        arrived(param_row(1, 3), z_k + 3)
        yield 2
        arrived(param_row(0, 2), z_k + 2)
        arrived(param_row(1, 2), z_k + 5)
        for e in range(2):
            for h in range(2):
                for n, d in ((0, 1), (1, 3)):
                    forward(lambda h=h, e=e: own_piece(h, e, 0), psem(h, e) + n, xy(axis_of(h, 0), d))
        yield 3
        for e in range(2):
            for h in range(2):
                k = psem(h, e)
                arrived(own_piece(h, e, 3), k)
                if e == 0:
                    forward(lambda h=h, e=e: own_piece(h, e, 3), k + 2, xy(axis_of(h, 0), 1))
                arrived(own_piece(h, e, 1), k + 1)
                if e == 1:
                    forward(lambda h=h, e=e: own_piece(h, e, 1), k + 2, xy(axis_of(h, 0), 3))
        for e in range(2):
            for h in range(2):
                k = psem(h, e)
                arrived(own_piece(h, e, 2), k + 2)
                for n, d in ((3, 1), (4, 3)):
                    forward(lambda h=h, e=e: own_line(h, e, 0), k + n, xy(axis_of(h, 1), d))
        for e in range(2):
            for h in range(2):
                forward(lambda h=h, e=e: own_line(h, e, 0), sib_k(h, e), sib)
        yield 4
        for e in range(2):
            for h in range(2):
                k = psem(h, e)
                arrived(own_line(h, e, 3), k + 3)
                if e == 0:
                    forward(lambda h=h, e=e: own_line(h, e, 3), k + 5, xy(axis_of(h, 1), 1))
                arrived(own_line(h, e, 1), k + 4)
                if e == 1:
                    forward(lambda h=h, e=e: own_line(h, e, 1), k + 5, xy(axis_of(h, 1), 3))
                for db in (3, 1):
                    forward(lambda h=h, e=e, db=db: own_line(h, e, db), sib_k(h, e), sib)
        yield 5
        for e in range(2):
            for h in range(2):
                arrived(own_line(h, e, 2), psem(h, e) + 5)
                forward(lambda h=h, e=e: own_line(h, e, 2), sib_k(h, e), sib)
            place_out(c, e)
        yield 6
        for e in range(2):
            for h in range(2):
                arrived(gathered.at[h, other * 2 + e, :, pl.ds(0, 32), pl.ds(0, 768)], sib_k(h, e))
            place_out(other, e)
        yield 7

    def sib_k(h, e):
        return wsem(1, 3) + h * 2 + e

    param_scatters = [scatter_xy(ParamPieces(h), h == 0, False, param_sent) for h in range(2)]

    def psvc():
        for h in range(2):
            next(param_scatters[h], None)

    def backward(dk_ref, dv_ref, dqkv_ref, dq_ref):
        dk_ref[...] = jnp.zeros((8, T, 128), F32)
        dv_ref[...] = jnp.zeros((8, T, 128), F32)
        swap_sent = []
        plan = {7: (1, 0), 6: (2,), 5: (1, 0), 4: (3, 2), 3: (3,), 2: (2,)}
        for i in range(7, -1, -1):
            attend_back(8 - i, dk_ref, dv_ref, dqkv_ref, dq_ref)
            if i == 7:
                scatter_w.step1()
            if i in plan:
                wsvc(*plan[i])
            if i == 5:
                scatter_w.step2()
            if i == 4:
                scatter_w.step3()
                place_projection()
                early_sum.start(0)
                drain(scatter_w.sent)
                copies = load_projection()
            if i == 3:
                early_sum.step(0)
                order_projection(copies)
            if i == 1:
                early_sum.step(1)
        for rel in range(1, 9):
            finish(rel, dk_ref, dv_ref, dqkv_ref, swap_sent)
        drain(att_sent)
        wsvc(3)
        drain(pending)
        drain(out_copies)
        for dev in (sib, up, down, xy("x", 1), xy("x", 3), xy("y", 1), xy("y", 3)):
            pl.semaphore_signal(free_xy, inc=1, device_id=dev, device_id_type=MESH)

        dk_ref[...] = jnp.zeros((8, T, 128), F32)
        arrived(dyg.at[7], swap_k)
        drain(swap_sent)

        def dw_part(r, carry):
            both = dyg[7, :, own_tile(r)].astype(F32)
            own = dqkv_ref[r, 1].astype(F32)
            mixed = jnp.where(low_half == even, own, pltpu.roll(both, 64, 1)).astype(BF)
            h1 = h1_rows(r, pl.ds(0, T))
            v = jnp.concatenate([tn(dqkv_ref[r, 0], h1), tn(mixed, h1)], axis=0)
            for n in range(8):
                dk_ref[n] += v[:, n * 128:n * 128 + 128]
            return carry

        lax.fori_loop(0, 8, dw_part, 0)
        for n in range(8):
            dw = dk_ref[n].T
            for s in range(2):
                for h in range(2):
                    rows = dw[s * 64 + h * 32:s * 64 + h * 32 + 32]
                    params[h, n * 2 + s, :, pl.ds(256, 512)] = jnp.concatenate([rows[:16], rows[16:]], axis=1).astype(BF)
        pl.semaphore_wait(free_xy, 7)
        psvc()
        scatter_m.step1()
        for part in range(2):
            for rel in range(1, 8):
                arrived(dall.at[part, :, own_tile(gs[8 - rel])], dq_k[part] + rel)
        drain(dq_sent)
        for n in range(4):
            part = nt(dall[0], drb[2 * n]) + nt(dall[1], drb[2 * n + 1])
            dv_ref[2 * n] = part[:, :128]
            dv_ref[2 * n + 1] = part[:, 128:]
        psvc()
        scatter_m.step2()

        def tokens_back(i, carry):
            rows = pl.ds(pl.multiple_of(i * 64, 64), 64)
            xf = xg[g, rows, :].astype(F32)
            inv = lax.rsqrt(jnp.mean(xf * xf, axis=-1, keepdims=True) + EPS)
            d_h1 = jnp.concatenate([dv_ref[n, rows, :] for n in range(8)], axis=1)
            v1 = d_h1 * attn_gain[...]
            inner = jnp.mean(v1 * xf, axis=-1, keepdims=True)
            h2own[rows, :] = (d_middle[rows, :] + inv * v1 - xf * (inv * inv * inv * inner)).astype(BF)
            return carry + jnp.sum(d_h1 * xf * inv, axis=0, keepdims=True)

        psvc()
        late[0, pl.ds(0, 1), :] = lax.fori_loop(0, 4, tokens_back, zero_row)
        late_sum.start(0)
        cp3 = local_copy(h2own, d_tokens)
        psvc()
        psvc()
        gather_p = params_gather()
        next(gather_p)
        late_sum.step(0)
        next(gather_p)
        next(gather_p)
        early_sum.finish()
        late_sum.step(1)
        next(gather_p)
        next(gather_p)
        scatter_m.step3()

        def result(i, carry):
            rows = pl.ds(pl.multiple_of(i * 64, 64), 64)
            att[rows, :] = (middle[rows, :] + scatter_m.result(rows)).astype(BF)
            return carry

        lax.fori_loop(0, 4, result, 0)
        cp2 = local_copy(att, block_out)
        late_sum.finish()
        for r in range(8):
            final[pl.ds(0, 1), :] += late_all[r, pl.ds(0, 1), :]
            final[pl.ds(3, 1), pl.ds(r * 128, 128)] = late_all[r, pl.ds(1, 1), pl.ds(0, 128)]
            two = late_all[r, pl.ds(2, 1), pl.ds(0, 128)]
            two = pltpu.roll(two, 2 * r, 1) if r else two
            final[pl.ds(5, 1), pl.ds(0, 128)] += jnp.where((lane >= 2 * r) & (lane < 2 * r + 2), two, 0.0)
        for n in range(4):
            a = late_all[2 * n, pl.ds(1, 1), pl.ds(128, 128)]
            b = late_all[2 * n + 1, pl.ds(1, 1), pl.ds(128, 128)]
            final[pl.ds(4, 1), pl.ds(n * 128, 128)] = jnp.where(low_half, a, pltpu.roll(b, 64, 1))
            final[pl.ds(4, 1), pl.ds(512 + n * 128, 128)] = jnp.where(low_half, pltpu.roll(a, 64, 1), b)
        final[pl.ds(1, 2), :] = early_all[0, pl.ds(12, 2), :]
        cp4 = local_copy(early_all, early_out)
        cp5 = local_copy(final, final_out)
        for _ in gather_p:
            pass
        drain(scatter_m.sent)
        drain([cp2, cp3, cp4, cp5])
        pltpu.make_async_copy(d_wout, d_wout, sems.at[out_k[0]]).wait()
        pltpu.make_async_copy(d_wqkv, d_wqkv, sems.at[out_k[1]]).wait()

    pl.run_scoped(
        backward, pltpu.VMEM((8, T, 128), F32), pltpu.VMEM((8, T, 128), F32), pltpu.VMEM((8, 2, T, 128), BF),
        pltpu.VMEM((128, 2 * T), F32))
    drain(param_sent)
    drain(early_sum.sent)
    drain(late_sum.sent)


ANY = pl.BlockSpec(memory_space=pl.ANY)
VM = pl.BlockSpec(memory_space=pltpu.VMEM)


def angle_tables():
    frequency = np.exp(np.arange(32, dtype=np.float32) * np.float32(-2.0 * np.log(THETA) / 64)).astype(np.float64)
    freq = np.tile(frequency, 4)[None, :]
    near = np.arange(T, dtype=np.float64)[:, None] * freq
    far = np.arange(8, dtype=np.float64)[:, None] * T * freq
    return [f(a).astype(np.float32) for a in (near, far) for f in (np.cos, np.sin)]


def per_device(
    tokens, cotangent, routes, slot_ids, attn_gain, w_qkv, b_qkv, w_out, b_out, sink_logits, moe_gain,
    w_router, b_router, gu_weight, gu_bias, down_weight, down_bias,
):
    g = lax.axis_index("expert")
    both = jnp.concatenate([gu_weight.transpose(0, 2, 1, 3), down_weight[:, None]], axis=1)
    shard = both.reshape(4, 3, 2, 16, D).transpose(2, 0, 1, 3, 4).reshape(2, 4, 48, D)
    target = jnp.pad((routes * 64 + slot_ids).T, ((0, 4), (0, 0)))

    def padded(v):
        return jnp.pad(v.reshape(8, 4, -1), ((0, 0), (0, 4), (0, 0))).reshape(64, -1)

    w_rt = padded(w_router.T)
    b_rt = jnp.broadcast_to(padded(b_router), (64, T))
    gub = gu_bias.reshape(4, 2, 4, 4, 2, 16)
    gub = jnp.concatenate([gub[:, :, :, :, 0].reshape(4, 2, 256), gub[:, :, :, :, 1].transpose(0, 1, 3, 2, 4).reshape(4, 2, 256)], axis=2)
    down_own = lax.dynamic_slice_in_dim(down_bias, g * 4, 4, 0)
    cos_a, sin_a, cos_b, sin_b = [jnp.asarray(t) for t in angle_tables()]
    shape = jax.ShapeDtypeStruct
    out = pl.pallas_call(
        layer_kernel,
        out_shape=(
            shape((T, D), BF), shape((T, D), BF), shape((4, 32, D), BF), shape((4, 32, D), BF), shape((4, 32, D), BF),
            shape((16, 64, 2048), BF), shape((8, 8, 16, D), BF), shape((8, 16, D), F32), shape((8, D), F32),
        ),
        in_specs=[ANY] * 4 + [VM] * 15,
        out_specs=[ANY] * 9,
        scratch_shapes=[
            pltpu.VMEM((8, T, D), BF), pltpu.VMEM((8, T, D), BF), pltpu.VMEM((8, T, D), BF),
            pltpu.VMEM((2, 4, 16, 48, D), BF),
            pltpu.VMEM((8, T, 128), BF), pltpu.VMEM((8, T, 128), BF), pltpu.VMEM((8, T, 128), BF),
            pltpu.VMEM((8, 128, T), BF), pltpu.VMEM((8, 128, T), BF),
            pltpu.VMEM((8, 1, 2 * T), F32), pltpu.VMEM((8, T, 128), BF), pltpu.VMEM((T, D), BF),
            pltpu.VMEM((T, D), F32), pltpu.VMEM((T, D), BF),
            pltpu.VMEM((8, 16, T), F32), pltpu.VMEM((8, 16, T), F32),
            pltpu.VMEM((8, T, D), BF), pltpu.VMEM((8, T, D), BF),
            pltpu.VMEM((4, T, D), BF), pltpu.VMEM((2, 128, D), BF), pltpu.VMEM((2, T, D), BF),
            pltpu.VMEM((4, 2, 2, 2, 48, D), BF), pltpu.VMEM((2, 2, 2, 4, 48, D), BF),
            pltpu.VMEM((4, 2, 48, D), BF), pltpu.VMEM((4, 2, 2, 48, D), BF),
            pltpu.VMEM((8, T, 128), BF), pltpu.VMEM((8, 8, T), F32), pltpu.VMEM((8, 8, T), F32),
            pltpu.VMEM((T, D), F32),
            pltpu.VMEM((64, T), F32), pltpu.VMEM((2, 16, 16, 768), BF),
            pltpu.VMEM((16, D), F32), pltpu.VMEM((8, D), F32),
            pltpu.VMEM((2, 16, D), F32), pltpu.VMEM((2, 3, 16, D), F32), pltpu.VMEM((8, 16, D), F32),
            pltpu.VMEM((2, 8, D), F32), pltpu.VMEM((2, 3, 8, D), F32), pltpu.VMEM((8, 8, D), F32),
            pltpu.VMEM((D, 256), BF), pltpu.VMEM((1, 256), F32), pltpu.VMEM((1, 512), F32), pltpu.VMEM((8, D), F32),
            pltpu.VMEM((2, T, D), BF),
            pltpu.SemaphoreType.DMA((NSEM,)), pltpu.SemaphoreType.REGULAR((2, 2)),
            pltpu.SemaphoreType.REGULAR, pltpu.SemaphoreType.REGULAR((4,)),
        ],
        compiler_params=pltpu.CompilerParams(collective_id=1, has_side_effects=True, vmem_limit_bytes=VLIM),
    )(tokens, cotangent, shard, w_qkv, target, attn_gain[None], b_qkv[None], w_out, b_out[None],
      jnp.pad(sink_logits, (0, 112))[None], moe_gain[None], w_rt, b_rt, gub, down_own, cos_a, sin_a, cos_b, sin_b)
    block_out, d_tokens, d_gate_w, d_up_w, d_down_w, d_wqkv, d_wout, early, final = out
    d_wr = early[:, :4].reshape(32, D).T
    d_br = early[0, 14, :64].reshape(8, 8)[:, :4].reshape(32)
    d_gub = lax.dynamic_index_in_dim(early, g, 0, keepdims=False)[8:12].reshape(4, 2, 2, 16, 16)
    dp = lax.axis_index("dp")
    turned = (dp % 4) * 4 + dp // 4
    d_gub = jnp.concatenate([lax.dynamic_index_in_dim(d_gub[:, :, 0], dp, 2, keepdims=False),
                             lax.dynamic_index_in_dim(d_gub[:, :, 1], turned, 2, keepdims=False)], axis=-1)
    return (
        block_out, d_tokens, final[0], d_wqkv.reshape(D, 2048).astype(F32), final[3:5].reshape(2048),
        d_wout.reshape(D, D).astype(F32), final[1], final[5, :16], final[2], d_wr, d_br,
        jnp.stack([d_gate_w, d_up_w], axis=2).astype(F32), d_gub, d_down_w.astype(F32), early[:, 4:8].reshape(32, D),
    )


def solution(mesh):
    rows = P(("dp", "expert"), None)
    in_specs = (rows,) * 4 + (P(),) * 9 + (
        P("expert", "dp", None, None), P("expert", None, None), P("expert", "dp", None), P())
    out_specs = (rows,) * 2 + (P(),) * 9 + (
        P("expert", "dp", None, None), P("expert", None, "dp"), P("expert", "dp", None), P())
    return jax.shard_map(per_device, mesh=mesh, in_specs=in_specs, out_specs=out_specs, check_vma=False)
```

```python
import functools

import jax
import jax.numpy as jnp
import numpy as np
from jax import lax
from jax.experimental import pallas as pl
from jax.experimental.pallas import tpu as pltpu
from jax.sharding import PartitionSpec as P

MESH = pl.DeviceIdType.MESH
BF = jnp.bfloat16
F32 = jnp.float32
EPS = 1e-05
THETA = 10000.0
LIMIT = 7.0
ALPHA = 1.702
NEG = -1000000000.0
NSEM = 380
VLIM = (64 << 20) - (1 << 16)
T = 256
D = 1024


def nt(a, b):
    return lax.dot_general(a, b, (((1,), (1,)), ((), ())), preferred_element_type=F32)


def tn(a, b):
    return lax.dot_general(a, b, (((0,), (0,)), ((), ())), preferred_element_type=F32)


def nn(a, b):
    return jnp.dot(a, b, preferred_element_type=F32)


def split_low(v):
    high = v.astype(BF)
    return high, (v - high.astype(F32)).astype(BF)


def layer_kernel(
    x_in, dy_in, w_in, w_qkv_in, target, attn_gain, b_qkv_in, w_out, b_out, sinks, moe_gain,
    w_rt, b_rt, gu_bias, down_bias, cos_a, sin_a, cos_b, sin_b,
    block_out, d_tokens, d_gate_w, d_up_w, d_down_w, d_wqkv, d_wout, early_out, final_out,
    xg, dyg, h2g, gathered, qs, kk, vv, kkt, vvt, lse, att_send, att, middle, h2own, metag, meta_send,
    outb, drb, sib_in, half_in, full_in, rs_half, rs_full, rs2_half, rs2_full, dob, dgt_send, dgt_in,
    d_middle, gates_ref, params, own_rows, common_rows, early, early_in, early_all, late, late_in, late_all,
    w_qkv, b_qkv, sink_row, final, dall, sems, credit, free_xy, passed,
):
    dp = lax.axis_index("dp")
    g = lax.axis_index("expert")
    y, x = lax.div(dp, 4), lax.rem(dp, 4)
    z, c = lax.div(g, 2), lax.rem(g, 2)
    xs = [lax.rem(x + d, 4) for d in range(4)]
    ys = [lax.rem(y + d, 4) for d in range(4)]
    zs = [lax.rem(z + d, 4) for d in range(4)]
    gs = [lax.rem(g + d, 8) for d in range(8)]
    other = 1 - c
    sib = {"expert": z * 2 + (1 - c)}
    up = {"expert": zs[1] * 2 + c}
    down = {"expert": zs[3] * 2 + c}

    neighbours = {
        "x": [{"dp": y * 4 + xs[d]} for d in range(4)],
        "y": [{"dp": ys[d] * 4 + x} for d in range(4)],
    }

    def xy(axis, d):
        return neighbours[axis][d]

    first = [xs, ys]
    second = [ys, xs]

    lines = [[second[h][db] * 4 for db in range(4)] for h in range(2)]

    def slot(h, da, db):
        return second[h][db] * 4 + first[h][da]

    counter = [0]

    def sem():
        counter[0] += 1
        assert counter[0] <= NSEM
        return counter[0] - 1

    def sem_block(n):
        first = counter[0]
        counter[0] += n
        assert counter[0] <= NSEM
        return first

    def view(ref):
        return ref() if callable(ref) else ref

    class Ring:
        def __init__(self, n):
            self.base, self.n, self.at, self.live = sem_block(n), n, 0, {}

        def take(self, copy):
            k = self.base + self.at % self.n
            self.at += 1
            if k in self.live:
                self.live[k].wait()
            self.live[k] = copy
            return k

    class Remote:
        def __init__(self, src, dst, recv, dev, ring):
            self.src, self.dst, self.recv, self.dev, self.done = src, dst, recv, dev, False
            self.n = ring.take(self)
            self.make().start()

        def make(self):
            return pltpu.make_async_remote_copy(
                src_ref=view(self.src), dst_ref=view(self.dst), send_sem=sems.at[self.n], recv_sem=sems.at[self.recv],
                device_id=self.dev, device_id_type=MESH)

        def wait(self):
            if not self.done:
                self.make().wait_send()
                self.done = True

    class Local(Remote):
        def __init__(self, src, dst, ring):
            self.src, self.dst, self.done = src, dst, False
            self.n = ring.take(self)
            self.make().start()

        def make(self):
            return pltpu.make_async_copy(view(self.src), view(self.dst), sems.at[self.n])

        def wait(self):
            if not self.done:
                self.make().wait()
                self.done = True

    ring_w, ring_z, ring_l = Ring(100), Ring(80), Ring(40)
    pending = []
    pending_weights = [[] for _ in range(4)]

    def send(src, dst, recv, dev, keep, ring=ring_z):
        keep.append(Remote(src, dst, recv, dev, ring))

    def local_copy(src, dst):
        return Local(src, dst, ring_l)

    def arrived(dst, recv):
        pltpu.make_async_remote_copy(
            src_ref=dst, dst_ref=dst, send_sem=sems.at[recv], recv_sem=sems.at[recv],
            device_id=sib, device_id_type=MESH,
        ).wait_recv()

    def drain(copies):
        for copy in copies:
            copy.wait()
        copies.clear()

    barrier = pltpu.get_barrier_semaphore()
    for rel in range(1, 8):
        pl.semaphore_signal(barrier, inc=1, device_id={"expert": gs[rel]}, device_id_type=MESH)
    for axis in ("x", "y"):
        for d in (1, 2, 3):
            pl.semaphore_signal(barrier, inc=1, device_id=xy(axis, d), device_id_type=MESH)
    pl.semaphore_wait(barrier, 13)

    class GatherZ:
        def __init__(self, buf, own):
            self.buf, self.own = buf, own
            self.k = sem_block(9)
            self.sent = []
            self.m1, self.p1, self.far = zs[3] * 2 + c, zs[1] * 2 + c, zs[2] * 2 + c
            s = 1 - c
            self.sm1, self.sp1, self.sfar, self.so = (
                zs[3] * 2 + s, zs[1] * 2 + s, zs[2] * 2 + s, z * 2 + s)

        def start(self):
            b, k = self.buf, self.k
            send(self.own, lambda: b.at[g], k + 1, up, self.sent)
            send(self.own, lambda: b.at[g], k + 2, down, self.sent)
            send(self.own, lambda: b.at[g], k + 0, sib, self.sent)

        def step_m1(self):
            b, k, s = self.buf, self.k, self.m1
            arrived(b.at[s], k + 1)
            send(lambda: b.at[s, pl.ds(0, 128)], lambda: b.at[s, pl.ds(0, 128)], k + 3, up, self.sent)
            send(lambda: b.at[s], lambda: b.at[s], k + 4, sib, self.sent)

        def step_p1(self):
            b, k, s = self.buf, self.k, self.p1
            arrived(b.at[s], k + 2)
            send(lambda: b.at[s, pl.ds(128, 128)], lambda: b.at[s, pl.ds(128, 128)], k + 5, down, self.sent)
            send(lambda: b.at[s], lambda: b.at[s], k + 6, sib, self.sent)

        def step_far(self):
            b, k, s = self.buf, self.k, self.far
            for i, kr, ks in ((0, 3, 7), (128, 5, 8)):
                arrived(b.at[s, pl.ds(i, 128)], k + kr)
                send(lambda i=i: b.at[s, pl.ds(i, 128)], lambda i=i: b.at[s, pl.ds(i, 128)], k + ks, sib, self.sent)

        def wait_sib_own(self):
            arrived(self.buf.at[self.so], self.k)

        def wait_sib_m1(self):
            arrived(self.buf.at[self.sm1], self.k + 4)

        def wait_sib_p1(self):
            arrived(self.buf.at[self.sp1], self.k + 6)

        def wait_sib_far(self):
            for i, ks in ((0, 7), (128, 8)):
                arrived(self.buf.at[self.sfar, pl.ds(i, 128)], self.k + ks)

    class ScatterZ:
        def __init__(self, k, buf, sib_ref, half_ref, full_ref, sizes=(128, 128)):
            self.buf, self.r, self.h, self.f = buf, sib_ref, half_ref, full_ref
            self.sizes, self.rows = sizes, sum(sizes)
            self.mine = [zs[d] * 2 + c for d in range(4)]
            self.k = k
            self.sent = []

        def chunks(self):
            return [zs[d] * 2 + (1 - c) for d in (2, 1, 3, 0)], [zs[d] * 2 + c for d in (2, 1, 3, 0)]

        def to_sibling(self, n):
            d = (2, 1, 3, 0)[n]
            zz = zs[d]
            send(lambda: self.buf.at[zz * 2 + (1 - c), pl.ds(0, self.rows)], lambda: self.r(d), self.k + n, sib, self.sent)

        def add(self, chunk, refs, base=0, rows=None):
            rows = rows or self.rows
            step = 64 if rows % 64 == 0 else 16

            def body(i, carry):
                at = pl.ds(pl.multiple_of(base + i * step, 16), step)
                ref_at = pl.ds(pl.multiple_of(i * step, 16), step)
                v = self.buf[chunk, at, :].astype(F32)
                for ref in refs:
                    v = v + ref[ref_at, :].astype(F32)
                self.buf[chunk, at, :] = v.astype(BF)
                return carry
            lax.fori_loop(0, rows // step, body, 0)

        def step1(self):
            b, k = self.buf, self.k
            chunk = self.mine[2]
            arrived(self.r(2), k + 0)
            self.add(chunk, [self.r(2)])
            lo, hi = self.sizes
            send(lambda: b.at[chunk, pl.ds(0, lo)], lambda: self.h(0), k + 4, up, self.sent)
            send(lambda: b.at[chunk, pl.ds(lo, hi)], lambda: self.h(1), k + 5, down, self.sent)

        def step2(self):
            b, k = self.buf, self.k
            for d, n, hi, dev in ((1, 1, 0, up), (3, 2, 1, down)):
                chunk = self.mine[d]
                arrived(self.r(d), k + n)
                self.add(chunk, [self.r(d)])
                arrived(self.h(hi), k + 4 + hi)
                self.add(chunk, [self.h(hi)], hi * self.sizes[0], self.sizes[hi])
                send(lambda chunk=chunk: b.at[chunk, pl.ds(0, self.rows)], lambda hi=hi: self.f(hi), k + 6 + hi, dev, self.sent)

        def step3(self):
            arrived(self.r(0), self.k + 3)
            arrived(self.f(0), self.k + 6)
            arrived(self.f(1), self.k + 7)

        def result(self, rows):
            return (self.buf[g, rows, :].astype(F32) + self.r(0)[rows, :].astype(F32)
                    + self.f(0)[rows, :].astype(F32) + self.f(1)[rows, :].astype(F32))

    around = [xy("x", 1), xy("x", 3), xy("y", 1), xy("y", 3)]

    def axis_of(h, ax):
        return "x" if (ax == 0) == (h == 0) else "y"

    gk = sem_block(2 * 4 * 7)

    def wsem(h, e):
        return gk + (h * 4 + e) * 7

    def row_of(h, e, db):
        return gathered.at[h, e, pl.ds(second[h][db] * 4, 4)]

    def one_of(h, e, da):
        return gathered.at[h, e, slot(h, da, 0)]

    local_w = {}

    def weights_start():
        for e in range(4):
            for h in range(2):
                for n, d in ((0, 1), (1, 3)):
                    send(lambda h=h, e=e: w_in.at[h, e], lambda h=h, e=e: one_of(h, e, 0), wsem(h, e) + n,
                         xy(axis_of(h, 0), d), pending_weights[e], ring_w)
                local_w[h, e] = local_copy(lambda h=h, e=e: w_in.at[h, e], lambda h=h, e=e: one_of(h, e, 0))

    def weights_near(e):
        for h in range(2):
            k = wsem(h, e)
            arrived(one_of(h, e, 3), k)
            if e % 2 == 0:
                send(lambda h=h: one_of(h, e, 3), lambda h=h: one_of(h, e, 3), k + 2, xy(axis_of(h, 0), 1),
                     pending_weights[e], ring_w)
            arrived(one_of(h, e, 1), k + 1)
            if e % 2 == 1:
                send(lambda h=h: one_of(h, e, 1), lambda h=h: one_of(h, e, 1), k + 2, xy(axis_of(h, 0), 3),
                     pending_weights[e], ring_w)

    def weights_turn(e):
        for h in range(2):
            k = wsem(h, e)
            arrived(one_of(h, e, 2), k + 2)
            local_w[h, e].wait()
            for n, d in ((3, 1), (4, 3)):
                send(lambda h=h: row_of(h, e, 0), lambda h=h: row_of(h, e, 0), k + n, xy(axis_of(h, 1), d),
                     pending_weights[e], ring_w)

    def weights_row(e):
        for h in range(2):
            k = wsem(h, e)
            arrived(row_of(h, e, 3), k + 3)
            if e % 2 == 0:
                send(lambda h=h: row_of(h, e, 3), lambda h=h: row_of(h, e, 3), k + 5, xy(axis_of(h, 1), 1),
                     pending_weights[e], ring_w)
            arrived(row_of(h, e, 1), k + 4)
            if e % 2 == 1:
                send(lambda h=h: row_of(h, e, 1), lambda h=h: row_of(h, e, 1), k + 5, xy(axis_of(h, 1), 3),
                     pending_weights[e], ring_w)

    def weights_end(e):
        for h in range(2):
            arrived(row_of(h, e, 2), wsem(h, e) + 5)
        for dev in around:
            pl.semaphore_signal(passed.at[e], inc=1, device_id=dev, device_id_type=MESH)

    def weights_steps():
        order = [(weights_near, 0), (weights_near, 1), (weights_turn, 0), (weights_near, 2), (weights_turn, 1),
                 (weights_near, 3), (weights_turn, 2), (weights_turn, 3), (weights_row, 0), (weights_row, 1),
                 (weights_row, 2), (weights_row, 3), (weights_end, 0), (weights_end, 1), (weights_end, 2),
                 (weights_end, 3)]
        for step, e in order:
            step(e)
            yield (step, e)

    late[0] = jnp.zeros((8, D), F32)
    final[...] = jnp.zeros((8, D), F32)
    own_rows[...] = jnp.zeros((16, D), F32)
    common_rows[...] = jnp.zeros((8, D), F32)
    local_x = local_copy(x_in, lambda: xg.at[g])
    gather_x = GatherZ(xg, x_in)
    gather_x.start()
    weights_start()
    local_q = [
        local_copy(lambda: w_qkv_in.at[:, pl.ds(pl.multiple_of(g * 128, 128), 128)], lambda: w_qkv.at[:, pl.ds(0, 128)]),
        local_copy(lambda: w_qkv_in.at[:, pl.ds(pl.multiple_of(1024 + z * 128, 128), 128)], lambda: w_qkv.at[:, pl.ds(128, 128)]),
    ] + [
        local_copy(lambda n=n: w_qkv_in.at[pl.ds(n * T, T), pl.ds(pl.multiple_of(1536 + z * 128, 128), 128)],
                   lambda n=n: outb.at[n, :, pl.ds(0, 128)])
        for n in range(4)
    ]
    weights = weights_steps()

    def svc(n=1):
        for _ in range(n):
            if next(weights, None) is None:
                return

    lane = lax.broadcasted_iota(jnp.int32, (1, 128), 1)
    low_half = lane < 64
    first_quarter = (lane % 64) < 32
    mask0 = jnp.where(low_half, 1.0, 0.0).astype(F32)
    mask1 = 1.0 - mask0

    def swap(v):
        return jnp.where(first_quarter, pltpu.roll(v, 96, 1), pltpu.roll(v, 32, 1))

    def trig(r):
        cb, sb = cos_b[pl.ds(r, 1), :], sin_b[pl.ds(r, 1), :]
        ca, sa = cos_a[...], sin_a[...]
        cosine = ca * cb - sa * sb
        sine = sa * cb + ca * sb
        return cosine, jnp.where(first_quarter, -sine, sine)

    def h1_rows(r, rows):
        xf = xg[r, rows, :].astype(F32)
        inv = lax.rsqrt(jnp.mean(xf * xf, axis=-1, keepdims=True) + EPS)
        return (xf * inv * attn_gain[...]).astype(BF)

    def qkv_chunk(r):
        h1 = h1_rows(r, pl.ds(0, T))
        mixed = nn(h1, w_qkv[...]) + b_qkv[...]
        cosine, sine = trig(r)
        q = mixed[:, :128]
        kv = mixed[:, 128:]
        q = (q * cosine + swap(q) * sine) * 0.125
        kv = jnp.where(low_half, kv * cosine + swap(kv) * sine, kv)
        other = pltpu.roll(kv, 64, 1)
        kd = jnp.where(low_half, kv, other)
        vd = jnp.where(low_half, other, kv)
        qs[r] = q.astype(BF)
        kk[r] = kd.astype(BF)
        vv[r] = vd.astype(BF)
        kkt[r] = kd.T.astype(BF)
        vvt[r] = vd.T.astype(BF)

    even = c == 0

    def pair(first, second):
        k_own = jnp.where(even, first, pltpu.roll(first, 64, 1))
        v_own = jnp.where(even, pltpu.roll(second, 64, 1), second)
        return jnp.where(low_half, k_own, v_own)

    for copy in local_q:
        copy.wait()

    def pair_rows(i, carry):
        rows = pl.ds(pl.multiple_of(i * 256, 256), 256)
        w_qkv[rows, pl.ds(128, 128)] = pair(
            w_qkv[rows, pl.ds(128, 128)].astype(F32), outb[i, :, pl.ds(0, 128)].astype(F32)).astype(BF)
        return carry

    lax.fori_loop(0, 4, pair_rows, 0)
    b_qkv[:, pl.ds(0, 128)] = b_qkv_in[:, pl.ds(pl.multiple_of(g * 128, 128), 128)]
    b_qkv[:, pl.ds(128, 128)] = pair(
        b_qkv_in[:, pl.ds(pl.multiple_of(1024 + z * 128, 128), 128)],
        b_qkv_in[:, pl.ds(pl.multiple_of(1536 + z * 128, 128), 128)])
    lane_all = lax.broadcasted_iota(jnp.int32, (1, 16), 1)
    for n in range(2):
        one = jnp.sum(jnp.where(lane_all == g * 2 + n, sinks[...], 0.0), axis=1, keepdims=True)
        sink_row[:, pl.ds(n * T, T)] = jnp.broadcast_to(one, (1, T))

    gx = gather_x
    local_x.wait()
    qkv_chunk(g)
    gx.wait_sib_own()
    qkv_chunk(gx.so)
    svc(1)
    gx.step_m1()
    gx.step_p1()
    qkv_chunk(gx.m1)
    svc(1)
    qkv_chunk(gx.p1)
    svc(1)
    gx.wait_sib_m1()
    qkv_chunk(gx.sm1)
    svc(1)
    gx.wait_sib_p1()
    qkv_chunk(gx.sp1)
    svc(1)
    gx.step_far()
    local_dy = local_copy(dy_in, lambda: dyg.at[g])
    gather_dy = GatherZ(dyg, dy_in)
    gather_dy.start()
    qkv_chunk(gx.far)
    svc(1)
    gx.wait_sib_far()
    qkv_chunk(gx.sfar)
    svc(2)

    def stacked(v):
        vf = v.astype(F32)
        return jnp.concatenate([vf * mask0, vf * mask1], axis=0).astype(BF)

    key_at = lax.broadcasted_iota(jnp.int32, (T, 2 * T), 0)
    query_at = lax.broadcasted_iota(jnp.int32, (T, 2 * T), 1) % T
    allowed = key_at <= query_at

    att_k = sem_block(8)

    def own_tile(n):
        return pl.ds(pl.multiple_of(n * 128, 128), 128)

    def attend(rel, m_ref, l_ref, acc_ref):
        i = gs[rel % 8]
        q2 = stacked(qs[i])
        m_ref[...] = sink_row[...]
        l_ref[...] = jnp.ones((1, 2 * T), F32)
        acc_ref[...] = jnp.zeros((128, 2 * T), F32)

        def blocks(keys, diagonal):
            scores = [nt(kk[j], q2) for j in keys]
            if diagonal:
                scores = [jnp.where(allowed, s, NEG) for s in scores]
            m_old = m_ref[...]
            m_new = m_old
            for s in scores:
                m_new = jnp.maximum(m_new, jnp.max(s, axis=0, keepdims=True))
            alpha = jnp.exp(m_old - m_new)
            total = l_ref[...] * alpha
            acc = acc_ref[...] * alpha
            for j, s in zip(keys, scores):
                p = jnp.exp(s - m_new)
                total = total + jnp.sum(p, axis=0, keepdims=True)
                acc = acc + nn(vvt[j], p.astype(BF))
            l_ref[...] = total
            acc_ref[...] = acc
            m_ref[...] = m_new

        def body(j, carry):
            blocks((2 * j, 2 * j + 1), False)
            return carry

        lax.fori_loop(0, lax.div(i, 2), body, 0)

        @pl.when(lax.rem(i, 2) == 1)
        def _():
            blocks((i - 1,), False)

        blocks((i,), True)
        total = l_ref[...]
        lse[i] = m_ref[...] + jnp.log(total)
        o = (acc_ref[...] / total).T
        att_send[i] = jnp.where(low_half, o[:T], o[T:]).astype(BF)

        if rel < 8:
            send(lambda: att_send.at[i], lambda: att.at[:, own_tile(g)], att_k + rel, {"expert": i}, att_fwd)
        else:
            att[:, own_tile(g)] = att_send[i]

    att_fwd = []

    def forward_attention(m_ref, l_ref, acc_ref):
        gd = gather_dy
        for i in range(8):
            attend(i + 1, m_ref, l_ref, acc_ref)
            if i == 6:
                gd.step_m1()
                gd.step_p1()
            if i in (3, 6):
                svc(1)

    pl.run_scoped(
        forward_attention, pltpu.VMEM((1, 2 * T), F32), pltpu.VMEM((1, 2 * T), F32), pltpu.VMEM((128, 2 * T), F32))

    for rel in range(1, 8):
        arrived(att.at[:, own_tile(gs[8 - rel])], att_k + rel)
    drain(att_fwd)

    def project(i, carry):
        rows = pl.ds(pl.multiple_of(i * 64, 64), 64)
        m = xg[g, rows, :].astype(F32) + (nn(att[rows, :], w_out[...]) + b_out[...])
        middle[rows, :] = m
        inv = lax.rsqrt(jnp.mean(m * m, axis=-1, keepdims=True) + EPS)
        h2own[rows, :] = (m * inv * moe_gain[...]).astype(BF)
        return carry

    lax.fori_loop(0, 4, project, 0)
    gather_h = GatherZ(h2g, h2own)
    gather_h.start()
    gather_dy.step_far()

    logits = nt(w_rt[...], h2own[...]) + b_rt[...]
    row = lax.broadcasted_iota(jnp.int32, (64, T), 0)
    expert_of_row = jnp.where(row % 8 < 4, (row // 8) * 4 + row % 8, -1)
    slots = jnp.full((64, T), -1.0, F32)
    for k in range(4):
        tgt = target[pl.ds(k, 1), :]
        slots = jnp.where(expert_of_row == tgt // 64, (tgt % 64).astype(F32), slots)
    member = slots >= 0.0
    masked = jnp.where(member, logits, NEG)
    top = jnp.max(masked, axis=0, keepdims=True)
    weight = jnp.where(member, jnp.exp(masked - top), 0.0)
    gates = weight / jnp.sum(weight, axis=0, keepdims=True)
    gates_ref[...] = gates
    for r in range(8):
        meta_send[r, pl.ds(0, 8), :] = gates[r * 8:r * 8 + 8]
        meta_send[r, pl.ds(8, 8), :] = slots[r * 8:r * 8 + 8]
    meta_k = sem_block(8)
    meta_sent = []
    metag[g] = meta_send[g]
    for rel in range(1, 8):
        r = gs[rel]
        send(lambda r=r: meta_send.at[r], lambda: metag.at[g], meta_k + rel, {"expert": r}, meta_sent)
    svc(1)
    gh = gather_h
    slot_at = lax.broadcasted_iota(jnp.int32, (64, T), 0).astype(F32)

    def hot_rows(s, e):
        return (slot_at == metag[s, pl.ds(8 + e, 1), :]).astype(F32)

    def take(buf, s, src=None):
        hot = jnp.concatenate([hot_rows(s, e) for e in range(4)], axis=0).astype(BF)
        buf[s] = nn(hot, buf[s] if src is None else src[...]).astype(BF)

    take(h2g, g, h2own)
    gd = gather_dy
    local_dy.wait()
    gd.wait_sib_own()
    gd.wait_sib_m1()
    gd.wait_sib_p1()
    gd.wait_sib_far()
    drain(gd.sent)
    for rel in range(1, 8):
        arrived(metag.at[gs[8 - rel]], meta_k + rel)
    drain(meta_sent)
    gh.wait_sib_own()
    take(h2g, gh.so)
    for s in (g, gd.so, gd.sm1, gd.sp1):
        take(dyg, s)
    svc(1)
    gh.step_m1()
    gh.step_p1()
    for s in (gd.sfar, gd.m1, gd.p1, gd.far):
        take(dyg, s)
    gh.wait_sib_m1()
    take(h2g, gh.sm1)
    gh.wait_sib_p1()
    take(h2g, gh.sp1)
    gh.step_far()
    gh.wait_sib_far()
    take(h2g, gh.sfar)
    drain(gh.sent)
    for s in (gh.m1, gh.p1, gh.far):
        take(h2g, s)

    def weight_of(h, e, n):
        return gathered[h, e, :, pl.ds(n * 16, 16), :].reshape(T, D)

    def rows_of(buf, e, i):
        return buf[pl.ds(i * 4, 4), pl.ds(e * 64, 64), :].reshape(T, D)

    def expert(e, gated_ref, dg_ref, du_ref):
        for item in weights:
            if item == (weights_end, e):
                break

        def some_rows(i, carry):
            rows = pl.ds(pl.multiple_of(i * T, T), T)
            rv = rows_of(h2g, e, i)
            dyv = rows_of(dyg, e, i)
            hots = [hot_rows(i * 4 + n, e) for n in range(4)]
            gcol = jnp.concatenate(
                [jnp.sum(hots[n] * metag[i * 4 + n, pl.ds(e, 1), :], axis=1, keepdims=True) for n in range(4)], axis=0)
            sums = []
            acts, grads = [], []
            for h in range(2):
                cols = pl.ds(h * T, T)
                wg, wu, wd = weight_of(h, e, 0), weight_of(h, e, 1), weight_of(h, e, 2)
                gr = jnp.tanh((nt(rv, wg) + gu_bias[e, pl.ds(0, 1), cols]) * (1.0 / LIMIT))
                ur = jnp.tanh((nt(rv, wu) + gu_bias[e, pl.ds(1, 1), cols]) * (1.0 / LIMIT))
                da = nt(dyv, wd) * gcol
                gc = LIMIT * gr
                uc = LIMIT * ur + 1.0
                sig = 0.5 * jnp.tanh((0.5 * ALPHA) * gc) + 0.5
                glu = gc * sig
                act = uc * glu
                act_low = act.astype(BF)
                gated_ref[rows, cols] = (act * gcol).astype(BF)
                dg = (da * uc * (sig + ALPHA * glu * (1.0 - sig)) * (1.0 - gr * gr)).astype(BF)
                du = (da * glu * (1.0 - ur * ur)).astype(BF)
                dg_ref[rows, cols] = dg
                du_ref[rows, cols] = du
                sums.append(jnp.sum(dg.astype(F32), axis=0, keepdims=True))
                sums.append(jnp.sum(du.astype(F32), axis=0, keepdims=True))
                acts.append(act_low)
                grads.extend([dg, du])
            for h in range(2):
                part = nn(acts[h], weight_of(h, e, 2))
                out = part + down_bias[pl.ds(e, 1), :] if h == 0 else out + part
            out_low = out.astype(BF)
            dyf = dyv.astype(F32)
            dgate = jnp.sum(dyf * out_low.astype(F32), axis=1, keepdims=True)
            for n in range(4):
                s = i * 4 + n
                outb[s, pl.ds(e * 64, 64), :] = out_low[n * 64:n * 64 + 64]
                dgt_send[s, pl.ds(e, 1), :] = jnp.sum(hots[n] * dgate[n * 64:n * 64 + 64], axis=0, keepdims=True)
            for n, (h, m) in enumerate(((0, 0), (0, 1), (1, 0), (1, 1))):
                part = nn(grads[n], weight_of(h, e, m))
                drow = part if n == 0 else drow + part
            drow_low = drow.astype(BF)
            for n in range(4):
                drb[i * 4 + n, pl.ds(e * 64, 64), :] = drow_low[n * 64:n * 64 + 64]
            sums.append(jnp.sum(dyf * gcol, axis=0, keepdims=True))
            return tuple(a + b for a, b in zip(carry, sums))

        zero = jnp.zeros((1, T), F32)
        sums = lax.fori_loop(0, 2, some_rows, (zero, zero, zero, zero, jnp.zeros((1, D), F32)))
        for h in range(2):
            own_rows[pl.ds(8 + e, 1), pl.ds(h * T, T)] = sums[2 * h]
            own_rows[pl.ds(8 + e, 1), pl.ds(512 + h * T, T)] = sums[2 * h + 1]
        own_rows[pl.ds(4 + e, 1), :] = sums[4]

    def weight_grads(e, gated_ref, dg_ref, du_ref):
        drain(pending_weights[e])
        for h in range(2):
            for n, (left, buf) in enumerate(((dg_ref, h2g), (du_ref, h2g), (gated_ref, dyg))):
                right = buf[:, pl.ds(e * 64, 64), :].reshape(512, D)
                grad = tn(left[:, pl.ds(h * T, T)], right)
                gathered[h, e, :, pl.ds(n * 16, 16), :] = grad.astype(BF).reshape(16, 16, D)

    out_copies = []

    class WeightPieces:
        def __init__(self, e, h):
            self.e, self.h, self.k = e, h, wsem(h, e)

        def own(self, s):
            return gathered.at[self.h, self.e, s]

        def rows(self, first_slot, n):
            return gathered.at[self.h, self.e, pl.ds(first_slot, n)]

        def half(self, side):
            return rs_half.at[self.e, self.h, side]

        def full(self, side):
            if self.e < 2:
                return rs_full.at[self.e, self.h, side]
            return h2g.at[self.lent(side), pl.ds(0, 192)]

        def lent(self, side):
            return ((self.e - 2) * 2 + self.h) * 2 + side

        def full_one(self, side, a):
            if self.e < 2:
                return rs_full.at[self.e, self.h, side, a]
            return h2g.at[self.lent(side), pl.ds(a * 48 if isinstance(a, int) else pl.multiple_of(a * 48, 48), 48)]

        def send_row(self, first_slot, side, recv, dev, keep):
            if self.e < 2:
                send(lambda: self.rows(first_slot, 4), lambda: self.full(side), recv, dev, keep, ring_w)
            else:
                for a in range(4):
                    send(lambda a=a: self.own(first_slot + a), lambda a=a: self.full_one(side, a), recv, dev, keep, ring_w)

        def half2(self):
            return rs2_half.at[self.e, self.h]

        def full2(self, side):
            return rs2_full.at[self.e, self.h, side]

        def finish(self):
            for n, out in enumerate((d_gate_w, d_up_w, d_down_w)):
                out_copies.append(local_copy(
                    lambda n=n: self.own(slot(self.h, 0, 0)).at[pl.ds(n * 16, 16)],
                    lambda out=out: out.at[self.e, pl.ds(self.h * 16, 16)]))

    class ParamPieces(WeightPieces):
        def __init__(self, h):
            self.e, self.h, self.k = 0, h, wsem(h, 0)

        def own(self, s):
            return params.at[self.h, s]

        def rows(self, first_slot, n):
            return params.at[self.h, pl.ds(first_slot, n)]

        def half(self, side):
            return rs_half.at[0, self.h, side, :, pl.ds(0, 16), pl.ds(0, 768)]

        def full(self, side):
            return rs_full.at[0, self.h, side, :, pl.ds(0, 16), pl.ds(0, 768)]

        def full_one(self, side, a):
            return rs_full.at[0, self.h, side, a, pl.ds(0, 16), pl.ds(0, 768)]

        def half2(self):
            return rs2_half.at[0, self.h, pl.ds(0, 16), pl.ds(0, 768)]

        def full2(self, side):
            return rs2_full.at[0, self.h, side, pl.ds(0, 16), pl.ds(0, 768)]

        def finish(self):
            pass

    def scatter_xy(p, even_way, wait_for, keep):
        h, k = p.h, p.k
        fwd, back = xy(axis_of(h, 1), 1), xy(axis_of(h, 1), 3)
        fwd2, back2 = xy(axis_of(h, 0), 1), xy(axis_of(h, 0), 3)
        line = lines[h]

        def add(s, refs):
            v = p.own(s)[...].astype(F32)
            for ref in refs:
                v = v + ref[...].astype(F32)
            p.own(s)[...] = v.astype(BF)

        send(lambda: p.rows(line[2], 2), lambda: p.half(0), k, fwd, keep, ring_w)
        send(lambda: p.rows(line[2] + 2, 2), lambda: p.half(1), k + 1, back, keep, ring_w)
        yield 1
        for side, db, dev in ((0, 1, fwd), (1, 3, back)):
            if wait_for:
                pl.semaphore_wait(credit.at[h, side], 1)
            arrived(p.half(side), k + side)
            for n in range(2):
                add(line[db] + side * 2 + n, [p.half(side).at[n]])
            p.send_row(line[db], side, k + 2 + side, dev, keep)
        yield 2
        arrived(p.full(0), k + 2)
        arrived(p.full(1), k + 3)
        for da in (2, 1, 3, 0):
            a = first[h][da]
            add(line[0] + a, [p.full_one(0, a), p.full_one(1, a)])
            if da == 2:
                send(lambda: p.own(slot(h, 2, 0)), p.half2, k + 4, fwd2 if even_way else back2, keep, ring_w)
        yield 3
        arrived(p.half2(), k + 4)
        add(slot(h, 1 if even_way else 3, 0), [p.half2()])
        send(lambda: p.own(slot(h, 1, 0)), lambda: p.full2(0), k + 5, fwd2, keep, ring_w)
        send(lambda: p.own(slot(h, 3, 0)), lambda: p.full2(1), k + 6, back2, keep, ring_w)
        yield 4
        for side in range(2):
            arrived(p.full2(side), k + 5 + side)
        add(slot(h, 0, 0), [p.full2(0), p.full2(1)])
        p.finish()
        yield 5

    scatters = [[scatter_xy(WeightPieces(e, h), e % 2 == 0, e == 2, pending) for h in range(2)] for e in range(4)]

    started = set()

    def wsvc(*experts):
        for e in experts:
            if e not in started:
                started.add(e)
                pl.semaphore_wait(passed.at[e], 4)
            for h in range(2):
                next(scatters[e][h], None)

    dg_k = att_k
    dgt_sent = []

    def combine(buf, s, gated):
        pieces = []
        for e in range(4):
            hot = hot_rows(s, e)
            if gated:
                hot = hot * metag[s, pl.ds(e, 1), :]
            pieces.append(hot)
        spread = jnp.concatenate(pieces, axis=0).T.astype(BF)
        buf[s] = nn(spread, buf[s]).astype(BF)

    scatter_d = ScatterZ(gather_x.k, drb, lambda n: sib_in.at[n], lambda n: half_in.at[n], lambda n: full_in.at[n])
    far_chunks, own_chunks = scatter_d.chunks()

    def experts(*refs):
        for e in range(4):
            expert(e, *refs)
            if e < 3:
                weight_grads(e, *refs)
                wsvc(e)
            if e in (1, 2):
                wsvc(e - 1)
        dgt_in[g] = dgt_send[g]
        for rel in range(1, 8):
            r = gs[rel]
            send(lambda r=r: dgt_send.at[r], lambda: dgt_in.at[g], dg_k + rel, {"expert": r}, dgt_sent)
        for n in range(4):
            combine(drb, far_chunks[n], False)
            scatter_d.to_sibling(n)
        combine(drb, own_chunks[0], False)
        scatter_d.step1()
        weight_grads(3, *refs)
        for h in range(2):
            pl.semaphore_signal(credit.at[h, 1], inc=1, device_id=xy(axis_of(h, 1), 1), device_id_type=MESH)
            pl.semaphore_signal(credit.at[h, 0], inc=1, device_id=xy(axis_of(h, 1), 3), device_id_type=MESH)
        wsvc(3)
        combine(drb, own_chunks[1], False)
        combine(drb, own_chunks[2], False)
        scatter_d.step2()
        combine(drb, own_chunks[3], False)

    pl.run_scoped(
        experts,
        pltpu.VMEM((512, 512), BF), pltpu.VMEM((512, 512), BF), pltpu.VMEM((512, 512), BF))
    local_dy = local_copy(dy_in, lambda: dyg.at[g])
    wsvc(2, 0)
    for n in range(4):
        combine(outb, far_chunks[n], True)
    for n in range(4):
        combine(outb, own_chunks[n], True)
    scatter_d.step3()

    for rel in range(1, 8):
        arrived(dgt_in.at[gs[8 - rel]], dg_k + rel)
    d_gates = jnp.where(row % 8 < 4, jnp.concatenate([dgt_in[r] for r in range(8)], axis=0), 0.0)
    d_logits = gates_ref[...] * (d_gates - jnp.sum(gates_ref[...] * d_gates, axis=0, keepdims=True))
    dl_high, dl_low = split_low(d_logits)
    d_wrt = nn(dl_high, h2own[...]) + nn(dl_low, h2own[...])
    common_rows[pl.ds(6, 1), pl.ds(0, 64)] = jnp.sum(d_logits.T, axis=0, keepdims=True)
    dl_high_t, dl_low_t = split_low(d_logits.T)
    d_middle[...] = nn(dl_high_t, w_rt[...]) + nn(dl_low_t, w_rt[...])
    drain(scatter_d.sent)
    drain(gather_x.sent)
    local_dy.wait()
    att_grad, branch_at = h2own, 7

    def middle_back(i, carry):
        rows = pl.ds(pl.multiple_of(i * 64, 64), 64)
        m = middle[rows, :]
        inv = lax.rsqrt(jnp.mean(m * m, axis=-1, keepdims=True) + EPS)
        d_h2 = scatter_d.result(rows) + d_middle[rows, :]
        v2 = d_h2 * moe_gain[...]
        inner = jnp.mean(v2 * m, axis=-1, keepdims=True)
        dm = dyg[g, rows, :].astype(F32) + inv * v2 - m * (inv * inv * inv * inner)
        d_middle[rows, :] = dm
        low = dm.astype(BF)
        dyg[branch_at, rows, :] = low
        att_grad[rows, :] = nt(low, w_out[...]).astype(BF)
        return (carry[0] + jnp.sum(low.astype(F32), axis=0, keepdims=True),
                carry[1] + jnp.sum(d_h2 * m * inv, axis=0, keepdims=True))

    zero_row = jnp.zeros((1, D), F32)
    sum_b, sum_m = lax.fori_loop(0, 4, middle_back, (zero_row, zero_row))
    common_rows[pl.ds(4, 1), :] = sum_b
    common_rows[pl.ds(5, 1), :] = sum_m

    do_k = meta_k
    att_sent = []
    dob[g] = att_grad[:, pl.ds(pl.multiple_of(g * 128, 128), 128)]
    for rel in range(1, 8):
        r = gs[rel]
        send(lambda r=r: att_grad.at[:, pl.ds(pl.multiple_of(r * 128, 128), 128)], lambda: dob.at[g], do_k + rel, {"expert": r}, att_sent)
    drain(dgt_sent)

    eight = lax.broadcasted_iota(jnp.int32, (8, D), 0)
    for r in range(8):
        rows = pl.ds(r * 128, 128)
        drb[r, pl.ds(0, 128), :] = tn(att[:, rows], dyg[branch_at]).astype(BF)
        mine = jnp.where(g == r, 1.0, 0.0).astype(F32)
        top = jnp.where(eight < 4, d_wrt[r * 8:r * 8 + 8], own_rows[pl.ds(0, 8), :] * mine)
        low_rows = own_rows[pl.ds(8, 8), :] * mine
        if r == 0:
            low_rows = jnp.where(eight < 4, low_rows, common_rows[...])
        drb[r, pl.ds(128, 16), :] = jnp.concatenate([top, low_rows], axis=0).astype(BF)
    wsvc(1, 3)
    for rel in range(1, 8):
        arrived(dob.at[gs[8 - rel]], do_k + rel)

    scatter_m = ScatterZ(
        gather_dy.k, outb, lambda n: dyg.at[n], lambda n: dyg.at[4, pl.ds(n * 128, 128)], lambda n: dyg.at[5 + n])
    for n in range(4):
        scatter_m.to_sibling(n)
    scatter_w = ScatterZ(
        gather_h.k, drb, lambda n: sib_in.at[n, pl.ds(0, 144)], lambda n: half_in.at[n, pl.ds(0, (80, 64)[n])],
        lambda n: full_in.at[n, pl.ds(0, 144)], (80, 64))
    for n in range(4):
        scatter_w.to_sibling(n)

    class Exchange:
        def __init__(self, stage, inbox, everyone, k):
            self.stage, self.inbox, self.everyone, self.spread_k = stage, inbox, everyone, k
            self.k = sem_block(6)
            self.sent = []

        def start(self, n):
            for d in (1, 2, 3):
                send(lambda: self.stage.at[n], lambda d=d: self.inbox.at[n, d - 1], self.k + n * 3 + d - 1,
                     xy("xy"[n], d), self.sent)

        def total(self, n):
            v = self.stage[n]
            for d in (1, 2, 3):
                arrived(self.inbox.at[n, d - 1], self.k + n * 3 + d - 1)
            for d in (1, 2, 3):
                v = v + self.inbox[n, d - 1]
            return v

        def spread(self):
            for rel in range(1, 8):
                send(lambda: self.everyone.at[g], lambda: self.everyone.at[g], self.spread_k + rel,
                     spread_group[rel], self.sent)

        def step(self, n):
            v = self.total(n)
            if n == 0:
                self.stage[1] = v
                self.start(1)
            else:
                self.everyone[g] = v
                self.spread()

        def finish(self):
            for rel in range(1, 8):
                arrived(self.everyone.at[gs[8 - rel]], self.spread_k + rel)

    early_sum = Exchange(early, early_in, early_all, att_k)
    late_sum = Exchange(late, late_in, late_all, meta_k)
    spread_group = [{"expert": gs[rel]} for rel in range(8)]

    sub_low = lax.broadcasted_iota(jnp.int32, (128, 1), 0) < 64
    smask0 = jnp.where(sub_low, 1.0, 0.0).astype(F32)
    smask1 = 1.0 - smask0

    def stacked_t(v_t):
        return jnp.concatenate([v_t * smask0, v_t * smask1], axis=1).astype(BF)

    def attend_back(rel, dk_ref, dv_ref, dqkv_ref, dq_ref):
        i = gs[rel % 8]
        q2 = stacked(qs[i])
        q2t = stacked_t(qs[i].astype(F32).T)
        do2 = stacked(dob[i])
        do_t = dob[i].astype(F32).T
        do2t = stacked_t(do_t)
        prod = do_t * att_send[i].astype(F32).T
        delta = jnp.concatenate(
            [jnp.sum(prod[:64], axis=0, keepdims=True), jnp.sum(prod[64:], axis=0, keepdims=True)], axis=1)
        lse_row = lse[i]
        share = jnp.exp(sink_row[...] - lse_row) * delta
        for n in range(2):
            part = jnp.sum(share[:, n * T:n * T + T], axis=1, keepdims=True)
            late[0, pl.ds(2, 1), pl.ds(0, 128)] -= jnp.where(lane == n, part, 0.0)
        dq_ref[...] = jnp.zeros((128, 2 * T), F32)

        def blocks(keys, diagonal):
            probs = [jnp.exp(nn(kk[j], q2t) - lse_row) for j in keys]
            if diagonal:
                probs = [jnp.where(allowed, p, 0.0) for p in probs]
            dq = dq_ref[...]
            for j, p in zip(keys, probs):
                ds = (p * (nn(vv[j], do2t) - delta)).astype(BF)
                dv_ref[j] += nn(p.astype(BF), do2)
                dk_ref[j] += nn(ds, q2)
                dq = dq + nn(kkt[j], ds)
            dq_ref[...] = dq

        def body(j, carry):
            blocks((2 * j, 2 * j + 1), False)
            return carry

        lax.fori_loop(0, lax.div(i, 2), body, 0)

        @pl.when(lax.rem(i, 2) == 1)
        def _():
            blocks((i - 1,), False)

        blocks((i,), True)
        dq = dq_ref[...].T
        dq = jnp.where(low_half, dq[:T], dq[T:]) * 0.125
        cosine, sine = trig(i)
        dqkv_ref[i, 0] = (dq * cosine - swap(dq) * sine).astype(BF)
        give(0, rel, dqkv_ref, dq_sent)

    dq_k = [sem_block(8), sem_block(8)]
    swap_k = sem_block(1)
    dq_sent = []

    def give(part, rel, dqkv_ref, keep):
        i = gs[rel % 8]
        if rel < 8:
            send(lambda: dqkv_ref.at[i, part], lambda: dall.at[part, :, own_tile(g)], dq_k[part] + rel,
                 {"expert": i}, keep)
        else:
            dall[part, :, own_tile(g)] = dqkv_ref[i, part]

    def finish(rel, dk_ref, dv_ref, dqkv_ref, swap_sent):
        r = gs[rel % 8]
        cosine, sine = trig(r)
        dk = dk_ref[r]
        dk = dk + pltpu.roll(dk, 64, 1)
        dv = dv_ref[r]
        dv = dv + pltpu.roll(dv, 64, 1)
        dqkv_ref[r, 1] = jnp.where(low_half, dk * cosine - swap(dk) * sine, dv).astype(BF)
        for n in range(2):
            late[0, pl.ds(1, 1), pl.ds(n * 128, 128)] += jnp.sum(dqkv_ref[r, n].astype(F32), axis=0, keepdims=True)
        send(lambda: dqkv_ref.at[r, 1], lambda: dyg.at[7, :, own_tile(r)], swap_k, sib, swap_sent)
        give(1, rel, dqkv_ref, dq_sent)

    def load_projection():
        return [local_copy(lambda n=n, half=half: w_qkv_in.at[pl.ds(n * T, T), pl.ds(half * D, D)],
                           lambda n=n, half=half: drb.at[n * 2 + half]) for n in range(4) for half in range(2)]

    def order_projection(copies):
        drain(copies)

        def some(i, carry):
            rows = pl.ds(pl.multiple_of(lax.rem(i, 4) * 64, 64), 64)
            at = lax.div(i, 4) * 2 + 1
            v = drb[at, rows, :].astype(F32)
            tiles = [v[:, n * 128:n * 128 + 128] for n in range(8)]
            turned = [pltpu.roll(t, 64, 1) for t in tiles]
            for n in range(4):
                drb[at, rows, pl.ds(n * 256, 128)] = jnp.where(low_half, tiles[n], turned[n + 4]).astype(BF)
                drb[at, rows, pl.ds(n * 256 + 128, 128)] = jnp.where(low_half, turned[n], tiles[n + 4]).astype(BF)
            return carry

        lax.fori_loop(0, 16, some, 0)

    def place_projection():
        for t in range(8):
            v = scatter_w.result(pl.ds(t * 16, 16)).astype(BF)
            for side in range(2):
                for h in range(2):
                    at = side * 512 + h * 256
                    params[h, side * 8 + t, :, pl.ds(0, 256)] = v[:, at:at + 256]
        early[0] = scatter_w.result(pl.ds(128, 16))

    zloc = [(lax.div(zs[d], 2), lax.rem(zs[d], 2)) for d in range(4)]

    def param_piece(h, col, s):
        return gathered.at[h, col, s, pl.ds(0, 32), pl.ds(0, 768)]

    def param_row(h, d):
        hi, lo = zloc[d]
        return gathered.at[h, c * 2 + hi, slot(h, 0, 0), pl.ds(pl.multiple_of(lo * 16, 16), 16), pl.ds(0, 768)]

    param_sent = []

    def own_line(h, e, db):
        return gathered.at[h, c * 2 + e, pl.ds(second[h][db] * 4, 4), pl.ds(0, 32), pl.ds(0, 768)]

    def own_piece(h, e, da):
        return param_piece(h, c * 2 + e, slot(h, da, 0))

    def psem(h, e):
        return wsem(h, 1 + e)

    def forward(piece, recv, dev):
        send(piece, piece, recv, dev, param_sent, ring_w)

    out_k = [sem_block(1) for _ in range(2)]

    def place_out(core, e):
        for h in range(2):
            col = core * 2 + e
            for zl in range(2):
                rows = pl.ds(zl * 16, 16)
                member = (e * 2 + zl) * 2 + core
                for side in range(2):
                    pltpu.make_async_copy(
                        gathered.at[h, col, pl.ds(side * 8, 8), rows, pl.ds(0, 256)],
                        d_wout.at[member, :, :, pl.ds(side * 512 + h * 256, 256)], sems.at[out_k[0]]).start()
                    for part, to in ((0, member * 128), (1, 1024 + core * 512 + (e * 2 + zl) * 128)):
                        pltpu.make_async_copy(
                            gathered.at[h, col, :, rows, pl.ds(256 + side * 256 + part * 128, 128)],
                            d_wqkv.at[:, pl.ds(h * 32 + side * 16, 16), pl.ds(pl.multiple_of(to, 128), 128)],
                            sems.at[out_k[1]]).start()

    def params_gather():
        z_k = wsem(0, 3)
        for h in range(2):
            param_row(h, 0)[...] = params[h, slot(h, 0, 0)]
            forward(lambda h=h: param_row(h, 0), z_k + h * 3, up)
            forward(lambda h=h: param_row(h, 0), z_k + h * 3 + 1, down)
        yield 1
        arrived(param_row(0, 3), z_k + 0)
        forward(lambda: param_row(0, 3), z_k + 2, up)
        arrived(param_row(1, 1), z_k + 4)
        forward(lambda: param_row(1, 1), z_k + 5, down)
        arrived(param_row(0, 1), z_k + 1)
        arrived(param_row(1, 3), z_k + 3)
        yield 2
        arrived(param_row(0, 2), z_k + 2)
        arrived(param_row(1, 2), z_k + 5)
        for e in range(2):
            for h in range(2):
                for n, d in ((0, 1), (1, 3)):
                    forward(lambda h=h, e=e: own_piece(h, e, 0), psem(h, e) + n, xy(axis_of(h, 0), d))
        yield 3
        for e in range(2):
            for h in range(2):
                k = psem(h, e)
                arrived(own_piece(h, e, 3), k)
                if e == 0:
                    forward(lambda h=h, e=e: own_piece(h, e, 3), k + 2, xy(axis_of(h, 0), 1))
                arrived(own_piece(h, e, 1), k + 1)
                if e == 1:
                    forward(lambda h=h, e=e: own_piece(h, e, 1), k + 2, xy(axis_of(h, 0), 3))
        for e in range(2):
            for h in range(2):
                k = psem(h, e)
                arrived(own_piece(h, e, 2), k + 2)
                for n, d in ((3, 1), (4, 3)):
                    forward(lambda h=h, e=e: own_line(h, e, 0), k + n, xy(axis_of(h, 1), d))
        for e in range(2):
            for h in range(2):
                forward(lambda h=h, e=e: own_line(h, e, 0), sib_k(h, e), sib)
        yield 4
        for e in range(2):
            for h in range(2):
                k = psem(h, e)
                arrived(own_line(h, e, 3), k + 3)
                if e == 0:
                    forward(lambda h=h, e=e: own_line(h, e, 3), k + 5, xy(axis_of(h, 1), 1))
                arrived(own_line(h, e, 1), k + 4)
                if e == 1:
                    forward(lambda h=h, e=e: own_line(h, e, 1), k + 5, xy(axis_of(h, 1), 3))
                for db in (3, 1):
                    forward(lambda h=h, e=e, db=db: own_line(h, e, db), sib_k(h, e), sib)
        yield 5
        for e in range(2):
            for h in range(2):
                arrived(own_line(h, e, 2), psem(h, e) + 5)
                forward(lambda h=h, e=e: own_line(h, e, 2), sib_k(h, e), sib)
            place_out(c, e)
        yield 6
        for e in range(2):
            for h in range(2):
                arrived(gathered.at[h, other * 2 + e, :, pl.ds(0, 32), pl.ds(0, 768)], sib_k(h, e))
            place_out(other, e)
        yield 7

    def sib_k(h, e):
        return wsem(1, 3) + h * 2 + e

    param_scatters = [scatter_xy(ParamPieces(h), h == 0, False, param_sent) for h in range(2)]

    def psvc():
        for h in range(2):
            next(param_scatters[h], None)

    def backward(dk_ref, dv_ref, dqkv_ref, dq_ref):
        dk_ref[...] = jnp.zeros((8, T, 128), F32)
        dv_ref[...] = jnp.zeros((8, T, 128), F32)
        swap_sent = []
        plan = {7: (0,), 6: (1,), 5: (2,), 4: (3,), 3: (2,), 2: (3,), 1: (0, 1), 0: (2,)}
        for i in range(7, -1, -1):
            attend_back(8 - i, dk_ref, dv_ref, dqkv_ref, dq_ref)
            if i == 7:
                scatter_w.step1()
            if i in plan:
                wsvc(*plan[i])
            if i == 5:
                scatter_w.step2()
            if i == 4:
                scatter_w.step3()
                place_projection()
                early_sum.start(0)
                drain(scatter_w.sent)
                copies = load_projection()
            if i == 3:
                early_sum.step(0)
                order_projection(copies)
            if i == 1:
                early_sum.step(1)
        for rel in range(1, 9):
            finish(rel, dk_ref, dv_ref, dqkv_ref, swap_sent)
        drain(att_sent)
        wsvc(3)
        drain(pending)
        drain(out_copies)
        for dev in (sib, up, down, xy("x", 1), xy("x", 3), xy("y", 1), xy("y", 3)):
            pl.semaphore_signal(free_xy, inc=1, device_id=dev, device_id_type=MESH)

        dk_ref[...] = jnp.zeros((8, T, 128), F32)
        arrived(dyg.at[7], swap_k)
        drain(swap_sent)

        def dw_part(r, carry):
            both = dyg[7, :, own_tile(r)].astype(F32)
            own = dqkv_ref[r, 1].astype(F32)
            mixed = jnp.where(low_half == even, own, pltpu.roll(both, 64, 1)).astype(BF)
            h1 = h1_rows(r, pl.ds(0, T))
            v = jnp.concatenate([tn(dqkv_ref[r, 0], h1), tn(mixed, h1)], axis=0)
            for n in range(8):
                dk_ref[n] += v[:, n * 128:n * 128 + 128]
            return carry

        lax.fori_loop(0, 8, dw_part, 0)
        for n in range(8):
            dw = dk_ref[n].T
            for s in range(2):
                for h in range(2):
                    rows = dw[s * 64 + h * 32:s * 64 + h * 32 + 32]
                    params[h, n * 2 + s, :, pl.ds(256, 512)] = jnp.concatenate([rows[:16], rows[16:]], axis=1).astype(BF)
        pl.semaphore_wait(free_xy, 7)
        psvc()
        scatter_m.step1()
        for part in range(2):
            for rel in range(1, 8):
                arrived(dall.at[part, :, own_tile(gs[8 - rel])], dq_k[part] + rel)
        drain(dq_sent)
        for n in range(4):
            part = nt(dall[0], drb[2 * n]) + nt(dall[1], drb[2 * n + 1])
            dv_ref[2 * n] = part[:, :128]
            dv_ref[2 * n + 1] = part[:, 128:]
        psvc()
        scatter_m.step2()

        def tokens_back(i, carry):
            rows = pl.ds(pl.multiple_of(i * 64, 64), 64)
            xf = xg[g, rows, :].astype(F32)
            inv = lax.rsqrt(jnp.mean(xf * xf, axis=-1, keepdims=True) + EPS)
            d_h1 = jnp.concatenate([dv_ref[n, rows, :] for n in range(8)], axis=1)
            v1 = d_h1 * attn_gain[...]
            inner = jnp.mean(v1 * xf, axis=-1, keepdims=True)
            h2own[rows, :] = (d_middle[rows, :] + inv * v1 - xf * (inv * inv * inv * inner)).astype(BF)
            return carry + jnp.sum(d_h1 * xf * inv, axis=0, keepdims=True)

        psvc()
        late[0, pl.ds(0, 1), :] = lax.fori_loop(0, 4, tokens_back, zero_row)
        late_sum.start(0)
        cp3 = local_copy(h2own, d_tokens)
        psvc()
        psvc()
        gather_p = params_gather()
        next(gather_p)
        late_sum.step(0)
        next(gather_p)
        next(gather_p)
        early_sum.finish()
        late_sum.step(1)
        next(gather_p)
        next(gather_p)
        scatter_m.step3()

        def result(i, carry):
            rows = pl.ds(pl.multiple_of(i * 64, 64), 64)
            att[rows, :] = (middle[rows, :] + scatter_m.result(rows)).astype(BF)
            return carry

        lax.fori_loop(0, 4, result, 0)
        cp2 = local_copy(att, block_out)
        late_sum.finish()
        for r in range(8):
            final[pl.ds(0, 1), :] += late_all[r, pl.ds(0, 1), :]
            final[pl.ds(3, 1), pl.ds(r * 128, 128)] = late_all[r, pl.ds(1, 1), pl.ds(0, 128)]
            two = late_all[r, pl.ds(2, 1), pl.ds(0, 128)]
            two = pltpu.roll(two, 2 * r, 1) if r else two
            final[pl.ds(5, 1), pl.ds(0, 128)] += jnp.where((lane >= 2 * r) & (lane < 2 * r + 2), two, 0.0)
        for n in range(4):
            a = late_all[2 * n, pl.ds(1, 1), pl.ds(128, 128)]
            b = late_all[2 * n + 1, pl.ds(1, 1), pl.ds(128, 128)]
            final[pl.ds(4, 1), pl.ds(n * 128, 128)] = jnp.where(low_half, a, pltpu.roll(b, 64, 1))
            final[pl.ds(4, 1), pl.ds(512 + n * 128, 128)] = jnp.where(low_half, pltpu.roll(a, 64, 1), b)
        final[pl.ds(1, 2), :] = early_all[0, pl.ds(12, 2), :]
        cp4 = local_copy(early_all, early_out)
        cp5 = local_copy(final, final_out)
        for _ in gather_p:
            pass
        drain(scatter_m.sent)
        drain([cp2, cp3, cp4, cp5])
        pltpu.make_async_copy(d_wout, d_wout, sems.at[out_k[0]]).wait()
        pltpu.make_async_copy(d_wqkv, d_wqkv, sems.at[out_k[1]]).wait()

    pl.run_scoped(
        backward, pltpu.VMEM((8, T, 128), F32), pltpu.VMEM((8, T, 128), F32), pltpu.VMEM((8, 2, T, 128), BF),
        pltpu.VMEM((128, 2 * T), F32))
    drain(param_sent)
    drain(early_sum.sent)
    drain(late_sum.sent)


ANY = pl.BlockSpec(memory_space=pl.ANY)
VM = pl.BlockSpec(memory_space=pltpu.VMEM)


def angle_tables():
    frequency = np.exp(np.arange(32, dtype=np.float32) * np.float32(-2.0 * np.log(THETA) / 64)).astype(np.float64)
    freq = np.tile(frequency, 4)[None, :]
    near = np.arange(T, dtype=np.float64)[:, None] * freq
    far = np.arange(8, dtype=np.float64)[:, None] * T * freq
    return [f(a).astype(np.float32) for a in (near, far) for f in (np.cos, np.sin)]


def per_device(
    tokens, cotangent, routes, slot_ids, attn_gain, w_qkv, b_qkv, w_out, b_out, sink_logits, moe_gain,
    w_router, b_router, gu_weight, gu_bias, down_weight, down_bias,
):
    g = lax.axis_index("expert")
    both = jnp.concatenate([gu_weight.transpose(0, 2, 1, 3), down_weight[:, None]], axis=1)
    shard = both.reshape(4, 3, 2, 16, D).transpose(2, 0, 1, 3, 4).reshape(2, 4, 48, D)
    target = jnp.pad((routes * 64 + slot_ids).T, ((0, 4), (0, 0)))

    def padded(v):
        return jnp.pad(v.reshape(8, 4, -1), ((0, 0), (0, 4), (0, 0))).reshape(64, -1)

    w_rt = padded(w_router.T)
    b_rt = jnp.broadcast_to(padded(b_router), (64, T))
    gub = gu_bias.reshape(4, 2, 4, 4, 2, 16)
    gub = jnp.concatenate([gub[:, :, :, :, 0].reshape(4, 2, 256), gub[:, :, :, :, 1].transpose(0, 1, 3, 2, 4).reshape(4, 2, 256)], axis=2)
    down_own = lax.dynamic_slice_in_dim(down_bias, g * 4, 4, 0)
    cos_a, sin_a, cos_b, sin_b = [jnp.asarray(t) for t in angle_tables()]
    shape = jax.ShapeDtypeStruct
    out = pl.pallas_call(
        layer_kernel,
        out_shape=(
            shape((T, D), BF), shape((T, D), BF), shape((4, 32, D), BF), shape((4, 32, D), BF), shape((4, 32, D), BF),
            shape((16, 64, 2048), BF), shape((8, 8, 16, D), BF), shape((8, 16, D), F32), shape((8, D), F32),
        ),
        in_specs=[ANY] * 4 + [VM] * 15,
        out_specs=[ANY] * 9,
        scratch_shapes=[
            pltpu.VMEM((8, T, D), BF), pltpu.VMEM((8, T, D), BF), pltpu.VMEM((8, T, D), BF),
            pltpu.VMEM((2, 4, 16, 48, D), BF),
            pltpu.VMEM((8, T, 128), BF), pltpu.VMEM((8, T, 128), BF), pltpu.VMEM((8, T, 128), BF),
            pltpu.VMEM((8, 128, T), BF), pltpu.VMEM((8, 128, T), BF),
            pltpu.VMEM((8, 1, 2 * T), F32), pltpu.VMEM((8, T, 128), BF), pltpu.VMEM((T, D), BF),
            pltpu.VMEM((T, D), F32), pltpu.VMEM((T, D), BF),
            pltpu.VMEM((8, 16, T), F32), pltpu.VMEM((8, 16, T), F32),
            pltpu.VMEM((8, T, D), BF), pltpu.VMEM((8, T, D), BF),
            pltpu.VMEM((4, T, D), BF), pltpu.VMEM((2, 128, D), BF), pltpu.VMEM((2, T, D), BF),
            pltpu.VMEM((4, 2, 2, 2, 48, D), BF), pltpu.VMEM((2, 2, 2, 4, 48, D), BF),
            pltpu.VMEM((4, 2, 48, D), BF), pltpu.VMEM((4, 2, 2, 48, D), BF),
            pltpu.VMEM((8, T, 128), BF), pltpu.VMEM((8, 8, T), F32), pltpu.VMEM((8, 8, T), F32),
            pltpu.VMEM((T, D), F32),
            pltpu.VMEM((64, T), F32), pltpu.VMEM((2, 16, 16, 768), BF),
            pltpu.VMEM((16, D), F32), pltpu.VMEM((8, D), F32),
            pltpu.VMEM((2, 16, D), F32), pltpu.VMEM((2, 3, 16, D), F32), pltpu.VMEM((8, 16, D), F32),
            pltpu.VMEM((2, 8, D), F32), pltpu.VMEM((2, 3, 8, D), F32), pltpu.VMEM((8, 8, D), F32),
            pltpu.VMEM((D, 256), BF), pltpu.VMEM((1, 256), F32), pltpu.VMEM((1, 512), F32), pltpu.VMEM((8, D), F32),
            pltpu.VMEM((2, T, D), BF),
            pltpu.SemaphoreType.DMA((NSEM,)), pltpu.SemaphoreType.REGULAR((2, 2)),
            pltpu.SemaphoreType.REGULAR, pltpu.SemaphoreType.REGULAR((4,)),
        ],
        compiler_params=pltpu.CompilerParams(collective_id=1, has_side_effects=True, vmem_limit_bytes=VLIM),
    )(tokens, cotangent, shard, w_qkv, target, attn_gain[None], b_qkv[None], w_out, b_out[None],
      sink_logits[None], moe_gain[None], w_rt, b_rt, gub, down_own, cos_a, sin_a, cos_b, sin_b)
    block_out, d_tokens, d_gate_w, d_up_w, d_down_w, d_wqkv, d_wout, early, final = out
    d_wr = early[:, :4].reshape(32, D).T
    d_br = early[0, 14, :64].reshape(8, 8)[:, :4].reshape(32)
    d_gub = lax.dynamic_index_in_dim(early, g, 0, keepdims=False)[8:12].reshape(4, 2, 2, 16, 16)
    dp = lax.axis_index("dp")
    turned = (dp % 4) * 4 + dp // 4
    d_gub = jnp.concatenate([lax.dynamic_index_in_dim(d_gub[:, :, 0], dp, 2, keepdims=False),
                             lax.dynamic_index_in_dim(d_gub[:, :, 1], turned, 2, keepdims=False)], axis=-1)
    return (
        block_out, d_tokens, final[0], d_wqkv.reshape(D, 2048).astype(F32), final[3:5].reshape(2048),
        d_wout.reshape(D, D).astype(F32), final[1], final[5, :16], final[2], d_wr, d_br,
        jnp.stack([d_gate_w, d_up_w], axis=2).astype(F32), d_gub, d_down_w.astype(F32), early[:, 4:8].reshape(32, D),
    )


def solution(mesh):
    rows = P(("dp", "expert"), None)
    in_specs = (rows,) * 4 + (P(),) * 9 + (
        P("expert", "dp", None, None), P("expert", None, None), P("expert", "dp", None), P())
    out_specs = (rows,) * 2 + (P(),) * 9 + (
        P("expert", "dp", None, None), P("expert", None, "dp"), P("expert", "dp", None), P())
    return jax.shard_map(per_device, mesh=mesh, in_specs=in_specs, out_specs=out_specs, check_vma=False)
```
